256 devices in a mesh: tile: 8 (over z), grp: 32 (over x, y, core).
Axes of the slice: x: 4, y: 4, z: 8, core: 2. Of those that a mesh axis runs over, the one named last changes fastest.
Arguments:
- inputs: bfloat16 [2, 64, 64, 2112], P(None, 'tile', None, 'grp'), may hold values from -6 to 6
- cotangent: bfloat16 [2, 64, 64, 2112], P(None, 'tile', None, 'grp'), may hold values from -6 to 6
- first_weight: bfloat16 [2112, 2112], P(None, 'grp'), may hold values from -0.25 to 0.25
- first_bias: float32 [2112], P('grp'), may hold values from -3 to 3
- conv_weight: bfloat16 [2112, 9, 264], P('grp'), may hold values from -0.125 to 0.125
- conv_bias: float32 [2112], P('grp'), may hold values from -3 to 3
- squeeze_weight: bfloat16 [2112, 528], P('grp'), may hold values from -0.125 to 0.125
- squeeze_bias: float32 [528], replicated, may hold values from -3 to 3
- excite_weight: bfloat16 [528, 2112], P(None, 'grp'), may hold values from -0.25 to 0.25
- excite_bias: float32 [2112], P('grp'), may hold values from -0.5 to 0.5
- second_weight: bfloat16 [2112, 2112], P('grp'), may hold values from -0.25 to 0.25
- first_basis: float32 [2112, 256], replicated, may hold values from -0.125 to 0.125
- second_basis: float32 [2112, 256], P('grp'), may hold values from -0.125 to 0.125
Outputs:
- block_out: bfloat16 [2, 64, 64, 2112], P(None, 'tile', None, 'grp')
- input_grad: bfloat16 [2, 64, 64, 2112], P(None, 'tile', None, 'grp')
- first_grad: float32 [2112, 2112], P(None, 'grp')
- second_grad: float32 [2112, 2112], P('grp')
- conv_grad: float32 [2112, 9, 264], P('grp')
- squeeze_grad: float32 [2112, 528], P('grp')
- excite_grad: float32 [528, 2112], P(None, 'grp')
The draws below stay inside these ranges and needn't reach their ends.
All inputs are finite; a program needn't handle non-finite values.
Results may differ from the reference program's by a relative error of at most 0.015.
Values may be sent and summed in bfloat16 or wider, within the bound.
A program may use at most 128 MiB of HBM per device.

```python
import math
import jax
import jax.numpy as jnp
from jax import lax

IMAGES = 2
COLS = 64
GW = 264
BASIS = 256
ROWS = 64
CH = 2112
CH_DEV = 66
SQ = 528


def draw_cotangent(key, part):
    key = jax.random.fold_in(key, 11)
    sign_key, size_key, noise_key = jax.random.split(key, 3)
    signs = jax.random.rademacher(sign_key, (CH,), jnp.float32)
    offsets = signs * jax.random.uniform(size_key, (CH,), jnp.float32, 1.5, 3.0)
    noise = jax.random.normal(noise_key, (IMAGES, ROWS, COLS, CH), jnp.float32)
    return jnp.clip(offsets + noise, -6.0, 6.0).astype(jnp.bfloat16)


def with_spikes(drawn, rng, source, target, parts, factor):
    def block_of(position):
        return (jnp.arange(drawn.shape[position]) // (drawn.shape[position] // parts)).reshape((-1,) + (1,) * (drawn.ndim - 1 - position))

    near = jax.random.permutation(rng, parts)[block_of(target)]
    second = (block_of(target) + parts // 2) % parts
    return jnp.where((block_of(source) == near) | (block_of(source) == second), factor * drawn, drawn)


def block_scale(stream_key, dims, shards, smallest, largest):
    level = 1.0
    for position, blocks in shards:
        steps = jax.random.uniform(jax.random.fold_in(jax.random.fold_in(stream_key, 6), position), (blocks,), jnp.float32, smallest / len(shards), largest / len(shards))
        level = level * jnp.repeat(jnp.exp(steps), dims[position] // blocks).reshape((-1,) + (1,) * (len(dims) - 1 - position))
    return level


def centred(stream_key, shape, width, most, pieces=(), dtype=jnp.bfloat16):
    level = block_scale(stream_key, shape, pieces, -0.22, 0.18) if pieces else 1.0
    entries = jax.random.normal(stream_key, shape, jnp.float32) * width * level
    return jnp.minimum(jnp.maximum(entries, -most), most).astype(dtype)


def gaussian_with(rng, shape, deviation, most, shards, heavy, held_as=jnp.bfloat16):
    values = deviation * jax.random.normal(rng, shape, jnp.float32)
    if shards:
        values = values * block_scale(rng, shape, shards, -0.22, 0.18)
    return jnp.clip(with_spikes(values, jax.random.fold_in(rng, 3), *heavy), -most, most).astype(held_as)


def setup_inputs(seed: int = 0) -> dict:
    streams_of = jax.random.split(jax.random.key(seed), 14)
    inputs = centred(streams_of[0], (IMAGES, ROWS, COLS, CH), 1.0, 6.0, ((1, 8), (3, 32)))
    cotangent = draw_cotangent(jax.random.fold_in(streams_of[13], 71), 0)
    first_weight = gaussian_with(streams_of[2], (CH, CH), CH ** -0.5, 0.25, ((1, 32),), (1, 0, 32, 2.75))
    first_bias = centred(streams_of[3], (CH,), 0.5, 3.0, ((0, 32),), jnp.float32)
    conv_weight = centred(streams_of[4], (CH, 9, GW), (9 * GW) ** -0.5, 0.125, ((0, 32),))
    conv_bias = centred(streams_of[5], (CH,), 0.5, 3.0, ((0, 32),), jnp.float32)
    squeeze_weight = centred(streams_of[6], (CH, SQ), CH ** -0.5, 0.125, ((0, 32),))
    squeeze_bias = centred(streams_of[7], (SQ,), 0.5, 3.0, (), jnp.float32)
    excite_weight = centred(streams_of[8], (SQ, CH), SQ ** -0.5, 0.25, ((1, 32),))
    excite_bias = jnp.clip(jax.random.uniform(streams_of[9], (CH,), jnp.float32, -0.5, 0.5) * block_scale(streams_of[9], (CH,), ((0, 32),), -0.4, 0.0), -0.5, 0.5)
    second_weight = gaussian_with(streams_of[10], (CH, CH), CH ** -0.5, 0.25, ((0, 32),), (0, 1, 32, 2.75))
    first_basis = centred(streams_of[11], (CH, BASIS), CH ** -0.5, 0.125, (), jnp.float32)
    second_basis = centred(streams_of[12], (CH, BASIS), CH ** -0.5, 0.125, ((0, 32),), jnp.float32)
    return dict(inputs=inputs, cotangent=cotangent, first_weight=first_weight, first_bias=first_bias, conv_weight=conv_weight, conv_bias=conv_bias, squeeze_weight=squeeze_weight, squeeze_bias=squeeze_bias, excite_weight=excite_weight, excite_bias=excite_bias, second_weight=second_weight, first_basis=first_basis, second_basis=second_basis)


highest = lax.Precision.HIGHEST

def slope(value):
    sig = jax.nn.sigmoid(value)
    return sig * (1.0 + value * (1.0 - sig))

def block_sum(left_blocks, right_blocks):

    def step(running, pair):
        term = jnp.dot(pair[0], pair[1], preferred_element_type=jnp.float32)
        rounded = lax.optimization_barrier(term.astype(jnp.bfloat16))
        return (running + rounded.astype(jnp.float32), None)
    start_value = jnp.zeros((left_blocks.shape[1], right_blocks.shape[2]), jnp.float32)
    result, unused = lax.scan(step, start_value, (left_blocks, right_blocks))
    return result

def reference(inputs, cotangent, first_weight, first_bias, conv_weight, conv_bias, squeeze_weight, squeeze_bias, excite_weight, excite_bias, second_weight, first_basis, second_basis):
    groups = CH // GW
    blocks = CH // CH_DEV
    pixels = IMAGES * ROWS * COLS
    grad_scale = 1.0 / math.sqrt(pixels)
    flat_in = inputs.reshape(pixels, CH)
    first_pre = jnp.dot(flat_in, first_weight, preferred_element_type=jnp.float32) + first_bias
    active = jax.nn.silu(first_pre).astype(jnp.bfloat16)
    grid = active.reshape(IMAGES, ROWS, COLS, groups, GW)
    padded = jnp.pad(grid, ((0, 0), (1, 1), (1, 1), (0, 0), (0, 0)))
    kernel = conv_weight.reshape(groups, GW, 9, GW).astype(jnp.float32)
    conv_pre = jnp.zeros((IMAGES, ROWS, COLS, groups, GW), jnp.float32)
    for tap_index in range(9):
        row_shift, col_shift = (tap_index // 3, tap_index % 3)
        shifted = padded[:, row_shift:row_shift + ROWS, col_shift:col_shift + COLS].astype(jnp.float32)
        conv_pre = conv_pre + jnp.einsum('nhwgi,goi->nhwgo', shifted, kernel[:, :, tap_index, :])
    conv_out = conv_pre.reshape(IMAGES, ROWS, COLS, CH) + conv_bias
    hidden = jax.nn.silu(conv_out)
    means = lax.optimization_barrier(jnp.sum(hidden, axis=(1, 2))) / (ROWS * COLS)
    squeeze_pre = jnp.dot(means, squeeze_weight.astype(jnp.float32), precision=highest) + squeeze_bias
    squeeze = jax.nn.silu(squeeze_pre)
    excite = jax.nn.sigmoid(jnp.dot(squeeze, excite_weight.astype(jnp.float32), precision=highest) + excite_bias)
    scaled = (hidden * excite[:, None, None, :]).astype(jnp.bfloat16)
    flat_scaled = scaled.reshape(pixels, CH)
    scaled_blocks = flat_scaled.reshape(pixels, blocks, CH_DEV).transpose(1, 0, 2)
    second = block_sum(scaled_blocks, second_weight.reshape(blocks, CH_DEV, CH))
    total = flat_in.astype(jnp.float32) + second
    block_out = jax.nn.silu(total).astype(jnp.bfloat16)
    back = (cotangent.reshape(pixels, CH).astype(jnp.float32) * slope(total)).astype(jnp.bfloat16)
    second_raw = jnp.dot(flat_scaled.T, back, preferred_element_type=jnp.float32)
    second_grad = jnp.dot(second_basis, jnp.dot(second_basis.T, second_raw, precision=highest), precision=highest) * grad_scale
    scaled_back = jnp.dot(back, second_weight.T, preferred_element_type=jnp.float32).reshape(IMAGES, ROWS, COLS, CH)
    excite_back = lax.optimization_barrier(jnp.sum(scaled_back * hidden, axis=(1, 2)))
    sig_back = excite_back * excite * (1.0 - excite)
    excite_grad = jnp.dot(squeeze.T, sig_back, precision=highest) * grad_scale
    squeeze_back = jnp.dot(sig_back, excite_weight.astype(jnp.float32).T, precision=highest) * slope(squeeze_pre)
    squeeze_grad = jnp.dot(means.T, squeeze_back, precision=highest) * grad_scale
    means_back = jnp.dot(squeeze_back, squeeze_weight.astype(jnp.float32).T, precision=highest)
    hidden_back = ((scaled_back * excite[:, None, None, :] + means_back[:, None, None, :] / (ROWS * COLS)) * slope(conv_out)).astype(jnp.bfloat16)
    back_grid = hidden_back.reshape(IMAGES, ROWS, COLS, groups, GW).astype(jnp.float32)
    back_pad = jnp.pad(back_grid, ((0, 0), (1, 1), (1, 1), (0, 0), (0, 0)))
    conv_parts = []
    active_sum = jnp.zeros((IMAGES, ROWS, COLS, groups, GW), jnp.float32)
    for tap_index in range(9):
        row_shift, col_shift = (tap_index // 3, tap_index % 3)
        shifted = padded[:, row_shift:row_shift + ROWS, col_shift:col_shift + COLS].astype(jnp.float32)
        conv_parts.append(jnp.einsum('nhwgo,nhwgi->goi', back_grid, shifted))
        moved = back_pad[:, 2 - row_shift:2 - row_shift + ROWS, 2 - col_shift:2 - col_shift + COLS]
        active_sum = active_sum + jnp.einsum('nhwgo,goi->nhwgi', moved, kernel[:, :, tap_index, :])
    conv_grad = jnp.stack(conv_parts, axis=2).reshape(CH, 9, GW) * grad_scale
    active_grad = (active_sum.reshape(pixels, CH) * slope(first_pre)).astype(jnp.bfloat16)
    first_raw = jnp.dot(flat_in.T, active_grad, preferred_element_type=jnp.float32)
    first_grad = jnp.dot(first_basis, jnp.dot(first_basis.T, first_raw, precision=highest), precision=highest) * grad_scale
    grad_blocks = active_grad.reshape(pixels, blocks, CH_DEV).transpose(1, 0, 2)
    weight_blocks = first_weight.reshape(CH, blocks, CH_DEV).transpose(1, 2, 0)
    input_sum = back.astype(jnp.float32) + block_sum(grad_blocks, weight_blocks)
    input_grad = input_sum.astype(jnp.bfloat16).reshape(IMAGES, ROWS, COLS, CH)
    return (block_out.reshape(IMAGES, ROWS, COLS, CH), input_grad, first_grad, second_grad, conv_grad, squeeze_grad, excite_grad)
```

```python
import math

import jax
import jax.numpy as jnp
from jax import lax
from jax.experimental import pallas as pl
from jax.experimental.pallas import tpu as pltpu
from jax.sharding import PartitionSpec as P

MESH = pl.DeviceIdType.MESH
highest = lax.Precision.HIGHEST
bf16, f32 = jnp.bfloat16, jnp.float32

TILES = 8
GRP = 32
CH_DEV = 66
CB = 80
PX = 256
GP = 4 * CB
AP = GRP * CB
CI = 272
SQ = 528
SQP = 640
BASIS = 256
ZC = 384
CELLS = 4096.0
NSEM = 240


def flip(index, mask):
    out = index
    for bit in range(5):
        if mask >> bit & 1:
            step = 1 << bit
            out = out + step * (1 - 2 * ((index // step) % 2))
    return out


def sigmoid(v):
    return 1.0 / (1.0 + jnp.exp(-v))


def slope(v):
    sig = sigmoid(v)
    return sig * (1.0 + v * (1.0 - sig))


def dot(a, b):
    return lax.dot_general(a, b, (((1,), (0,)), ((), ())), preferred_element_type=f32)


def dot_nt(a, b):
    return lax.dot_general(a, b, (((1,), (1,)), ((), ())), preferred_element_type=f32)


def pieces(v, count):
    out = []
    for _ in range(count - 1):
        top = v.astype(bf16)
        out.append(top)
        v = v - top.astype(f32)
    out.append(v.astype(bf16))
    return out


def split_left(op, a, b, count=3):
    return sum(op(p, b) for p in pieces(a, count))


def split_right(op, a, b, count=3):
    return sum(op(a, p) for p in pieces(b, count))


def body(
    xq, cq, w1, wc, w2, sm, fp, fbt, sqb,
    bo, ig, zo, sg, se,
    xall, ball, w1g, wcg, w2g, w1t, wct, w2t, smg, fpg,
    ext, extg, ext2, cols, pre, conv_out, hidden, sback, xbt, sbt, zbuf,
    rs_send, rs_own, rs_recv, rs2_send, rs2_recv, bq,
    usend, urecv, c2s, c2r, c2z, c2zr, c2all,
    hs, hz, hb8, es, ez, eb8, hbs, hbr, c1s, c1r, zs, zf, zr, zall,
    send, recv, local,
):
    z = lax.axis_index("tile")
    me = lax.axis_index("grp")
    xx = me // 8
    col = me % 8
    m = me % 4
    g = me // 4
    core = me % 2
    img = (me // 2) % 2
    count = [0]
    started = []
    locals_ = []

    def copy(src, dst, tile, grp):
        i = count[0]
        count[0] += 1
        c = pltpu.make_async_remote_copy(
            src_ref=src, dst_ref=dst, send_sem=send.at[i], recv_sem=recv.at[i],
            device_id=(tile, grp), device_id_type=MESH,
        )
        c.start()
        started.append(c)
        return c

    def keep(src, dst):
        c = pltpu.make_async_copy(src, dst, local.at[len(locals_)])
        c.start()
        locals_.append(c)
        return c

    def peer(mask):
        return flip(me, mask)

    other = (lax.rem(z + 2 * core - 1 + TILES, TILES), flip(me, 1))
    grp_masks = [1, 2, 3, 4, 5, 6, 7, 8, 16, 24, 12, 20, 28]
    g_masks = [4, 8, 12, 16, 20, 24, 28]

    barrier = pltpu.get_barrier_semaphore()
    for mask in grp_masks:
        pl.semaphore_signal(barrier, inc=1, device_id=(z, peer(mask)), device_id_type=MESH)
    for mask in range(1, 8):
        pl.semaphore_signal(barrier, inc=1, device_id=(flip(z, mask), me), device_id_type=MESH)
    pl.semaphore_signal(barrier, inc=1, device_id=other, device_id_type=MESH)
    pl.semaphore_wait(barrier, len(grp_masks) + 8)

    def gather_column(pick, dst, slot):
        return [copy(pick(k), dst.at[slot(0)], z, peer(k)) for k in range(1, 8)]

    def gather_rows(arrived, dst, slot):
        done = []
        for k in range(8):
            if k:
                arrived[k - 1].wait_recv()
            for mask in (8, 16, 24):
                done.append(copy(dst.at[slot(k)], dst.at[slot(k)], z, peer(mask)))
        return done

    def group_start(src, dst):
        mine = keep(src, dst.at[m])
        return mine, copy(src, dst.at[m], z, peer(1)), copy(src, dst.at[m], z, peer(2))

    def group_forward(state, dst):
        mine, near, far = state
        far.wait_recv()
        slot = flip(m, 2)
        return mine, near, copy(dst.at[slot], dst.at[slot], z, peer(1))

    def group_finish(state):
        state[0].wait()
        state[1].wait_recv()
        state[2].wait_recv()

    def halo_start(buf):
        return (
            copy(buf.at[2 - core], buf.at[3 * core], z, peer(1)),
            copy(buf.at[1 + core], buf.at[3 - 3 * core], other[0], other[1]),
        )

    def halo_finish(buf, copies):
        for c in copies:
            c.wait_recv()

        @pl.when((z == 0) & (core == 0))
        def _():
            buf[0] = jnp.zeros(buf.shape[1:], buf.dtype)

        @pl.when((z == TILES - 1) & (core == 1))
        def _():
            buf[3] = jnp.zeros(buf.shape[1:], buf.dtype)

    def wide(buf):
        return jnp.concatenate([buf[0], buf[1], buf[2], buf[3]], axis=1)

    def block(k):
        return flip(me, k)

    xs = gather_column(lambda k: xq.at[flip(m, k & 3)], xall, block)
    s1 = group_start(w1, w1g)
    sc = group_start(wc, wcg)
    ssm = group_start(sm, smg)
    sfp = group_start(fp, fpg)
    s2 = group_start(w2, w2g)
    keep(xq.at[m], xall.at[me]).wait()
    xrows = gather_rows(xs, xall, block)
    s1 = group_forward(s1, w1g)
    sfp_ = group_forward(sfp, fpg)

    row = lax.broadcasted_iota(jnp.int32, (CI, GP), 0)
    lane = lax.broadcasted_iota(jnp.int32, (CI, GP), 1)
    shifted = row
    for part in (1, 2, 3):
        shifted = shifted + jnp.where(row >= CH_DEV * part, CB - CH_DEV, 0)
    pack = jnp.where((shifted == lane) & (row < 4 * CH_DEV), 1.0, 0.0).astype(bf16)
    row_t = lax.broadcasted_iota(jnp.int32, (GP, CI), 1)
    lane_t = lax.broadcasted_iota(jnp.int32, (GP, CI), 0)
    shifted_t = row_t
    for part in (1, 2, 3):
        shifted_t = shifted_t + jnp.where(row_t >= CH_DEV * part, CB - CH_DEV, 0)
    unpack = jnp.where((shifted_t == lane_t) & (row_t < 4 * CH_DEV), 1.0, 0.0).astype(bf16)

    group_finish(s1)
    group_finish(sfp_)
    for c in xrows:
        c.wait_recv()

    x_rows = xall[...].reshape(AP, PX)
    first_pre = dot(w1g[...].reshape(GP, AP), x_rows) + fpg[...].reshape(GP, 384)[:, 0:1]
    active = (first_pre * sigmoid(first_pre)).astype(bf16)
    packed = dot(pack, active).astype(bf16)
    ext[1] = packed[:, 0:128]
    ext[2] = packed[:, 128:256]
    halo = halo_start(ext)
    pre[...] = split_right(dot, pack, first_pre)
    sc = group_forward(sc, wcg)
    ssm = group_forward(ssm, smg)
    s2 = group_forward(s2, w2g)

    cols[...] = jnp.zeros(cols.shape, bf16)

    def build(read, target):
        lanes = lax.broadcasted_iota(jnp.int32, (16, 512), 1) % 64

        def step(i, carry):
            r = pl.multiple_of(i * 16, 16)
            e = jnp.concatenate([read(n, r) for n in range(4)], axis=1).astype(f32)
            for b in (-1, 0, 1):
                if b == 0:
                    v = e
                elif b == 1:
                    v = jnp.where(lanes == 63, 0.0, pltpu.roll(e, 511, 1))
                else:
                    v = jnp.where(lanes == 0, 0.0, pltpu.roll(e, 1, 1))
                s = pltpu.roll(v, 64, 1)
                for a, win in ((-1, s[:, 128:384]), (0, v[:, 128:384]), (1, s[:, 256:512])):
                    t = 3 * (a + 1) + b + 1
                    target[pl.ds(pl.multiple_of(t * CI + r, 16), 16), :] = win.astype(bf16)
            return carry

        lax.fori_loop(0, CI // 16, step, 0)

    halo_finish(ext, halo)
    sext = group_start(ext, extg)
    build(lambda n, r: ext[n, pl.ds(r, 16), :], cols)
    group_finish(sc)

    co = dot(wcg[...].reshape(GP, AP), cols[...]) + fpg[...].reshape(GP, 384)[:, 1:2]
    conv_out[...] = co
    hid = co * sigmoid(co)
    hidden[...] = hid
    ones = jnp.ones((8, PX), bf16)
    images = lax.broadcasted_iota(jnp.int32, (8, GP), 0)

    def sums_start(v, buf):
        buf[0] = jnp.zeros((8, 384), f32)
        buf[0, :, 0:GP] = jnp.where(images == img, split_right(dot_nt, ones, v), 0.0)
        return [copy(buf.at[0], buf.at[k], z, peer(k)) for k in range(1, 4)]

    def sums_tiles(copies, buf, wider):
        for c in copies:
            c.wait_recv()
        wider[0] = buf[0] + buf[1] + buf[2] + buf[3]
        return [copy(wider.at[0], wider.at[k], flip(z, k), me) for k in range(1, 8)]

    def sums_finish(copies, wider):
        for c in copies:
            c.wait_recv()
        return sum(wider[k] for k in range(8))[:, 0:GP]

    def squeeze_start(v, buf):
        buf[0] = v
        return [copy(buf.at[0], buf.at[n + 1], z, peer(k)) for n, k in enumerate(g_masks)]

    def squeeze_finish(copies, buf):
        for c in copies:
            c.wait_recv()
        return sum(buf[n] for n in range(8))

    ah = sums_start(hid, hs)

    def transposed(src, dst):
        def step(j, carry):
            at = pl.multiple_of(j * 128, 128)
            v = src[:, :, pl.ds(at, 128)].reshape(GP, 128)
            dst[pl.ds(at, 128), :] = v.T
            return carry

        lax.fori_loop(0, AP // 128, step, 0)

    sh = sums_tiles(ah, hs, hz)
    group_finish(ssm)
    group_finish(s2)
    transposed(w2g, w2t)
    sb = fpg[...].reshape(GP, 384)[:, 128:384]
    sb_top = sb.astype(bf16)
    sbt[0:BASIS, :] = sb_top.T
    sbt[BASIS:, :] = (sb - sb_top.astype(f32)).astype(bf16).T
    means = sums_finish(sh, hz) * (1.0 / CELLS)
    sq_w = smg[:, :, 0:SQP].reshape(GP, SQP)
    ex_w = smg[:, :, SQP:].reshape(GP, SQP)
    bh = squeeze_start(split_left(dot, means, sq_w), hb8)
    sext = group_forward(sext, extg)
    xb2 = dot(fbt[...], x_rows)
    xb = xb2[0:BASIS] + xb2[BASIS:]
    xb_top = xb.astype(bf16)
    xbt[0:BASIS, :] = xb_top
    xbt[BASIS:, :] = (xb - xb_top.astype(f32)).astype(bf16)
    squeeze_pre = squeeze_finish(bh, hb8) + sqb[...]
    squeeze = squeeze_pre * sigmoid(squeeze_pre)
    ex_logit = split_right(dot_nt, ex_w, squeeze) + fpg[...].reshape(GP, 384)[:, 2:3]
    excite = sigmoid(ex_logit)
    ex_col = jnp.where(img == 0, excite[:, 0:1], excite[:, 1:2])
    scaled = (hidden[...] * ex_col).astype(bf16)

    def reduce_start(left, right, inner):
        out = []
        for k in (3, 2, 1, 0):
            at = pl.multiple_of(flip(xx, k) * (8 * CB), 128)
            p = dot(left[pl.ds(at, 8 * CB), :], right)
            if k:
                rs_send[inner, k] = p.astype(bf16).reshape(8, CB, PX)
                out.append(copy(rs_send.at[inner, k], rs_recv.at[inner, k], z, peer(8 * k)))
            else:
                rs_own[...] = p
        return out

    def reduce_column(copies, inner):
        for c in copies:
            c.wait_recv()
        total = rs_own[...]
        for k in (1, 2, 3):
            total = total + rs_recv[inner, k].reshape(8 * CB, PX).astype(f32)
        rs2_send[inner] = total.astype(bf16).reshape(8, CB, PX)
        return [
            copy(rs2_send.at[inner, flip(col, k)], rs2_recv.at[inner, k], z, peer(k))
            for k in range(1, 8)
        ]

    def reduce_quarter(copies, inner, kk):
        copies[kk + 3].wait_recv()
        if kk:
            copies[kk - 1].wait_recv()
            first = rs2_recv[inner, kk]
        else:
            first = rs2_send[inner, col]
        return first.astype(f32) + rs2_recv[inner, kk + 4].astype(f32)

    r1 = reduce_start(w2t, scaled, 0)
    u2 = dot(sbt[...], scaled)
    usend[...] = (u2[0:BASIS] + u2[BASIS:]).astype(bf16).reshape(8, 32, PX)
    us = [copy(usend.at[flip(g, k // 4)], urecv.at[n + 1], z, peer(k)) for n, k in enumerate(g_masks)]
    transposed(w1g, w1t)
    transposed(wcg, wct)
    c2cols = reduce_column(r1, 0)
    back_copies = [None] * 7
    for kk in range(4):
        q = flip(m, kk)
        total = xq[q].astype(f32) + reduce_quarter(c2cols, 0, kk)
        sig = sigmoid(total)
        bo[q] = (total * sig).astype(bf16)
        bq[q] = (cq[q].astype(f32) * (sig * (1.0 + total * (1.0 - sig)))).astype(bf16)
        for k in (kk, kk + 4):
            if k:
                back_copies[k - 1] = copy(bq.at[q], ball.at[me], z, peer(k))
    ball[me] = bq[m]
    brows = gather_rows(back_copies, ball, block)
    group_finish(sext)
    for c in us:
        c.wait_recv()
    u_own = usend[g].astype(f32)
    for n in range(1, 8):
        u_own = u_own + urecv[n].astype(f32)
    u_top = u_own.astype(bf16)
    u_low = (u_own - u_top.astype(f32)).astype(bf16)
    for c in brows:
        c.wait_recv()

    back_rows = ball[...].reshape(AP, PX)
    scaled_back = dot(w2g[...].reshape(GP, AP), back_rows)
    sback[...] = scaled_back
    ae = sums_start(scaled_back * hidden[...], es)
    coords = dot_nt(u_top, back_rows) + dot_nt(u_low, back_rows)
    se_ = sums_tiles(ae, es, ez)
    for k in range(4):
        c2s[k] = coords[:, 640 * k : 640 * (k + 1)].astype(bf16)
    c2g = [copy(c2s.at[flip(m, k)], c2r.at[k], z, peer(k)) for k in range(1, 4)]
    ex_row = sigmoid(
        split_left(dot_nt, squeeze, ex_w)
        + split_right(
            dot_nt,
            jnp.where(lax.broadcasted_iota(jnp.int32, (8, 128), 1) == 2, 1.0, 0.0).astype(bf16),
            fpg[...].reshape(GP, 384)[:, 0:128],
        )
    )
    excite_back = sums_finish(se_, ez)
    sig_back = excite_back * ex_row * (1.0 - ex_row)
    be = squeeze_start(split_left(dot, sig_back, ex_w), eb8)
    for c in c2g:
        c.wait_recv()
    c2 = c2s[m].astype(f32) + c2r[1].astype(f32) + c2r[2].astype(f32) + c2r[3].astype(f32)
    c2z[...] = c2.astype(bf16)
    c2t = [copy(c2z, c2zr.at[k], flip(z, k), me) for k in range(1, 8)]
    squeeze_back = squeeze_finish(be, eb8) * slope(squeeze_pre)
    means_back = split_right(dot_nt, sq_w, squeeze_back)
    mb_col = jnp.where(img == 0, means_back[:, 0:1], means_back[:, 1:2]) * (1.0 / CELLS)
    hb = ((sback[...] * ex_col + mb_col) * slope(conv_out[...])).astype(bf16)
    ext2[1] = hb[:, 0:128]
    ext2[2] = hb[:, 128:256]
    halo2 = halo_start(ext2)
    hbs[...] = hb.reshape(4, CB, PX)
    hsw = [copy(hbs.at[flip(m, k)], hbr.at[k], z, peer(k)) for k in range(1, 4)]
    se[0] = jnp.zeros((8, SQP), f32)
    se[1] = jnp.zeros((8, SQP), f32)
    se[0, :, 0:GP] = means
    se[1, :, 0:GP] = sig_back
    se[2] = squeeze
    se[3] = squeeze_back

    for c in c2t:
        c.wait_recv()
    c2 = c2z[...].astype(f32)
    for k in range(1, 8):
        c2 = c2 + c2zr[k].astype(f32)

    def slot2(k):
        return flip(m, k & 3) * 8 + flip(g, k >> 2)

    c2all[slot2(0)] = c2.astype(bf16)
    c2c = gather_column(lambda k: c2all.at[slot2(0)], c2all, slot2)
    halo_finish(ext2, halo2)

    zbuf[...] = dot(wct[...], wide(ext2))
    lanes8 = lax.broadcasted_iota(jnp.int32, (16, PX), 1) % 64

    def gathered(i, carry):
        r = pl.multiple_of(i * 16, 16)
        acc = jnp.zeros((16, PX), f32)
        for b in (-1, 0, 1):
            up = zbuf[pl.ds(pl.multiple_of(CI * (b + 1) + r, 16), 16), :]
            mid = zbuf[pl.ds(pl.multiple_of(CI * (b + 4) + r, 16), 16), :]
            down = zbuf[pl.ds(pl.multiple_of(CI * (b + 7) + r, 16), 16), :]
            y = mid[:, 128:384] + pltpu.roll(up, 64, 1)[:, 256:512] + pltpu.roll(down, 64, 1)[:, 128:384]
            if b == 1:
                y = jnp.where(lanes8 == 0, 0.0, pltpu.roll(y, 1, 1))
            elif b == -1:
                y = jnp.where(lanes8 == 63, 0.0, pltpu.roll(y, PX - 1, 1))
            acc = acc + y
        pre[pl.ds(r, 16), :] = acc * slope(pre[pl.ds(r, 16), :])
        return carry

    lax.fori_loop(0, CI // 16, gathered, 0)
    ag = dot(unpack, pre[...].astype(bf16)).astype(bf16)
    r2 = reduce_start(w1t, ag, 1)
    c2rows = gather_rows(c2c, c2all, slot2)

    c1 = dot_nt(ag, xbt[0:BASIS, :]) + dot_nt(ag, xbt[BASIS:, :])
    c1s[...] = c1.astype(bf16).reshape(4, CB, BASIS)
    c1g = [copy(c1s.at[flip(m, k)], c1r.at[k], z, peer(k)) for k in range(1, 4)]
    for c in hsw:
        c.wait_recv()
    grads = dot_nt(hbs[m], cols[...])
    for k in range(1, 4):
        q = flip(m, k)
        build(lambda n, r: extg[q, n, pl.ds(r, 16), :], cols)
        grads = grads + dot_nt(hbr[k], cols[...])
    for c in c1g:
        c.wait_recv()
    c1 = c1s[m].astype(f32) + c1r[1].astype(f32) + c1r[2].astype(f32) + c1r[3].astype(f32)
    both = jnp.concatenate([grads, c1, jnp.zeros((CB, TILES * ZC - AP - BASIS), f32)], axis=1)
    for k in range(TILES):
        zf[k] = both[:, ZC * k : ZC * (k + 1)]
        zs[k] = both[:, ZC * k : ZC * (k + 1)].astype(bf16)
    z1 = [copy(zs.at[flip(z, k)], zr.at[k], flip(z, k), me) for k in range(1, 8)]
    c2cols = reduce_column(r2, 1)
    for c in z1:
        c.wait_recv()
    chunk = zf[z]
    for k in range(1, 8):
        chunk = chunk + zr[k].astype(f32)
    zall[z] = chunk.astype(bf16)
    z2 = [copy(zall.at[z], zall.at[z], flip(z, k), me) for k in range(1, 8)]
    for kk in range(4):
        q = flip(m, kk)
        ig[q] = (bq[q].astype(f32) + reduce_quarter(c2cols, 1, kk)).astype(bf16)
    for c in c2rows:
        c.wait_recv()
    own = fp[:, 128:384]
    own_top = own.astype(bf16)
    own_low = (own - own_top.astype(f32)).astype(bf16)
    for k in range(4):
        rows = c2all[8 * k : 8 * (k + 1)].reshape(BASIS, 640)
        sg[:, 640 * k : 640 * (k + 1)] = dot(own_top, rows) + dot(own_low, rows)
    for c in z2:
        c.wait_recv()
    zo[...] = zall[...]
    for c in started:
        c.wait_send()


def per_device(
    inputs,
    cotangent,
    first_weight,
    first_bias,
    conv_weight,
    conv_bias,
    squeeze_weight,
    squeeze_bias,
    excite_weight,
    excite_bias,
    second_weight,
    first_basis,
    second_basis,
):
    grad_scale = 1.0 / math.sqrt(8192.0)

    def quarters(v):
        v = v.reshape(2, 2, PX, CH_DEV).transpose(0, 1, 3, 2)
        return jnp.pad(v, ((0, 0), (0, 0), (0, CB - CH_DEV), (0, 0))).reshape(4, CB, PX)

    def spread(v):
        v = v.reshape(CH_DEV, GRP, CH_DEV)
        return jnp.pad(v, ((0, CB - CH_DEV), (0, 0), (0, CB - CH_DEV))).reshape(CB, AP)

    xq, cq = quarters(inputs), quarters(cotangent)
    w1 = spread(first_weight.T)
    w2 = spread(second_weight)
    wc = jnp.pad(conv_weight, ((0, CB - CH_DEV), (0, 0), (0, CI - 264))).reshape(CB, 9 * CI)
    wc = jnp.pad(wc, ((0, 0), (0, AP - 9 * CI)))
    side = ((0, CB - CH_DEV), (0, SQP - SQ))
    sm = jnp.concatenate([jnp.pad(squeeze_weight, side), jnp.pad(excite_weight.T, side)], axis=1)
    biases = jnp.stack([first_bias, conv_bias, excite_bias], axis=1)
    fp = jnp.concatenate([jnp.pad(biases, ((0, 0), (0, 125))), second_basis], axis=1)
    fp = jnp.pad(fp, ((0, CB - CH_DEV), (0, 0)))
    fb = first_basis.reshape(GRP, CH_DEV, BASIS)
    fb = jnp.pad(fb, ((0, 0), (0, CB - CH_DEV), (0, 0))).reshape(AP, BASIS).T
    fb_top = fb.astype(bf16)
    fbt = jnp.concatenate([fb_top, (fb - fb_top.astype(f32)).astype(bf16)], axis=0)
    sqb = jnp.broadcast_to(jnp.pad(squeeze_bias, (0, SQP - SQ))[None], (8, SQP))

    V = pltpu.VMEM
    scratch = [
        V((GRP, CB, PX), bf16),
        V((GRP, CB, PX), bf16),
        V((4, CB, AP), bf16),
        V((4, CB, AP), bf16),
        V((4, CB, AP), bf16),
        V((AP, GP), bf16),
        V((AP, GP), bf16),
        V((AP, GP), bf16),
        V((4, CB, 2 * SQP), bf16),
        V((4, CB, 384), f32),
        V((4, CI, 128), bf16),
        V((4, 4, CI, 128), bf16),
        V((4, GP, 128), bf16),
        V((AP, PX), bf16),
        V((CI, PX), f32),
        V((GP, PX), f32),
        V((GP, PX), f32),
        V((GP, PX), f32),
        V((2 * BASIS, PX), bf16),
        V((2 * BASIS, GP), bf16),
        V((AP, 512), f32),
        V((2, 4, 8, CB, PX), bf16),
        V((8 * CB, PX), f32),
        V((2, 4, 8, CB, PX), bf16),
        V((2, 8, CB, PX), bf16),
        V((2, 8, CB, PX), bf16),
        V((4, CB, PX), bf16),
        V((8, 32, PX), bf16),
        V((8, 32, PX), bf16),
        V((4, 32, 640), bf16),
        V((4, 32, 640), bf16),
        V((32, 640), bf16),
        V((8, 32, 640), bf16),
        V((32, 32, 640), bf16),
        V((4, 8, 384), f32),
        V((8, 8, 384), f32),
        V((8, 8, SQP), f32),
        V((4, 8, 384), f32),
        V((8, 8, 384), f32),
        V((8, 8, SQP), f32),
        V((4, CB, PX), bf16),
        V((4, CB, PX), bf16),
        V((4, CB, BASIS), bf16),
        V((4, CB, BASIS), bf16),
        V((TILES, CB, ZC), bf16),
        V((TILES, CB, ZC), f32),
        V((TILES, CB, ZC), bf16),
        V((TILES, CB, ZC), bf16),
        pltpu.SemaphoreType.DMA((NSEM,)),
        pltpu.SemaphoreType.DMA((NSEM,)),
        pltpu.SemaphoreType.DMA((16,)),
    ]
    spec = pl.BlockSpec(memory_space=pltpu.VMEM)
    shape = jax.ShapeDtypeStruct
    bo, ig, zo, sg, se = pl.pallas_call(
        body,
        out_shape=[
            shape((4, CB, PX), bf16),
            shape((4, CB, PX), bf16),
            shape((TILES, CB, ZC), bf16),
            shape((CB, AP), f32),
            shape((4, 8, SQP), f32),
        ],
        in_specs=[spec] * 9,
        out_specs=[spec] * 5,
        scratch_shapes=scratch,
        compiler_params=pltpu.CompilerParams(
            collective_id=0, has_side_effects=True, vmem_limit_bytes=60 * 1024 * 1024
        ),
    )(xq, cq, w1, wc, w2, sm, fp, fbt, sqb)

    def pixels(v):
        v = v[:, :CH_DEV].reshape(2, 2, CH_DEV, PX).transpose(0, 1, 3, 2)
        return v.reshape(inputs.shape)

    sums = zo.transpose(1, 0, 2).reshape(CB, TILES * ZC)[:CH_DEV].astype(f32) * grad_scale
    conv_grad = sums[:, : 9 * CI].reshape(CH_DEV, 9, CI)[:, :, :264]
    first_grad = jnp.dot(first_basis, sums[:, AP : AP + BASIS].T, precision=highest)
    second_grad = (sg[:CH_DEV] * grad_scale).reshape(CH_DEV, GRP, CB)[:, :, :CH_DEV].reshape(CH_DEV, 2112)
    at = (lax.axis_index("grp") % 4) * CB
    means = lax.dynamic_slice(se[0], (0, at), (2, CH_DEV))
    sig_back = lax.dynamic_slice(se[1], (0, at), (2, CH_DEV))
    squeeze, squeeze_back = se[2, :2, :SQ], se[3, :2, :SQ]
    squeeze_grad = (means[0][:, None] * squeeze_back[0] + means[1][:, None] * squeeze_back[1]) * grad_scale
    excite_grad = (sig_back[0] * squeeze[0][:, None] + sig_back[1] * squeeze[1][:, None]) * grad_scale
    return (pixels(bo), pixels(ig), first_grad, second_grad, conv_grad, squeeze_grad, excite_grad)


def solution(mesh):
    placed = (
        P(None, "tile", None, "grp"),
        P(None, "tile", None, "grp"),
        P(None, "grp"),
        P("grp"),
        P("grp", None, None),
        P("grp"),
        P("grp", None),
        P(),
        P(None, "grp"),
        P("grp"),
        P("grp", None),
        P(),
        P("grp", None),
    )
    return jax.shard_map(
        per_device,
        mesh=mesh,
        in_specs=placed,
        out_specs=(
            P(None, "tile", None, "grp"),
            P(None, "tile", None, "grp"),
            P(None, "grp"),
            P("grp", None),
            P("grp", None, None),
            P("grp", None),
            P(None, "grp"),
        ),
        check_vma=False,
    )
```

```python
import math

import jax
import jax.numpy as jnp
from jax import lax
from jax.experimental import pallas as pl
from jax.experimental.pallas import tpu as pltpu
from jax.sharding import PartitionSpec as P

MESH = pl.DeviceIdType.MESH
highest = lax.Precision.HIGHEST
bf16, f32 = jnp.bfloat16, jnp.float32

TILES = 8
GRP = 32
CH_DEV = 66
CB = 80
PX = 256
GP = 4 * CB
AP = GRP * CB
CI = 272
SQ = 528
SQP = 640
BASIS = 256
ZC = 384
CELLS = 4096.0
NSEM = 250
RAW = 2176
NCH = 2112
GRAD_SCALE = 1.0 / math.sqrt(8192.0)


def flip(index, mask):
    out = index
    for bit in range(5):
        if mask >> bit & 1:
            step = 1 << bit
            out = out + step * (1 - 2 * ((index // step) % 2))
    return out


def sigmoid(v):
    return 1.0 / (1.0 + jnp.exp(-v))


def slope(v):
    sig = sigmoid(v)
    return sig * (1.0 + v * (1.0 - sig))


def dot(a, b):
    return lax.dot_general(a, b, (((1,), (0,)), ((), ())), preferred_element_type=f32)


def dot_nt(a, b):
    return lax.dot_general(a, b, (((1,), (1,)), ((), ())), preferred_element_type=f32)


def pieces(v, count):
    out = []
    for _ in range(count - 1):
        top = v.astype(bf16)
        out.append(top)
        v = v - top.astype(f32)
    out.append(v.astype(bf16))
    return out


def dot_tn(a, b):
    return lax.dot_general(a, b, (((0,), (0,)), ((), ())), preferred_element_type=f32)


def one_hot(rows, row_start, lanes, lane_start, out_width, in_width):
    r = lax.broadcasted_iota(jnp.int32, (rows, lanes), 0) + row_start
    out = lax.broadcasted_iota(jnp.int32, (rows, lanes), 1) + lane_start
    blk = (out * ((1 << 22) // out_width + 1)) >> 22
    hit = (out - out_width * blk < CH_DEV) & (r == out + (in_width - out_width) * blk) & (blk < GRP)
    return jnp.where(hit, 1.0, 0.0).astype(bf16)


def windows(out_lanes, out_width, in_lanes, in_width):
    for start in range(0, out_lanes, 256):
        width = min(256, out_lanes - start)
        low = min(start // out_width * in_width // 128 * 128, in_lanes - 512)
        yield start, width, low


def split_left(op, a, b, count=3):
    return sum(op(p, b) for p in pieces(a, count))


def split_right(op, a, b, count=3):
    return sum(op(a, p) for p in pieces(b, count))


def body(
    xq, cq, w1, wc, w2, sqw, exw, sb_in, fb_in, side,
    bo, ig, fg, sg, cg, sqg, exg,
    xall, ball, w1p, w2p, wcp, smp, bip, w1r, w2r, w1g, wcg, w2g, smg, big,
    hots, hots2, fbp, fbn,
    ext, extg, exts, exta, cols, pre, conv_out, hidden, sback, xbt, zbuf,
    rs_far, rs_rel, rs_keep, rs_out, rs_in, rs_own, rs2_send, rs2_recv, bq,
    usend, urecv, c2s, c2r, c2z, c2zr, c2all,
    hs, hz, hb8, es, ez, eb8, hbs, hbr, c1s, c1r, zs, zf, zr, zall,
    send, recv, local,
):
    z = lax.axis_index("tile")
    me = lax.axis_index("grp")
    xx = me // 8
    col = me % 8
    m = me % 4
    g = me // 4
    core = me % 2
    img = (me // 2) % 2
    count = [0]
    started = []
    locals_ = []

    def copy(src, dst, tile, grp):
        i = count[0]
        count[0] += 1
        c = pltpu.make_async_remote_copy(
            src_ref=src, dst_ref=dst, send_sem=send.at[i], recv_sem=recv.at[i],
            device_id=(tile, grp), device_id_type=MESH,
        )
        c.start()
        started.append(c)
        return c

    def keep(src, dst):
        c = pltpu.make_async_copy(src, dst, local.at[len(locals_)])
        c.start()
        locals_.append(c)
        return c

    def peer(mask):
        return flip(me, mask)

    right, left = lax.rem(me + 8, GRP), lax.rem(me + 24, GRP)
    other = (lax.rem(z + 2 * core - 1 + TILES, TILES), flip(me, 1))
    grp_masks = [1, 2, 3, 4, 5, 6, 7, 8, 16, 24, 12, 20, 28]
    g_masks = [4, 8, 12, 16, 20, 24, 28]

    barrier = pltpu.get_barrier_semaphore()
    for mask in grp_masks:
        pl.semaphore_signal(barrier, inc=1, device_id=(z, peer(mask)), device_id_type=MESH)
    for mask in range(1, 8):
        pl.semaphore_signal(barrier, inc=1, device_id=(flip(z, mask), me), device_id_type=MESH)
    pl.semaphore_signal(barrier, inc=1, device_id=other, device_id_type=MESH)

    w1p[...] = jnp.zeros(w1p.shape, bf16)
    w1p[0:CH_DEV, 0:NCH] = w1[...]
    bip[...] = jnp.zeros(bip.shape, f32)
    bip[:, 0:8] = side[8:16, 0:128].T[0:CB]
    pl.semaphore_wait(barrier, len(grp_masks) + 8)

    def gather_column(pick, dst, slot, masks=range(1, 8)):
        return [copy(pick(k), dst.at[slot(me, 0)], z, peer(k)) for k in masks]

    def ring_start(arrived, dst, slot, masks=range(8)):
        to_right, to_left = [], []
        for n, k in enumerate(masks):
            if n:
                arrived[n - 1].wait_recv()
            at = slot(me, k)
            to_right.append(copy(dst.at[at], dst.at[at], z, right))
            to_left.append(copy(dst.at[at], dst.at[at], z, left))
        return to_right, to_left

    def ring_relay(state, dst, slot, masks=range(8)):
        to_right, to_left = state
        half = len(masks) // 2
        relayed = []
        for n in range(half):
            to_right[n].wait_recv()
            at = slot(left, masks[n])
            relayed.append(copy(dst.at[at], dst.at[at], z, right))
            to_left[n + half].wait_recv()
            at = slot(right, masks[n + half])
            relayed.append(copy(dst.at[at], dst.at[at], z, left))
        return to_right[half:] + to_left[:half] + relayed

    def group_start(src, dst):
        mine = keep(src, dst.at[m])
        return mine, copy(src, dst.at[m], z, peer(1)), copy(src, dst.at[m], z, peer(2))

    def group_forward(state, dst):
        mine, near, far = state
        far.wait_recv()
        slot = flip(m, 2)
        return mine, near, copy(dst.at[slot], dst.at[slot], z, peer(1))

    def group_finish(state):
        state[0].wait()
        state[1].wait_recv()
        state[2].wait_recv()

    def halo_start(buf):
        return (
            copy(buf.at[2 - core], buf.at[3 * core], z, peer(1)),
            copy(buf.at[1 + core], buf.at[3 - 3 * core], other[0], other[1]),
        )

    def halo_finish(buf, copies):
        for c in copies:
            c.wait_recv()

        @pl.when((z == 0) & (core == 0))
        def _():
            buf[0] = jnp.zeros(buf.shape[1:], buf.dtype)

        @pl.when((z == TILES - 1) & (core == 1))
        def _():
            buf[3] = jnp.zeros(buf.shape[1:], buf.dtype)

    def block(device, k):
        return flip(device, k)

    def bias(n):
        return big[...].reshape(GP, 128)[:, n : n + 1]

    def spread(source, target):
        for n, (start, width, low) in enumerate(windows(AP, CB, RAW, CH_DEV)):
            v = dot(source[:, :, low : low + 512].reshape(GP, 512), hots[n])
            target[:, start : start + 256] = v.astype(bf16)

    xs = gather_column(lambda k: xq.at[flip(m, k & 3)], xall, block)
    s1 = group_start(w1p, w1r)
    sbi = group_start(bip, big)
    keep(xq.at[m], xall.at[me]).wait()
    xring = ring_start(xs, xall, block)
    wcp[...] = jnp.zeros(wcp.shape, bf16)
    for t in range(9):
        wcp[0:CH_DEV, CI * t : CI * t + 264] = wc[t]
    xrows = ring_relay(xring, xall, block)
    sc = group_start(wcp, wcg)
    for n, (start, width, low) in enumerate(windows(AP, CB, RAW, CH_DEV)):
        hots[n] = one_hot(512, low, 256, start, CB, CH_DEV)
    s1 = group_forward(s1, w1r)
    sbi = group_forward(sbi, big)
    smp[...] = jnp.zeros(smp.shape, bf16)
    smp[0:CH_DEV, 0:SQ] = sqw[...]
    smp[0:CH_DEV, SQP : SQP + SQ] = exw[...]
    sb = sb_in[...]
    sb_top = sb.astype(bf16)
    smp[0:CH_DEV, 2 * SQP : 2 * SQP + BASIS] = sb_top
    smp[0:CH_DEV, 2 * SQP + BASIS :] = (sb - sb_top.astype(f32)).astype(bf16)
    w2p[...] = jnp.zeros(w2p.shape, bf16)
    w2p[0:CH_DEV, 0:NCH] = w2[...]

    def packing(shape, packed_dim):
        row = lax.broadcasted_iota(jnp.int32, shape, packed_dim)
        lane = lax.broadcasted_iota(jnp.int32, shape, 1 - packed_dim)
        shifted = row
        for part in (1, 2, 3):
            shifted = shifted + jnp.where(row >= CH_DEV * part, CB - CH_DEV, 0)
        return jnp.where((shifted == lane) & (row < 4 * CH_DEV), 1.0, 0.0).astype(bf16)

    group_finish(s1)
    spread(w1r, w1g)
    group_finish(sbi)
    for c in xrows:
        c.wait_recv()

    x_rows = xall[...].reshape(AP, PX)
    first_pre = dot(w1g[...], x_rows) + bias(0)
    active = (first_pre * sigmoid(first_pre)).astype(bf16)
    pack = packing((CI, GP), 0)
    packed = dot(pack, active).astype(bf16)
    ext[1] = packed[:, 0:128]
    ext[2] = packed[:, 128:256]
    halo = halo_start(ext)
    ssm = group_start(smp, smg)
    s2 = group_start(w2p, w2r)
    pre[...] = split_right(dot, pack, first_pre)
    sc = group_forward(sc, wcg)
    for k in range(4):
        cols[k, 9 * CI :, :] = jnp.zeros((AP - 9 * CI, PX), bf16)

    def build(read, n_target):
        lanes = lax.broadcasted_iota(jnp.int32, (16, 512), 1) % 64
        for i in range(CI // 16):
            r = 16 * i
            e = jnp.concatenate([read(n, r) for n in range(4)], axis=1).astype(f32)
            for b in (-1, 0, 1):
                if b == 0:
                    v = e
                elif b == 1:
                    v = jnp.where(lanes == 63, 0.0, pltpu.roll(e, 511, 1))
                else:
                    v = jnp.where(lanes == 0, 0.0, pltpu.roll(e, 1, 1))
                s = pltpu.roll(v, 64, 1)
                for a, win in ((-1, s[:, 128:384]), (0, v[:, 128:384]), (1, s[:, 256:512])):
                    t = 3 * (a + 1) + b + 1
                    cols[n_target, t * CI + r : t * CI + r + 16, :] = win.astype(bf16)

    halo_finish(ext, halo)
    build(lambda n, r: ext[n, r : r + 16, :], 0)
    group_finish(sc)

    co = dot(wcg[...].reshape(GP, AP), cols[0]) + bias(1)
    conv_out[...] = co
    hid = co * sigmoid(co)
    hidden[...] = hid
    ones = jnp.ones((8, PX), bf16)
    rows8 = lax.broadcasted_iota(jnp.int32, (8, 128), 0)

    def sums_start(v, buf):
        tile = jnp.zeros((8, 128), f32)
        for j in range(3):
            part = v[128 * j : min(128 * (j + 1), GP)]
            if j == 2:
                part = jnp.concatenate([part, jnp.zeros((64, PX), f32)], axis=0)
            tile = jnp.where(rows8 == 3 * img + j, split_right(dot_nt, ones, part), tile)
        buf[0] = tile
        return [copy(buf.at[0], buf.at[k], z, peer(k)) for k in range(1, 4)]

    def sums_tiles(copies, buf, wider):
        for c in copies:
            c.wait_recv()
        wider[0] = buf[0] + buf[1] + buf[2] + buf[3]
        return [copy(wider.at[0], wider.at[k], flip(z, k), me) for k in (4, 3, 5, 2, 6, 1, 7)]

    def sums_finish(copies, wider):
        for c in copies:
            c.wait_recv()
        tile = sum(wider[k] for k in range(8))
        parts = [
            jnp.where(rows8 == 0, tile[j : j + 1], jnp.where(rows8 == 1, tile[3 + j : 4 + j], 0.0))
            for j in range(3)
        ]
        return jnp.concatenate(parts, axis=1)[:, 0:GP]

    def squeeze_start(v, buf):
        low, high = jnp.zeros((8, 128), f32), jnp.zeros((8, 128), f32)
        for j in range(5):
            part = v[:, 128 * j : 128 * (j + 1)]
            low = jnp.where(rows8 == j, part[0:1], low)
            high = jnp.where(rows8 == j, part[1:2], high)
        buf[0, 0] = low
        buf[0, 1] = high
        return [copy(buf.at[0], buf.at[n + 1], z, peer(k)) for n, k in enumerate(g_masks)]

    def squeeze_finish(copies, buf):
        for c in copies:
            c.wait_recv()
        low = sum(buf[n, 0] for n in range(8))
        high = sum(buf[n, 1] for n in range(8))
        parts = [
            jnp.where(rows8 == 0, low[j : j + 1], jnp.where(rows8 == 1, high[j : j + 1], 0.0))
            for j in range(5)
        ]
        return jnp.concatenate(parts, axis=1)

    ah = sums_start(hid, hs)
    ssm = group_forward(ssm, smg)
    sext = group_start(ext, extg)
    sh = sums_tiles(ah, hs, hz)
    s2 = group_forward(s2, w2r)
    group_finish(ssm)
    means = sums_finish(sh, hz) * (1.0 / CELLS)
    sq_w = smg[:, :, 0:SQP].reshape(GP, SQP)
    ex_w = smg[:, :, SQP : 2 * SQP].reshape(GP, SQP)
    bh = squeeze_start(split_left(dot, means, sq_w), hb8)
    group_finish(s2)
    spread(w2r, w2g)
    squeeze_pre = squeeze_finish(bh, hb8) + side[0:8]
    squeeze = squeeze_pre * sigmoid(squeeze_pre)
    excite = sigmoid(split_right(dot_nt, ex_w, squeeze) + bias(2))
    ex_col = jnp.where(img == 0, excite[:, 0:1], excite[:, 1:2])
    scaled = (hidden[...] * ex_col).astype(bf16)

    def reduce_start(weights, rhs, inner):
        def part(step):
            at = pl.multiple_of(lax.rem(xx + step, 4) * (8 * CB), 128)
            return dot_tn(weights[:, pl.ds(at, 8 * CB)], rhs).reshape(8, CB, PX)

        rs_far[inner] = part(2).astype(bf16)
        far = [
            copy(rs_far.at[inner, 0:4], rs_rel.at[inner, 0], z, right),
            copy(rs_far.at[inner, 4:8], rs_rel.at[inner, 1], z, left),
        ]
        p = part(1)
        rs_out[inner, 0, 4:8] = p[4:8].astype(bf16)
        near = [copy(rs_out.at[inner, 0, 4:8], rs_in.at[inner, 0, 4:8], z, right)]
        rs_keep[0] = p[0:4]
        p = part(3)
        rs_out[inner, 1, 0:4] = p[0:4].astype(bf16)
        near.append(copy(rs_out.at[inner, 1, 0:4], rs_in.at[inner, 1, 0:4], z, left))
        rs_keep[1] = p[4:8]
        rs_own[...] = part(0)
        return far, near

    def reduce_relay(state, inner):
        far, near = state
        far[0].wait_recv()
        rs_out[inner, 0, 0:4] = (rs_keep[0] + rs_rel[inner, 0].astype(f32)).astype(bf16)
        near.append(copy(rs_out.at[inner, 0, 0:4], rs_in.at[inner, 0, 0:4], z, right))
        far[1].wait_recv()
        rs_out[inner, 1, 4:8] = (rs_keep[1] + rs_rel[inner, 1].astype(f32)).astype(bf16)
        near.append(copy(rs_out.at[inner, 1, 4:8], rs_in.at[inner, 1, 4:8], z, left))
        return near

    def reduce_column(copies, inner):
        for c in copies:
            c.wait_recv()
        total = rs_own[...] + rs_in[inner, 0].astype(f32) + rs_in[inner, 1].astype(f32)
        rs2_send[inner] = total.astype(bf16)
        return [
            copy(rs2_send.at[inner, flip(col, k)], rs2_recv.at[inner, k], z, peer(k))
            for k in range(1, 8)
        ]

    def reduce_quarter(copies, inner, kk):
        copies[kk + 3].wait_recv()
        if kk:
            copies[kk - 1].wait_recv()
            first = rs2_recv[inner, kk]
        else:
            first = rs2_send[inner, col]
        return first.astype(f32) + rs2_recv[inner, kk + 4].astype(f32)

    r1 = reduce_start(w2g, scaled, 0)
    sl = slope(conv_out[...]).astype(bf16)
    for n in range(2):
        exts[n + 1] = sl[:, 128 * n : 128 * (n + 1)]
    halo_s = halo_start(exts)
    sext = group_forward(sext, extg)
    sb_top = smg[:, :, 2 * SQP : 2 * SQP + BASIS].reshape(GP, BASIS)
    sb_low = smg[:, :, 2 * SQP + BASIS :].reshape(GP, BASIS)
    u2 = dot_tn(sb_top, scaled) + dot_tn(sb_low, scaled)
    usend[...] = u2.astype(bf16).reshape(8, 32, PX)
    us = [copy(usend.at[flip(g, k // 4)], urecv.at[n + 1], z, peer(k)) for n, k in enumerate(g_masks)]
    r1 = reduce_relay(r1, 0)
    for b in range(GRP):
        v = fb_in[CH_DEV * b : CH_DEV * (b + 1), :]
        v = jnp.concatenate([v, jnp.zeros((CB - CH_DEV, BASIS), f32)], axis=0)
        top = v.astype(bf16)
        fbp[0, CB * b : CB * (b + 1), :] = top
        fbp[1, CB * b : CB * (b + 1), :] = (v - top.astype(f32)).astype(bf16)
    xb = dot_tn(fbp[0], x_rows) + dot_tn(fbp[1], x_rows)
    xb_top = xb.astype(bf16)
    xbt[0:BASIS, :] = xb_top
    xbt[BASIS:, :] = (xb - xb_top.astype(f32)).astype(bf16)
    ex_row = sigmoid(
        split_left(dot_nt, squeeze, ex_w)
        + split_right(
            dot_nt,
            jnp.where(lax.broadcasted_iota(jnp.int32, (8, 128), 1) == 2, 1.0, 0.0).astype(bf16),
            big[...].reshape(GP, 128),
        )
    )
    halo_finish(exts, halo_s)
    c2cols = reduce_column(r1, 0)
    back_copies = [None] * 7
    for kk in range(4):
        q = flip(m, kk)
        total = xq[q].astype(f32) + reduce_quarter(c2cols, 0, kk)
        sig = sigmoid(total)
        bo[q] = (total * sig).astype(bf16)
        bq[q] = (cq[q].astype(f32) * (sig * (1.0 + total * (1.0 - sig)))).astype(bf16)
        for k in (kk, kk + 4):
            if k:
                back_copies[k - 1] = copy(bq.at[q], ball.at[me], z, peer(k))
    ball[me] = bq[m]
    bring = ring_start(back_copies, ball, block)
    brows = ring_relay(bring, ball, block)
    for c in us:
        c.wait_recv()
    u_own = usend[g].astype(f32)
    for n in range(1, 8):
        u_own = u_own + urecv[n].astype(f32)
    u_top = u_own.astype(bf16)
    u_low = (u_own - u_top.astype(f32)).astype(bf16)
    group_finish(sext)

    def build_other(k, carry):
        q = m + (k % 2) * (1 - 2 * (m % 2)) + 2 * (k // 2) * (1 - 2 * (m // 2))
        build(lambda n, r: extg[q, n, r : r + 16, :], k)
        return carry

    lax.fori_loop(1, 4, build_other, 0)
    for c in brows:
        c.wait_recv()

    back_rows = ball[...].reshape(AP, PX)
    scaled_back = dot(w2g[...], back_rows)
    ae = sums_start(scaled_back * hidden[...], es)
    scaled_back = scaled_back * ex_col
    sback[...] = scaled_back
    edge = scaled_back.astype(bf16)
    for n in range(2):
        exta[n + 1] = edge[:, 128 * n : 128 * (n + 1)]
    halo_a = halo_start(exta)
    se_ = sums_tiles(ae, es, ez)
    coords = dot_nt(u_top, back_rows) + dot_nt(u_low, back_rows)
    for k in range(4):
        c2s[k] = coords[:, 640 * k : 640 * (k + 1)].astype(bf16)
    c2g = [copy(c2s.at[flip(m, k)], c2r.at[k], z, peer(k)) for k in range(1, 4)]
    excite_back = sums_finish(se_, ez)
    sig_back = excite_back * ex_row * (1.0 - ex_row)
    be = squeeze_start(split_left(dot, sig_back, ex_w), eb8)
    halo_finish(exta, halo_a)
    squeeze_back = squeeze_finish(be, eb8) * slope(squeeze_pre)
    means_back = split_right(dot_nt, sq_w, squeeze_back)
    mb_col = jnp.where(img == 0, means_back[:, 0:1], means_back[:, 1:2]) * (1.0 / CELLS)
    hb = ((sback[...] + mb_col) * slope(conv_out[...])).astype(bf16)
    hbs[...] = hb.reshape(4, CB, PX)
    hsw = [copy(hbs.at[flip(m, k)], hbr.at[k], z, peer(k)) for k in range(1, 4)]
    before, after = [
        ((exta[n].astype(f32) + mb_col) * exts[n].astype(f32)).astype(bf16) for n in (0, 3)
    ]
    hb_wide = jnp.concatenate([before, hb, after], axis=1)

    zbuf[...] = dot_tn(wcg[...].reshape(GP, AP), hb_wide)
    lanes8 = lax.broadcasted_iota(jnp.int32, (16, PX), 1) % 64
    for i in range(CI // 16):
        r = 16 * i
        acc = jnp.zeros((16, PX), f32)
        for b in (-1, 0, 1):
            up = zbuf[CI * (b + 1) + r : CI * (b + 1) + r + 16, :]
            mid = zbuf[CI * (b + 4) + r : CI * (b + 4) + r + 16, :]
            down = zbuf[CI * (b + 7) + r : CI * (b + 7) + r + 16, :]
            y = mid[:, 128:384] + pltpu.roll(up, 64, 1)[:, 256:512] + pltpu.roll(down, 64, 1)[:, 128:384]
            if b == 1:
                y = jnp.where(lanes8 == 0, 0.0, pltpu.roll(y, 1, 1))
            elif b == -1:
                y = jnp.where(lanes8 == 63, 0.0, pltpu.roll(y, PX - 1, 1))
            acc = acc + y
        pre[r : r + 16, :] = acc * slope(pre[r : r + 16, :])
    unpack = packing((GP, CI), 1)
    ag = dot(unpack, pre[...].astype(bf16)).astype(bf16)
    r2 = reduce_start(w1g, ag, 1)

    c1 = dot_nt(ag, xbt[0:BASIS, :]) + dot_nt(ag, xbt[BASIS:, :])
    c1s[...] = c1.astype(bf16).reshape(4, CB, BASIS)
    c1g = [copy(c1s.at[flip(m, k)], c1r.at[k], z, peer(k)) for k in range(1, 4)]
    for c in c2g:
        c.wait_recv()
    c2 = c2s[m].astype(f32) + c2r[1].astype(f32) + c2r[2].astype(f32) + c2r[3].astype(f32)
    c2z[...] = c2.astype(bf16)
    c2t = [copy(c2z, c2zr.at[k], flip(z, k), me) for k in range(1, 8)]
    r2 = reduce_relay(r2, 1)
    for c in hsw:
        c.wait_recv()
    grads = dot_nt(hbs[m], cols[0])
    for k in range(1, 4):
        grads = grads + dot_nt(hbr[k], cols[k])
    for c in c1g:
        c.wait_recv()
    c1 = c1s[m].astype(f32) + c1r[1].astype(f32) + c1r[2].astype(f32) + c1r[3].astype(f32)
    both = jnp.concatenate([grads, c1, jnp.zeros((CB, TILES * ZC - AP - BASIS), f32)], axis=1)
    for k in range(TILES):
        zf[k] = both[:, ZC * k : ZC * (k + 1)]
        zs[k] = both[:, ZC * k : ZC * (k + 1)].astype(bf16)
    z1 = [copy(zs.at[flip(z, k)], zr.at[k], flip(z, k), me) for k in range(1, 8)]
    for c in c2t:
        c.wait_recv()
    c2 = c2z[...].astype(f32)
    for k in range(1, 8):
        c2 = c2 + c2zr[k].astype(f32)

    def slot2(device, k):
        d = flip(device, k)
        return (d % 4) * 8 + d // 4

    same = (0, 2, 4, 6)
    c2all[slot2(me, 0)] = c2.astype(bf16)
    c2c = gather_column(lambda k: c2all.at[slot2(me, 0)], c2all, slot2, same[1:])
    c2cols = reduce_column(r2, 1)
    c2ring = ring_start(c2c, c2all, slot2, same)
    for c in z1:
        c.wait_recv()
    chunk = zf[z]
    for k in range(1, 8):
        chunk = chunk + zr[k].astype(f32)
    zall[z] = chunk.astype(bf16)
    z2 = [copy(zall.at[z], zall.at[z], flip(z, k), me) for k in range(1, 8)]
    c2rows = ring_relay(c2ring, c2all, slot2, same)
    for kk in range(4):
        q = flip(m, kk)
        ig[q] = (bq[q].astype(f32) + reduce_quarter(c2cols, 1, kk)).astype(bf16)
    swaps = [copy(c2all.at[slot2(me, k)], c2all.at[slot2(me, k)], z, peer(1)) for k in same]
    for c in c2rows:
        c.wait_recv()
    for step in (1, 2, 3):
        there = lax.rem(me + 8 * step, GRP)
        for k in same:
            at = slot2(there, k)
            swaps.append(copy(c2all.at[at], c2all.at[at], z, peer(1)))

    first = lax.broadcasted_iota(jnp.int32, (CB, GP), 0) + CB * m
    mine = jnp.where(first == lax.broadcasted_iota(jnp.int32, (CB, GP), 1), 1.0, 0.0).astype(bf16)
    own = split_right(dot_nt, mine, means)
    grad = own[:, 0:1] * squeeze_back[0:1] + own[:, 1:2] * squeeze_back[1:2]
    sqg[...] = (grad * GRAD_SCALE)[0:CH_DEV, 0:SQ]
    own = split_right(dot_nt, mine, sig_back)
    grad = own[:, 0:1] * squeeze[0:1] + own[:, 1:2] * squeeze[1:2]
    exg[...] = (grad * GRAD_SCALE)[0:CH_DEV, 0:SQ]
    for n, (start, width, low) in enumerate(windows(NCH, CH_DEV, AP, CB)):
        hots2[n] = one_hot(512, low, 256, start, CH_DEV, CB)
    fb = fb_in[...]
    top = fb.astype(bf16)
    fbn[0] = top
    fbn[1] = (fb - top.astype(f32)).astype(bf16)
    for c in swaps:
        c.wait_recv()
    wide = jnp.concatenate([c2all[8 * k : 8 * (k + 1)].reshape(BASIS, 640) for k in range(4)], axis=1)
    own_top = smp[:, 2 * SQP : 2 * SQP + BASIS]
    own_low = smp[:, 2 * SQP + BASIS :]
    for n, (start, width, low) in enumerate(windows(NCH, CH_DEV, AP, CB)):
        v = dot(wide[:, low : low + 512], hots2[n]).astype(bf16)
        v = (dot(own_top, v) + dot(own_low, v)) * GRAD_SCALE
        sg[:, start : start + width] = v[0:CH_DEV, 0:width]
    for c in z2:
        c.wait_recv()
    lanes_left = AP - ZC * 6
    c1 = jnp.concatenate([zall[6, :, lanes_left:], zall[7, :, 0 : BASIS - (ZC - lanes_left)]], axis=1)
    v = (dot_nt(c1, fbn[0]) + dot_nt(c1, fbn[1])) * GRAD_SCALE
    fg[...] = v[0:CH_DEV]
    sums = jnp.concatenate([zall[k] for k in range(7)], axis=1).astype(f32) * GRAD_SCALE
    for t in range(9):
        cg[t] = sums[0:CH_DEV, CI * t : CI * t + 264]
    for c in started:
        c.wait_send()


def per_device(
    inputs,
    cotangent,
    first_weight,
    first_bias,
    conv_weight,
    conv_bias,
    squeeze_weight,
    squeeze_bias,
    excite_weight,
    excite_bias,
    second_weight,
    first_basis,
    second_basis,
):
    def quarters(v):
        v = v.reshape(2, 2, PX, CH_DEV).transpose(0, 1, 3, 2)
        return jnp.pad(v, ((0, 0), (0, 0), (0, CB - CH_DEV), (0, 0))).reshape(4, CB, PX)

    xq, cq = quarters(inputs), quarters(cotangent)
    biases = jnp.pad(jnp.stack([first_bias, conv_bias, excite_bias]), ((0, 5), (0, SQP - CH_DEV)))
    squeeze_rows = jnp.broadcast_to(jnp.pad(squeeze_bias, (0, SQP - SQ))[None], (8, SQP))
    side = jnp.concatenate([squeeze_rows, biases])

    V = pltpu.VMEM
    scratch = [
        V((GRP, CB, PX), bf16),
        V((GRP, CB, PX), bf16),
        V((CB, RAW), bf16),
        V((CB, RAW), bf16),
        V((CB, AP), bf16),
        V((CB, 2 * SQP + 2 * BASIS), bf16),
        V((CB, 128), f32),
        V((4, CB, RAW), bf16),
        V((4, CB, RAW), bf16),
        V((GP, AP), bf16),
        V((4, CB, AP), bf16),
        V((GP, AP), bf16),
        V((4, CB, 2 * SQP + 2 * BASIS), bf16),
        V((4, CB, 128), f32),
        V((10, 512, 256), bf16),
        V((9, 512, 256), bf16),
        V((2, AP, BASIS), bf16),
        V((2, NCH, BASIS), bf16),
        V((4, CI, 128), bf16),
        V((4, 4, CI, 128), bf16),
        V((4, GP, 128), bf16),
        V((4, GP, 128), bf16),
        V((4, AP, PX), bf16),
        V((CI, PX), f32),
        V((GP, PX), f32),
        V((GP, PX), f32),
        V((GP, PX), f32),
        V((2 * BASIS, PX), bf16),
        V((AP, 512), f32),
        V((2, 8, CB, PX), bf16),
        V((2, 2, 4, CB, PX), bf16),
        V((2, 4, CB, PX), f32),
        V((2, 2, 8, CB, PX), bf16),
        V((2, 2, 8, CB, PX), bf16),
        V((8, CB, PX), f32),
        V((2, 8, CB, PX), bf16),
        V((2, 8, CB, PX), bf16),
        V((4, CB, PX), bf16),
        V((8, 32, PX), bf16),
        V((8, 32, PX), bf16),
        V((4, 32, 640), bf16),
        V((4, 32, 640), bf16),
        V((32, 640), bf16),
        V((8, 32, 640), bf16),
        V((32, 32, 640), bf16),
        V((4, 8, 128), f32),
        V((8, 8, 128), f32),
        V((8, 2, 8, 128), f32),
        V((4, 8, 128), f32),
        V((8, 8, 128), f32),
        V((8, 2, 8, 128), f32),
        V((4, CB, PX), bf16),
        V((4, CB, PX), bf16),
        V((4, CB, BASIS), bf16),
        V((4, CB, BASIS), bf16),
        V((TILES, CB, ZC), bf16),
        V((TILES, CB, ZC), f32),
        V((TILES, CB, ZC), bf16),
        V((TILES, CB, ZC), bf16),
        pltpu.SemaphoreType.DMA((NSEM,)),
        pltpu.SemaphoreType.DMA((NSEM,)),
        pltpu.SemaphoreType.DMA((16,)),
    ]
    spec = pl.BlockSpec(memory_space=pltpu.VMEM)
    shape = jax.ShapeDtypeStruct
    bo, ig, fg, sg, cg, sqg, exg = pl.pallas_call(
        body,
        out_shape=[
            shape((4, CB, PX), bf16),
            shape((4, CB, PX), bf16),
            shape((CH_DEV, NCH), f32),
            shape((CH_DEV, NCH), f32),
            shape((9, CH_DEV, 264), f32),
            shape((CH_DEV, SQ), f32),
            shape((CH_DEV, SQ), f32),
        ],
        in_specs=[spec] * 10,
        out_specs=[spec] * 7,
        scratch_shapes=scratch,
        compiler_params=pltpu.CompilerParams(
            collective_id=0, has_side_effects=True, vmem_limit_bytes=62 * 1024 * 1024
        ),
    )(
        xq, cq, first_weight.T, conv_weight.transpose(1, 0, 2), second_weight,
        squeeze_weight, excite_weight.T, second_basis, first_basis, side,
    )

    def pixels(v):
        v = v[:, :CH_DEV].reshape(2, 2, CH_DEV, PX).transpose(0, 1, 3, 2)
        return v.reshape(inputs.shape)

    return (pixels(bo), pixels(ig), fg.T, sg, cg.transpose(1, 0, 2), sqg, exg.T)


def solution(mesh):
    placed = (
        P(None, "tile", None, "grp"),
        P(None, "tile", None, "grp"),
        P(None, "grp"),
        P("grp"),
        P("grp", None, None),
        P("grp"),
        P("grp", None),
        P(),
        P(None, "grp"),
        P("grp"),
        P("grp", None),
        P(),
        P("grp", None),
    )
    return jax.shard_map(
        per_device,
        mesh=mesh,
        in_specs=placed,
        out_specs=(
            P(None, "tile", None, "grp"),
            P(None, "tile", None, "grp"),
            P(None, "grp"),
            P("grp", None),
            P("grp", None, None),
            P("grp", None),
            P(None, "grp"),
        ),
        check_vma=False,
    )
```

```python
import math

import jax
import jax.numpy as jnp
from jax import lax
from jax.experimental import pallas as pl
from jax.experimental.pallas import tpu as pltpu
from jax.sharding import PartitionSpec as P

MESH = pl.DeviceIdType.MESH
highest = lax.Precision.HIGHEST
bf16, f32 = jnp.bfloat16, jnp.float32

TILES = 8
GRP = 32
CH_DEV = 66
CB = 80
PX = 256
GP = 4 * CB
AP = GRP * CB
CI = 272
SQ = 528
SQP = 640
BASIS = 256
ZC = 384
CELLS = 4096.0
NSEM = 250
RAW = 2176
NCH = 2112
GRAD_SCALE = 1.0 / math.sqrt(8192.0)


def flip(index, mask):
    out = index
    for bit in range(5):
        if mask >> bit & 1:
            step = 1 << bit
            out = out + step * (1 - 2 * ((index // step) % 2))
    return out


def sigmoid(v):
    return 1.0 / (1.0 + jnp.exp(-v))


def slope(v):
    sig = sigmoid(v)
    return sig * (1.0 + v * (1.0 - sig))


def dot(a, b):
    return lax.dot_general(a, b, (((1,), (0,)), ((), ())), preferred_element_type=f32)


def dot_nt(a, b):
    return lax.dot_general(a, b, (((1,), (1,)), ((), ())), preferred_element_type=f32)


def pieces(v, count):
    out = []
    for _ in range(count - 1):
        top = v.astype(bf16)
        out.append(top)
        v = v - top.astype(f32)
    out.append(v.astype(bf16))
    return out


def dot_tn(a, b):
    return lax.dot_general(a, b, (((0,), (0,)), ((), ())), preferred_element_type=f32)


def one_hot(rows, row_start, lanes, lane_start, out_width, in_width):
    r = lax.broadcasted_iota(jnp.int32, (rows, lanes), 0) + row_start
    out = lax.broadcasted_iota(jnp.int32, (rows, lanes), 1) + lane_start
    blk = (out * ((1 << 22) // out_width + 1)) >> 22
    hit = (out - out_width * blk < CH_DEV) & (r == out + (in_width - out_width) * blk) & (blk < GRP)
    return jnp.where(hit, 1.0, 0.0).astype(bf16)


def windows(out_lanes, out_width, in_lanes, in_width):
    for start in range(0, out_lanes, 256):
        width = min(256, out_lanes - start)
        low = min(start // out_width * in_width // 128 * 128, in_lanes - 512)
        yield start, width, low


def split_left(op, a, b, count=3):
    return sum(op(p, b) for p in pieces(a, count))


def split_right(op, a, b, count=3):
    return sum(op(a, p) for p in pieces(b, count))


def body(
    x_in, c_in, w1, wc, w2, sqw, exw, sb_in, fb_hbm, b1, b2, b3, b4,
    bo_out, ig_out, fg, sg, cg, sqg, exg,
    xq, cq, fb_in, bt, sqb, xall, ball, w1p, w2p, wcp, smp, bip, w1r, w2r, w1g, wcg, w2g, smg, big,
    hots, hots2, fbp, fbn,
    ext, extg, exts, exta, cols, pre, conv_out, hidden, sback, xbt, zbuf,
    bo, rs_far, rs_rel, rs_keep, rs_out, rs_in, rs_own, rs2_send, rs2_recv, bq,
    usend, urecv, c2s, c2r, c2z, c2zr, c2all,
    hs, hz, hb8, es, ez, eb8, hbs, hbr, c1s, c1r, zs, zf, zr, zall,
    send, recv, local,
):
    z = lax.axis_index("tile")
    me = lax.axis_index("grp")
    xx = me // 8
    col = me % 8
    m = me % 4
    g = me // 4
    core = me % 2
    img = (me // 2) % 2
    count = [0]
    started = []
    locals_ = []

    def copy(src, dst, tile, grp):
        i = count[0]
        count[0] += 1
        c = pltpu.make_async_remote_copy(
            src_ref=src, dst_ref=dst, send_sem=send.at[i], recv_sem=recv.at[i],
            device_id=(tile, grp), device_id_type=MESH,
        )
        c.start()
        started.append(c)
        return c

    def keep(src, dst):
        c = pltpu.make_async_copy(src, dst, local.at[len(locals_)])
        c.start()
        locals_.append(c)
        return c

    def peer(mask):
        return flip(me, mask)

    right, left = lax.rem(me + 8, GRP), lax.rem(me + 24, GRP)
    other = (lax.rem(z + 2 * core - 1 + TILES, TILES), flip(me, 1))
    grp_masks = [1, 2, 3, 4, 5, 6, 7, 8, 16, 24, 12, 20, 28]
    g_masks = [4, 8, 12, 16, 20, 24, 28]

    barrier = pltpu.get_barrier_semaphore()
    for mask in grp_masks:
        pl.semaphore_signal(barrier, inc=1, device_id=(z, peer(mask)), device_id_type=MESH)
    for mask in range(1, 8):
        pl.semaphore_signal(barrier, inc=1, device_id=(flip(z, mask), me), device_id_type=MESH)
    pl.semaphore_signal(barrier, inc=1, device_id=other, device_id_type=MESH)

    fb_copy = keep(fb_hbm, fb_in)
    diagonal = lax.broadcasted_iota(jnp.int32, (CB, CH_DEV), 0) == lax.broadcasted_iota(jnp.int32, (CB, CH_DEV), 1)
    eye = jnp.where(diagonal, 1.0, 0.0).astype(bf16)
    for q in range(4):
        xq[q] = dot_nt(eye, x_in[q]).astype(bf16)
    w1p[...] = jnp.zeros(w1p.shape, bf16)
    w1p[0:CH_DEV, 0:NCH] = w1[...]
    bt[...] = jnp.zeros(bt.shape, f32)
    for n, vector in enumerate((b1, b2, b3)):
        bt[n : n + 1, 0:CH_DEV] = vector[...]
    bip[...] = jnp.zeros(bip.shape, f32)
    bip[:, 0:8] = bt[...].T[0:CB]
    pl.semaphore_wait(barrier, len(grp_masks) + 8)

    def gather_column(pick, dst, slot, masks=range(1, 8)):
        return [copy(pick(k), dst.at[slot(me, 0)], z, peer(k)) for k in masks]

    def ring_start(arrived, dst, slot, masks=range(8)):
        to_right, to_left = [], []
        for n, k in enumerate(masks):
            if n:
                arrived[n - 1].wait_recv()
            at = slot(me, k)
            to_right.append(copy(dst.at[at], dst.at[at], z, right))
            to_left.append(copy(dst.at[at], dst.at[at], z, left))
        return to_right, to_left

    def ring_relay(state, dst, slot, masks=range(8)):
        to_right, to_left = state
        half = len(masks) // 2
        relayed = []
        for n in range(half):
            to_right[n].wait_recv()
            at = slot(left, masks[n])
            relayed.append(copy(dst.at[at], dst.at[at], z, right))
            to_left[n + half].wait_recv()
            at = slot(right, masks[n + half])
            relayed.append(copy(dst.at[at], dst.at[at], z, left))
        return to_right[half:] + to_left[:half] + relayed

    def group_start(src, dst):
        mine = keep(src, dst.at[m])
        return mine, copy(src, dst.at[m], z, peer(1)), copy(src, dst.at[m], z, peer(2))

    def group_forward(state, dst):
        mine, near, far = state
        far.wait_recv()
        slot = flip(m, 2)
        return mine, near, copy(dst.at[slot], dst.at[slot], z, peer(1))

    def group_finish(state):
        state[0].wait()
        state[1].wait_recv()
        state[2].wait_recv()

    def halo_start(buf):
        return (
            copy(buf.at[2 - core], buf.at[3 * core], z, peer(1)),
            copy(buf.at[1 + core], buf.at[3 - 3 * core], other[0], other[1]),
        )

    def halo_finish(buf, copies):
        for c in copies:
            c.wait_recv()

        @pl.when((z == 0) & (core == 0))
        def _():
            buf[0] = jnp.zeros(buf.shape[1:], buf.dtype)

        @pl.when((z == TILES - 1) & (core == 1))
        def _():
            buf[3] = jnp.zeros(buf.shape[1:], buf.dtype)

    def block(device, k):
        return flip(device, k)

    def bias(n):
        return big[...].reshape(GP, 128)[:, n : n + 1]

    def spread(source, target):
        for n, (start, width, low) in enumerate(windows(AP, CB, RAW, CH_DEV)):
            v = dot(source[:, :, low : low + 512].reshape(GP, 512), hots[n])
            target[:, start : start + 256] = v.astype(bf16)

    xs = gather_column(lambda k: xq.at[flip(m, k & 3)], xall, block)
    s1 = group_start(w1p, w1r)
    sbi = group_start(bip, big)
    keep(xq.at[m], xall.at[me]).wait()
    xring = ring_start(xs, xall, block)
    sqb[...] = jnp.zeros(sqb.shape, f32)
    sqb[0:1, 0:SQ] = b4[...]
    wcp[...] = jnp.zeros(wcp.shape, bf16)
    for t in range(9):
        wcp[0:CH_DEV, CI * t : CI * t + 264] = wc[t]
    xrows = ring_relay(xring, xall, block)
    sc = group_start(wcp, wcg)
    for n, (start, width, low) in enumerate(windows(AP, CB, RAW, CH_DEV)):
        hots[n] = one_hot(512, low, 256, start, CB, CH_DEV)
    s1 = group_forward(s1, w1r)
    sbi = group_forward(sbi, big)
    smp[...] = jnp.zeros(smp.shape, bf16)
    smp[0:CH_DEV, 0:SQ] = sqw[...]
    smp[0:CH_DEV, SQP : SQP + SQ] = exw[...]
    sb = sb_in[...]
    sb_top = sb.astype(bf16)
    smp[0:CH_DEV, 2 * SQP : 2 * SQP + BASIS] = sb_top
    smp[0:CH_DEV, 2 * SQP + BASIS :] = (sb - sb_top.astype(f32)).astype(bf16)
    w2p[...] = jnp.zeros(w2p.shape, bf16)
    w2p[0:CH_DEV, 0:NCH] = w2[...]
    for q in range(4):
        cq[q] = dot_nt(eye, c_in[q]).astype(bf16)

    def packing(shape, packed_dim):
        row = lax.broadcasted_iota(jnp.int32, shape, packed_dim)
        lane = lax.broadcasted_iota(jnp.int32, shape, 1 - packed_dim)
        shifted = row
        for part in (1, 2, 3):
            shifted = shifted + jnp.where(row >= CH_DEV * part, CB - CH_DEV, 0)
        return jnp.where((shifted == lane) & (row < 4 * CH_DEV), 1.0, 0.0).astype(bf16)

    group_finish(s1)
    spread(w1r, w1g)
    group_finish(sbi)
    for c in xrows:
        c.wait_recv()

    x_rows = xall[...].reshape(AP, PX)
    first_pre = dot(w1g[...], x_rows) + bias(0)
    active = (first_pre * sigmoid(first_pre)).astype(bf16)
    pack = packing((CI, GP), 0)
    packed = dot(pack, active).astype(bf16)
    ext[1] = packed[:, 0:128]
    ext[2] = packed[:, 128:256]
    halo = halo_start(ext)
    ssm = group_start(smp, smg)
    s2 = group_start(w2p, w2r)
    pre[...] = split_right(dot, pack, first_pre)
    sc = group_forward(sc, wcg)
    for k in range(4):
        cols[k, 9 * CI :, :] = jnp.zeros((AP - 9 * CI, PX), bf16)

    def build(read, n_target):
        lanes = lax.broadcasted_iota(jnp.int32, (16, 512), 1) % 64
        for i in range(CI // 16):
            r = 16 * i
            e = jnp.concatenate([read(n, r) for n in range(4)], axis=1).astype(f32)
            for b in (-1, 0, 1):
                if b == 0:
                    v = e
                elif b == 1:
                    v = jnp.where(lanes == 63, 0.0, pltpu.roll(e, 511, 1))
                else:
                    v = jnp.where(lanes == 0, 0.0, pltpu.roll(e, 1, 1))
                s = pltpu.roll(v, 64, 1)
                for a, win in ((-1, s[:, 128:384]), (0, v[:, 128:384]), (1, s[:, 256:512])):
                    t = 3 * (a + 1) + b + 1
                    cols[n_target, t * CI + r : t * CI + r + 16, :] = win.astype(bf16)

    halo_finish(ext, halo)
    build(lambda n, r: ext[n, r : r + 16, :], 0)
    group_finish(sc)

    co = dot(wcg[...].reshape(GP, AP), cols[0]) + bias(1)
    conv_out[...] = co
    hid = co * sigmoid(co)
    hidden[...] = hid
    ones = jnp.ones((8, PX), bf16)
    rows8 = lax.broadcasted_iota(jnp.int32, (8, 128), 0)

    def sums_start(v, buf):
        tile = jnp.zeros((8, 128), f32)
        for j in range(3):
            part = v[128 * j : min(128 * (j + 1), GP)]
            if j == 2:
                part = jnp.concatenate([part, jnp.zeros((64, PX), f32)], axis=0)
            tile = jnp.where(rows8 == 3 * img + j, split_right(dot_nt, ones, part), tile)
        buf[0] = tile
        return [copy(buf.at[0], buf.at[k], z, peer(k)) for k in range(1, 4)]

    def sums_tiles(copies, buf, wider):
        for c in copies:
            c.wait_recv()
        wider[0] = buf[0] + buf[1] + buf[2] + buf[3]
        return [copy(wider.at[0], wider.at[k], flip(z, k), me) for k in (4, 3, 5, 2, 6, 1, 7)]

    def sums_finish(copies, wider):
        for c in copies:
            c.wait_recv()
        tile = sum(wider[k] for k in range(8))
        parts = [
            jnp.where(rows8 == 0, tile[j : j + 1], jnp.where(rows8 == 1, tile[3 + j : 4 + j], 0.0))
            for j in range(3)
        ]
        return jnp.concatenate(parts, axis=1)[:, 0:GP]

    def squeeze_start(v, buf):
        low, high = jnp.zeros((8, 128), f32), jnp.zeros((8, 128), f32)
        for j in range(5):
            part = v[:, 128 * j : 128 * (j + 1)]
            low = jnp.where(rows8 == j, part[0:1], low)
            high = jnp.where(rows8 == j, part[1:2], high)
        buf[0, 0] = low
        buf[0, 1] = high
        return [copy(buf.at[0], buf.at[n + 1], z, peer(k)) for n, k in enumerate(g_masks)]

    def squeeze_finish(copies, buf):
        for c in copies:
            c.wait_recv()
        low = sum(buf[n, 0] for n in range(8))
        high = sum(buf[n, 1] for n in range(8))
        parts = [
            jnp.where(rows8 == 0, low[j : j + 1], jnp.where(rows8 == 1, high[j : j + 1], 0.0))
            for j in range(5)
        ]
        return jnp.concatenate(parts, axis=1)

    ah = sums_start(hid, hs)
    ssm = group_forward(ssm, smg)
    sext = group_start(ext, extg)
    sh = sums_tiles(ah, hs, hz)
    s2 = group_forward(s2, w2r)
    group_finish(ssm)
    fb_copy.wait()
    for b in range(GRP):
        v = fb_in[CH_DEV * b : CH_DEV * (b + 1), :]
        v = jnp.concatenate([v, jnp.zeros((CB - CH_DEV, BASIS), f32)], axis=0)
        top = v.astype(bf16)
        fbp[0, CB * b : CB * (b + 1), :] = top
        fbp[1, CB * b : CB * (b + 1), :] = (v - top.astype(f32)).astype(bf16)
    means = sums_finish(sh, hz) * (1.0 / CELLS)
    sq_w = smg[:, :, 0:SQP].reshape(GP, SQP)
    ex_w = smg[:, :, SQP : 2 * SQP].reshape(GP, SQP)
    bh = squeeze_start(split_left(dot, means, sq_w), hb8)
    group_finish(s2)
    spread(w2r, w2g)
    xb = dot_tn(fbp[0], x_rows) + dot_tn(fbp[1], x_rows)
    xb_top = xb.astype(bf16)
    xbt[0:BASIS, :] = xb_top
    xbt[BASIS:, :] = (xb - xb_top.astype(f32)).astype(bf16)
    squeeze_pre = squeeze_finish(bh, hb8) + sqb[0:1]
    squeeze = squeeze_pre * sigmoid(squeeze_pre)
    excite = sigmoid(split_right(dot_nt, ex_w, squeeze) + bias(2))
    ex_col = jnp.where(img == 0, excite[:, 0:1], excite[:, 1:2])
    scaled = (hidden[...] * ex_col).astype(bf16)

    unit_a, unit_b, unit_c, unit_d = 2, 3, 1, 0

    def unit(r):
        return pl.ds(2 * flip(col // 2, r), 2)

    def reduce_send(inner, side, r, device):
        at = unit(r)
        return copy(rs_out.at[inner, side, at], rs_in.at[inner, side, at], z, device)

    def reduce_near(inner, side, r, device):
        at = unit(r)
        rs_out[inner, side, at] = rs_keep[side, at].astype(bf16)
        return reduce_send(inner, side, r, device)

    def reduce_pass(inner, side, r, device, arrived):
        at = unit(r)
        arrived.wait_recv()
        rs_out[inner, side, at] = (rs_keep[side, at] + rs_rel[inner, at].astype(f32)).astype(bf16)
        return reduce_send(inner, side, r, device)

    def reduce_start(weights, rhs, inner):
        def part(step):
            at = pl.multiple_of(lax.rem(xx + step, 4) * (8 * CB), 128)
            return dot_tn(weights[:, pl.ds(at, 8 * CB)], rhs).reshape(8, CB, PX)

        rs_far[inner] = part(2).astype(bf16)
        far = {}
        for r, device in ((unit_a, right), (unit_c, left), (unit_b, right), (unit_d, left)):
            far[r] = copy(rs_far.at[inner, unit(r)], rs_rel.at[inner, unit(r)], z, device)
        rs_keep[0] = part(1)
        near = {(0, unit_c): reduce_near(inner, 0, unit_c, right)}
        rs_keep[1] = part(3)
        near[1, unit_a] = reduce_near(inner, 1, unit_a, left)
        rs_own[...] = part(0)
        return far, near

    def reduce_relay(state, inner):
        far, near = state
        near[0, unit_a] = reduce_pass(inner, 0, unit_a, right, far[unit_a])
        near[1, unit_c] = reduce_pass(inner, 1, unit_c, left, far[unit_c])
        near[0, unit_d] = reduce_near(inner, 0, unit_d, right)
        near[1, unit_b] = reduce_near(inner, 1, unit_b, left)
        near[0, unit_b] = reduce_pass(inner, 0, unit_b, right, far[unit_b])
        near[1, unit_d] = reduce_pass(inner, 1, unit_d, left, far[unit_d])
        return near

    def reduce_column(near, inner):
        out = [None] * 7
        for r in (unit_a, unit_c, unit_b, unit_d):
            at = unit(r)
            near[0, r].wait_recv()
            near[1, r].wait_recv()
            total = rs_own[at] + rs_in[inner, 0, at].astype(f32) + rs_in[inner, 1, at].astype(f32)
            rs2_send[inner, at] = total.astype(bf16)
            for k in (2 * r, 2 * r + 1):
                if k:
                    out[k - 1] = copy(rs2_send.at[inner, flip(col, k)], rs2_recv.at[inner, k], z, peer(k))
        return out

    def reduce_quarter(copies, inner, kk):
        copies[kk + 3].wait_recv()
        if kk:
            copies[kk - 1].wait_recv()
            first = rs2_recv[inner, kk]
        else:
            first = rs2_send[inner, col]
        return first.astype(f32) + rs2_recv[inner, kk + 4].astype(f32)

    r1 = reduce_start(w2g, scaled, 0)
    sl = slope(conv_out[...]).astype(bf16)
    for n in range(2):
        exts[n + 1] = sl[:, 128 * n : 128 * (n + 1)]
    halo_s = halo_start(exts)
    sext = group_forward(sext, extg)
    sb_top = smg[:, :, 2 * SQP : 2 * SQP + BASIS].reshape(GP, BASIS)
    sb_low = smg[:, :, 2 * SQP + BASIS :].reshape(GP, BASIS)
    u2 = dot_tn(sb_top, scaled) + dot_tn(sb_low, scaled)
    usend[...] = u2.astype(bf16).reshape(8, 32, PX)
    us = [copy(usend.at[flip(g, k // 4)], urecv.at[n + 1], z, peer(k)) for n, k in enumerate(g_masks)]
    r1 = reduce_relay(r1, 0)
    ex_row = sigmoid(
        split_left(dot_nt, squeeze, ex_w)
        + split_right(
            dot_nt,
            jnp.where(lax.broadcasted_iota(jnp.int32, (8, 128), 1) == 2, 1.0, 0.0).astype(bf16),
            big[...].reshape(GP, 128),
        )
    )
    halo_finish(exts, halo_s)
    c2cols = reduce_column(r1, 0)
    back_copies = [None] * 7
    for kk in range(4):
        q = flip(m, kk)
        total = xq[q].astype(f32) + reduce_quarter(c2cols, 0, kk)
        sig = sigmoid(total)
        bo[q] = (total * sig).astype(bf16)
        bq[q] = (cq[q].astype(f32) * (sig * (1.0 + total * (1.0 - sig)))).astype(bf16)
        for k in (kk, kk + 4):
            if k:
                back_copies[k - 1] = copy(bq.at[q], ball.at[me], z, peer(k))
    ball[me] = bq[m]
    bring = ring_start(back_copies, ball, block)
    brows = ring_relay(bring, ball, block)
    for q in range(4):
        bo_out[q] = dot_tn(bo[q], eye).astype(bf16)
    for c in us:
        c.wait_recv()
    u_own = usend[g].astype(f32)
    for n in range(1, 8):
        u_own = u_own + urecv[n].astype(f32)
    u_top = u_own.astype(bf16)
    u_low = (u_own - u_top.astype(f32)).astype(bf16)
    group_finish(sext)

    def build_other(k, carry):
        q = m + (k % 2) * (1 - 2 * (m % 2)) + 2 * (k // 2) * (1 - 2 * (m // 2))
        build(lambda n, r: extg[q, n, r : r + 16, :], k)
        return carry

    lax.fori_loop(1, 4, build_other, 0)
    for c in brows:
        c.wait_recv()

    back_rows = ball[...].reshape(AP, PX)
    scaled_back = dot(w2g[...], back_rows)
    ae = sums_start(scaled_back * hidden[...], es)
    scaled_back = scaled_back * ex_col
    sback[...] = scaled_back
    edge = scaled_back.astype(bf16)
    for n in range(2):
        exta[n + 1] = edge[:, 128 * n : 128 * (n + 1)]
    halo_a = halo_start(exta)
    se_ = sums_tiles(ae, es, ez)
    coords = dot_nt(u_top, back_rows) + dot_nt(u_low, back_rows)
    for k in range(4):
        c2s[k] = coords[:, 640 * k : 640 * (k + 1)].astype(bf16)
    c2g = [copy(c2s.at[flip(m, k)], c2r.at[k], z, peer(k)) for k in range(1, 4)]
    excite_back = sums_finish(se_, ez)
    sig_back = excite_back * ex_row * (1.0 - ex_row)
    be = squeeze_start(split_left(dot, sig_back, ex_w), eb8)
    for c in c2g:
        c.wait_recv()
    c2 = c2s[m].astype(f32) + c2r[1].astype(f32) + c2r[2].astype(f32) + c2r[3].astype(f32)
    c2z[...] = c2.astype(bf16)
    c2t = [copy(c2z, c2zr.at[k], flip(z, k), me) for k in range(1, 8)]
    halo_finish(exta, halo_a)
    squeeze_back = squeeze_finish(be, eb8) * slope(squeeze_pre)
    means_back = split_right(dot_nt, sq_w, squeeze_back)
    mb_col = jnp.where(img == 0, means_back[:, 0:1], means_back[:, 1:2]) * (1.0 / CELLS)
    hb = ((sback[...] + mb_col) * slope(conv_out[...])).astype(bf16)
    hbs[...] = hb.reshape(4, CB, PX)
    hsw = [copy(hbs.at[flip(m, k)], hbr.at[k], z, peer(k)) for k in range(1, 4)]
    before, after = [
        ((exta[n].astype(f32) + mb_col) * exts[n].astype(f32)).astype(bf16) for n in (0, 3)
    ]
    hb_wide = jnp.concatenate([before, hb, after], axis=1)

    zbuf[...] = dot_tn(wcg[...].reshape(GP, AP), hb_wide)
    lanes8 = lax.broadcasted_iota(jnp.int32, (16, PX), 1) % 64
    for i in range(CI // 16):
        r = 16 * i
        acc = jnp.zeros((16, PX), f32)
        for b in (-1, 0, 1):
            up = zbuf[CI * (b + 1) + r : CI * (b + 1) + r + 16, :]
            mid = zbuf[CI * (b + 4) + r : CI * (b + 4) + r + 16, :]
            down = zbuf[CI * (b + 7) + r : CI * (b + 7) + r + 16, :]
            y = mid[:, 128:384] + pltpu.roll(up, 64, 1)[:, 256:512] + pltpu.roll(down, 64, 1)[:, 128:384]
            if b == 1:
                y = jnp.where(lanes8 == 0, 0.0, pltpu.roll(y, 1, 1))
            elif b == -1:
                y = jnp.where(lanes8 == 63, 0.0, pltpu.roll(y, PX - 1, 1))
            acc = acc + y
        pre[r : r + 16, :] = acc * slope(pre[r : r + 16, :])
    unpack = packing((GP, CI), 1)
    ag = dot(unpack, pre[...].astype(bf16)).astype(bf16)
    c1 = dot_nt(ag, xbt[0:BASIS, :]) + dot_nt(ag, xbt[BASIS:, :])
    c1s[...] = c1.astype(bf16).reshape(4, CB, BASIS)
    c1g = [copy(c1s.at[flip(m, k)], c1r.at[k], z, peer(k)) for k in range(1, 4)]
    r2 = reduce_start(w1g, ag, 1)

    for c in hsw:
        c.wait_recv()
    grads = dot_nt(hbs[m], cols[0])
    for k in range(1, 4):
        grads = grads + dot_nt(hbr[k], cols[k])
    for c in c1g:
        c.wait_recv()
    c1 = c1s[m].astype(f32) + c1r[1].astype(f32) + c1r[2].astype(f32) + c1r[3].astype(f32)
    both = jnp.concatenate([grads, c1, jnp.zeros((CB, TILES * ZC - AP - BASIS), f32)], axis=1)
    for k in range(TILES):
        zf[k] = both[:, ZC * k : ZC * (k + 1)]
        zs[k] = both[:, ZC * k : ZC * (k + 1)].astype(bf16)
    z1 = [copy(zs.at[flip(z, k)], zr.at[k], flip(z, k), me) for k in range(1, 8)]
    r2 = reduce_relay(r2, 1)
    for c in c2t:
        c.wait_recv()
    c2 = c2z[...].astype(f32)
    for k in range(1, 8):
        c2 = c2 + c2zr[k].astype(f32)

    def slot2(device, k):
        d = flip(device, k)
        return (d % 4) * 8 + d // 4

    same = (0, 2, 4, 6)
    c2all[slot2(me, 0)] = c2.astype(bf16)
    c2c = gather_column(lambda k: c2all.at[slot2(me, 0)], c2all, slot2, same[1:])
    c2cols = reduce_column(r2, 1)
    c2ring = ring_start(c2c, c2all, slot2, same)
    for c in z1:
        c.wait_recv()
    chunk = zf[z]
    for k in range(1, 8):
        chunk = chunk + zr[k].astype(f32)
    zall[z] = chunk.astype(bf16)
    z2 = [copy(zall.at[z], zall.at[z], flip(z, k), me) for k in range(1, 8)]
    c2rows = ring_relay(c2ring, c2all, slot2, same)
    for kk in range(4):
        q = flip(m, kk)
        ig_out[q] = dot_tn((bq[q].astype(f32) + reduce_quarter(c2cols, 1, kk)).astype(bf16), eye).astype(bf16)
    swaps = [copy(c2all.at[slot2(me, k)], c2all.at[slot2(me, k)], z, peer(1)) for k in same]
    for c in c2rows:
        c.wait_recv()
    for step in (1, 2, 3):
        there = lax.rem(me + 8 * step, GRP)
        for k in same:
            at = slot2(there, k)
            swaps.append(copy(c2all.at[at], c2all.at[at], z, peer(1)))

    first = lax.broadcasted_iota(jnp.int32, (CB, GP), 0) + CB * m
    mine = jnp.where(first == lax.broadcasted_iota(jnp.int32, (CB, GP), 1), 1.0, 0.0).astype(bf16)
    own = split_right(dot_nt, mine, means)
    grad = own[:, 0:1] * squeeze_back[0:1] + own[:, 1:2] * squeeze_back[1:2]
    sqg[...] = (grad * GRAD_SCALE)[0:CH_DEV, 0:SQ]
    own = split_right(dot_nt, mine, sig_back)
    grad = own[:, 0:1] * squeeze[0:1] + own[:, 1:2] * squeeze[1:2]
    exg[...] = (grad * GRAD_SCALE)[0:CH_DEV, 0:SQ]
    for n, (start, width, low) in enumerate(windows(NCH, CH_DEV, AP, CB)):
        hots2[n] = one_hot(512, low, 256, start, CH_DEV, CB)
    fb = fb_in[...]
    top = fb.astype(bf16)
    fbn[0] = top
    fbn[1] = (fb - top.astype(f32)).astype(bf16)
    for c in swaps:
        c.wait_recv()
    wide = jnp.concatenate([c2all[8 * k : 8 * (k + 1)].reshape(BASIS, 640) for k in range(4)], axis=1)
    own_top = smp[:, 2 * SQP : 2 * SQP + BASIS]
    own_low = smp[:, 2 * SQP + BASIS :]
    for n, (start, width, low) in enumerate(windows(NCH, CH_DEV, AP, CB)):
        v = dot(wide[:, low : low + 512], hots2[n]).astype(bf16)
        v = (dot(own_top, v) + dot(own_low, v)) * GRAD_SCALE
        sg[:, start : start + width] = v[0:CH_DEV, 0:width]
    for c in z2:
        c.wait_recv()
    lanes_left = AP - ZC * 6
    c1 = jnp.concatenate([zall[6, :, lanes_left:], zall[7, :, 0 : BASIS - (ZC - lanes_left)]], axis=1)
    v = (dot_nt(c1, fbn[0]) + dot_nt(c1, fbn[1])) * GRAD_SCALE
    fg[...] = v[0:CH_DEV]
    sums = jnp.concatenate([zall[k] for k in range(7)], axis=1).astype(f32) * GRAD_SCALE
    for t in range(9):
        cg[t] = sums[0:CH_DEV, CI * t : CI * t + 264]
    for c in started:
        c.wait_send()


def per_device(
    inputs,
    cotangent,
    first_weight,
    first_bias,
    conv_weight,
    conv_bias,
    squeeze_weight,
    squeeze_bias,
    excite_weight,
    excite_bias,
    second_weight,
    first_basis,
    second_basis,
):
    V = pltpu.VMEM
    scratch = [
        V((4, CB, PX), bf16),
        V((4, CB, PX), bf16),
        V((NCH, BASIS), f32),
        V((8, 128), f32),
        V((8, SQP), f32),
        V((GRP, CB, PX), bf16),
        V((GRP, CB, PX), bf16),
        V((CB, RAW), bf16),
        V((CB, RAW), bf16),
        V((CB, AP), bf16),
        V((CB, 2 * SQP + 2 * BASIS), bf16),
        V((CB, 128), f32),
        V((4, CB, RAW), bf16),
        V((4, CB, RAW), bf16),
        V((GP, AP), bf16),
        V((4, CB, AP), bf16),
        V((GP, AP), bf16),
        V((4, CB, 2 * SQP + 2 * BASIS), bf16),
        V((4, CB, 128), f32),
        V((10, 512, 256), bf16),
        V((9, 512, 256), bf16),
        V((2, AP, BASIS), bf16),
        V((2, NCH, BASIS), bf16),
        V((4, CI, 128), bf16),
        V((4, 4, CI, 128), bf16),
        V((4, GP, 128), bf16),
        V((4, GP, 128), bf16),
        V((4, AP, PX), bf16),
        V((CI, PX), f32),
        V((GP, PX), f32),
        V((GP, PX), f32),
        V((GP, PX), f32),
        V((2 * BASIS, PX), bf16),
        V((AP, 512), f32),
        V((4, CB, PX), bf16),
        V((2, 8, CB, PX), bf16),
        V((2, 8, CB, PX), bf16),
        V((2, 8, CB, PX), f32),
        V((2, 2, 8, CB, PX), bf16),
        V((2, 2, 8, CB, PX), bf16),
        V((8, CB, PX), f32),
        V((2, 8, CB, PX), bf16),
        V((2, 8, CB, PX), bf16),
        V((4, CB, PX), bf16),
        V((8, 32, PX), bf16),
        V((8, 32, PX), bf16),
        V((4, 32, 640), bf16),
        V((4, 32, 640), bf16),
        V((32, 640), bf16),
        V((8, 32, 640), bf16),
        V((32, 32, 640), bf16),
        V((4, 8, 128), f32),
        V((8, 8, 128), f32),
        V((8, 2, 8, 128), f32),
        V((4, 8, 128), f32),
        V((8, 8, 128), f32),
        V((8, 2, 8, 128), f32),
        V((4, CB, PX), bf16),
        V((4, CB, PX), bf16),
        V((4, CB, BASIS), bf16),
        V((4, CB, BASIS), bf16),
        V((TILES, CB, ZC), bf16),
        V((TILES, CB, ZC), f32),
        V((TILES, CB, ZC), bf16),
        V((TILES, CB, ZC), bf16),
        pltpu.SemaphoreType.DMA((NSEM,)),
        pltpu.SemaphoreType.DMA((NSEM,)),
        pltpu.SemaphoreType.DMA((16,)),
    ]
    spec = pl.BlockSpec(memory_space=pltpu.VMEM)
    shape = jax.ShapeDtypeStruct
    bo, ig, fg, sg, cg, sqg, exg = pl.pallas_call(
        body,
        out_shape=[
            shape((4, PX, CH_DEV), bf16),
            shape((4, PX, CH_DEV), bf16),
            shape((CH_DEV, NCH), f32),
            shape((CH_DEV, NCH), f32),
            shape((9, CH_DEV, 264), f32),
            shape((CH_DEV, SQ), f32),
            shape((CH_DEV, SQ), f32),
        ],
        in_specs=[spec] * 8 + [pl.BlockSpec(memory_space=pl.ANY)] + [spec] * 4,
        out_specs=[spec] * 7,
        scratch_shapes=scratch,
        compiler_params=pltpu.CompilerParams(
            collective_id=0, has_side_effects=True, vmem_limit_bytes=62 * 1024 * 1024
        ),
    )(
        inputs.reshape(4, PX, CH_DEV), cotangent.reshape(4, PX, CH_DEV),
        first_weight.T, conv_weight.transpose(1, 0, 2), second_weight,
        squeeze_weight, excite_weight.T, second_basis, first_basis,
        first_bias[None], conv_bias[None], excite_bias[None], squeeze_bias[None],
    )

    return (bo.reshape(inputs.shape), ig.reshape(inputs.shape), fg.T, sg, cg.transpose(1, 0, 2), sqg, exg.T)


def solution(mesh):
    placed = (
        P(None, "tile", None, "grp"),
        P(None, "tile", None, "grp"),
        P(None, "grp"),
        P("grp"),
        P("grp", None, None),
        P("grp"),
        P("grp", None),
        P(),
        P(None, "grp"),
        P("grp"),
        P("grp", None),
        P(),
        P("grp", None),
    )
    return jax.shard_map(
        per_device,
        mesh=mesh,
        in_specs=placed,
        out_specs=(
            P(None, "tile", None, "grp"),
            P(None, "tile", None, "grp"),
            P(None, "grp"),
            P("grp", None),
            P("grp", None, None),
            P("grp", None),
            P(None, "grp"),
        ),
        check_vma=False,
    )
```

```python
import math

import jax
import jax.numpy as jnp
from jax import lax
from jax.experimental import pallas as pl
from jax.experimental.pallas import tpu as pltpu
from jax.sharding import PartitionSpec as P

MESH = pl.DeviceIdType.MESH
highest = lax.Precision.HIGHEST
bf16, f32 = jnp.bfloat16, jnp.float32

TILES = 8
GRP = 32
CH_DEV = 66
CB = 80
PX = 256
GP = 4 * CB
AP = GRP * CB
CI = 272
SQ = 528
SQP = 640
BASIS = 256
ZC = 384
CELLS = 4096.0
NSEM = 250
RAW = 2176
NCH = 2112
GRAD_SCALE = 1.0 / math.sqrt(8192.0)


def flip(index, mask):
    out = index
    for bit in range(5):
        if mask >> bit & 1:
            step = 1 << bit
            out = out + step * (1 - 2 * ((index // step) % 2))
    return out


def sigmoid(v):
    return 1.0 / (1.0 + jnp.exp(-v))


def slope(v):
    sig = sigmoid(v)
    return sig * (1.0 + v * (1.0 - sig))


def dot(a, b):
    return lax.dot_general(a, b, (((1,), (0,)), ((), ())), preferred_element_type=f32)


def dot_nt(a, b):
    return lax.dot_general(a, b, (((1,), (1,)), ((), ())), preferred_element_type=f32)


def pieces(v, count):
    out = []
    for _ in range(count - 1):
        top = v.astype(bf16)
        out.append(top)
        v = v - top.astype(f32)
    out.append(v.astype(bf16))
    return out


def dot_tn(a, b):
    return lax.dot_general(a, b, (((0,), (0,)), ((), ())), preferred_element_type=f32)


def one_hot(rows, row_start, lanes, lane_start, out_width, in_width):
    r = lax.broadcasted_iota(jnp.int32, (rows, lanes), 0) + row_start
    out = lax.broadcasted_iota(jnp.int32, (rows, lanes), 1) + lane_start
    blk = (out * ((1 << 22) // out_width + 1)) >> 22
    hit = (out - out_width * blk < CH_DEV) & (r == out + (in_width - out_width) * blk) & (blk < GRP)
    return jnp.where(hit, 1.0, 0.0).astype(bf16)


def windows(out_lanes, out_width, in_lanes, in_width):
    for start in range(0, out_lanes, 256):
        width = min(256, out_lanes - start)
        low = min(start // out_width * in_width // 128 * 128, in_lanes - 512)
        yield start, width, low


def split_left(op, a, b, count=3):
    return sum(op(p, b) for p in pieces(a, count))


def split_right(op, a, b, count=3):
    return sum(op(a, p) for p in pieces(b, count))


def body(
    x_in, c_in, w1, wc, w2, sqw, exw, sb_in, fb_hbm, b1, b2, b3, b4,
    bo_out, ig_out, fg, sg, cg, sqg, exg,
    xq, cq, fb_in, bt, sqb, xall, ball, w1p, w2p, wcp, smp, sbp, bip, w1r, w2r, w1g, wcg, w2g, smg, sbg, big,
    hots, hots2, fbp, fbn,
    ext, extg, exts, exta, cols, pre, conv_out, hidden, sback, xbt, zbuf,
    bo, rs_far, rs_rel, rs_keep, rs_out, rs_in, rs_own, rs2_send, rs2_recv, bq,
    usend, urecv, c2s, c2r, c2z, c2zr, c2all,
    sls, slr, gs, ga, mb_all, hs, hz, hb8, es, ez, eb8, hbs, hbr, c1s, c1r, zs, zf, zr, zall,
    send, recv, local,
):
    z = lax.axis_index("tile")
    me = lax.axis_index("grp")
    xx = me // 8
    col = me % 8
    m = me % 4
    g = me // 4
    core = me % 2
    img = (me // 2) % 2
    count = [0]
    started = []
    locals_ = []

    def later(src, dst, tile, grp):
        i = count[0]
        count[0] += 1
        c = pltpu.make_async_remote_copy(
            src_ref=src, dst_ref=dst, send_sem=send.at[i], recv_sem=recv.at[i],
            device_id=(tile, grp), device_id_type=MESH,
        )
        started.append(c)
        return c

    def copy(src, dst, tile, grp):
        c = later(src, dst, tile, grp)
        c.start()
        return c

    def keep(src, dst):
        c = pltpu.make_async_copy(src, dst, local.at[len(locals_)])
        c.start()
        locals_.append(c)
        return c

    def peer(mask):
        return flip(me, mask)

    right, left = lax.rem(me + 8, GRP), lax.rem(me + 24, GRP)
    other = (lax.rem(z + 2 * core - 1 + TILES, TILES), flip(me, 1))
    grp_masks = [1, 2, 3, 4, 5, 6, 7, 8, 16, 24, 12, 20, 28]
    g_masks = [4, 8, 12, 16, 20, 24, 28]

    barrier = pltpu.get_barrier_semaphore()
    for mask in grp_masks:
        pl.semaphore_signal(barrier, inc=1, device_id=(z, peer(mask)), device_id_type=MESH)
    for mask in range(1, 8):
        pl.semaphore_signal(barrier, inc=1, device_id=(flip(z, mask), me), device_id_type=MESH)
    pl.semaphore_signal(barrier, inc=1, device_id=other, device_id_type=MESH)

    fb_copy = keep(fb_hbm, fb_in)
    diagonal = lax.broadcasted_iota(jnp.int32, (CB, CH_DEV), 0) == lax.broadcasted_iota(jnp.int32, (CB, CH_DEV), 1)
    eye = jnp.where(diagonal, 1.0, 0.0).astype(bf16)
    for q in range(4):
        xq[q] = dot_nt(eye, x_in[q]).astype(bf16)
    w1p[...] = jnp.zeros(w1p.shape, bf16)
    w1p[0:CH_DEV, 0:NCH] = w1[...]
    bt[...] = jnp.zeros(bt.shape, f32)
    for n, vector in enumerate((b1, b2, b3)):
        bt[n : n + 1, 0:CH_DEV] = vector[...]
    bip[...] = jnp.zeros(bip.shape, f32)
    bip[:, 0:8] = bt[...].T[0:CB]
    pl.semaphore_wait(barrier, len(grp_masks) + 8)

    def gather_column(pick, dst, slot, masks=range(1, 8)):
        return [copy(pick(k), dst.at[slot(me, 0)], z, peer(k)) for k in masks]

    def ring_start(arrived, dst, slot, masks=range(8)):
        to_right, to_left = [], []
        for n, k in enumerate(masks):
            if n:
                arrived[n - 1].wait_recv()
            at = slot(me, k)
            to_right.append(copy(dst.at[at], dst.at[at], z, right))
            to_left.append(copy(dst.at[at], dst.at[at], z, left))
        return to_right, to_left

    def ring_relay(state, dst, slot, masks=range(8)):
        to_right, to_left = state
        half = len(masks) // 2
        relayed = []
        for n in range(half):
            to_right[n].wait_recv()
            at = slot(left, masks[n])
            relayed.append(copy(dst.at[at], dst.at[at], z, right))
            to_left[n + half].wait_recv()
            at = slot(right, masks[n + half])
            relayed.append(copy(dst.at[at], dst.at[at], z, left))
        return to_right[half:] + to_left[:half] + relayed

    def group_start(src, dst):
        mine = keep(src, dst.at[m])
        return mine, copy(src, dst.at[m], z, peer(1)), copy(src, dst.at[m], z, peer(2))

    def group_forward(state, dst):
        mine, near, far = state
        far.wait_recv()
        slot = flip(m, 2)
        return mine, near, copy(dst.at[slot], dst.at[slot], z, peer(1))

    def group_finish(state):
        state[0].wait()
        state[1].wait_recv()
        state[2].wait_recv()

    def halo_start(buf):
        return (
            copy(buf.at[2 - core], buf.at[3 * core], z, peer(1)),
            copy(buf.at[1 + core], buf.at[3 - 3 * core], other[0], other[1]),
        )

    def halo_finish(buf, copies):
        for c in copies:
            c.wait_recv()

        @pl.when((z == 0) & (core == 0))
        def _():
            buf[0] = jnp.zeros(buf.shape[1:], buf.dtype)

        @pl.when((z == TILES - 1) & (core == 1))
        def _():
            buf[3] = jnp.zeros(buf.shape[1:], buf.dtype)

    def block(device, k):
        return flip(device, k)

    def bias(n):
        return big[...].reshape(GP, 128)[:, n : n + 1]

    def spread(source, target):
        for n, (start, width, low) in enumerate(windows(AP, CB, RAW, CH_DEV)):
            v = dot(source[:, :, low : low + 512].reshape(GP, 512), hots[n])
            target[:, start : start + 256] = v.astype(bf16)

    xs = gather_column(lambda k: xq.at[flip(m, k & 3)], xall, block)
    s1 = group_start(w1p, w1r)
    sbi = group_start(bip, big)
    keep(xq.at[m], xall.at[me]).wait()
    xring = ring_start(xs, xall, block)
    sqb[...] = jnp.zeros(sqb.shape, f32)
    sqb[0:1, 0:SQ] = b4[...]
    wcp[...] = jnp.zeros(wcp.shape, bf16)
    for t in range(9):
        wcp[0:CH_DEV, CI * t : CI * t + 264] = wc[t]
    xrows = ring_relay(xring, xall, block)
    sc = group_start(wcp, wcg)
    for n, (start, width, low) in enumerate(windows(AP, CB, RAW, CH_DEV)):
        hots[n] = one_hot(512, low, 256, start, CB, CH_DEV)
    s1 = group_forward(s1, w1r)
    sbi = group_forward(sbi, big)

    def packing(shape, packed_dim):
        row = lax.broadcasted_iota(jnp.int32, shape, packed_dim)
        lane = lax.broadcasted_iota(jnp.int32, shape, 1 - packed_dim)
        shifted = row
        for part in (1, 2, 3):
            shifted = shifted + jnp.where(row >= CH_DEV * part, CB - CH_DEV, 0)
        return jnp.where((shifted == lane) & (row < 4 * CH_DEV), 1.0, 0.0).astype(bf16)

    group_finish(s1)
    spread(w1r, w1g)
    group_finish(sbi)
    for c in xrows:
        c.wait_recv()

    x_rows = xall[...].reshape(AP, PX)
    first_pre = dot(w1g[...], x_rows) + bias(0)
    active = (first_pre * sigmoid(first_pre)).astype(bf16)
    pack = packing((CI, GP), 0)
    packed = dot(pack, active).astype(bf16)
    ext[1] = packed[:, 0:128]
    ext[2] = packed[:, 128:256]
    halo = halo_start(ext)
    smp[...] = jnp.zeros(smp.shape, bf16)
    smp[0:CH_DEV, 0:SQ] = sqw[...]
    smp[0:CH_DEV, SQP : SQP + SQ] = exw[...]
    ssm = group_start(smp, smg)
    w2p[...] = jnp.zeros(w2p.shape, bf16)
    w2p[0:CH_DEV, 0:NCH] = w2[...]
    s2 = group_start(w2p, w2r)
    sb = sb_in[...]
    sb_top = sb.astype(bf16)
    sbp[...] = jnp.zeros(sbp.shape, bf16)
    sbp[0:CH_DEV, 0:BASIS] = sb_top
    sbp[0:CH_DEV, BASIS:] = (sb - sb_top.astype(f32)).astype(bf16)
    ssb = group_start(sbp, sbg)
    pre[...] = split_right(dot, pack, first_pre)
    sc = group_forward(sc, wcg)
    for k in range(4):
        cols[k, 9 * CI :, :] = jnp.zeros((AP - 9 * CI, PX), bf16)

    def build(read, n_target):
        lanes = lax.broadcasted_iota(jnp.int32, (16, 512), 1) % 64
        for i in range(CI // 16):
            r = 16 * i
            e = jnp.concatenate([read(n, r) for n in range(4)], axis=1).astype(f32)
            for b in (-1, 0, 1):
                if b == 0:
                    v = e
                elif b == 1:
                    v = jnp.where(lanes == 63, 0.0, pltpu.roll(e, 511, 1))
                else:
                    v = jnp.where(lanes == 0, 0.0, pltpu.roll(e, 1, 1))
                s = pltpu.roll(v, 64, 1)
                for a, win in ((-1, s[:, 128:384]), (0, v[:, 128:384]), (1, s[:, 256:512])):
                    t = 3 * (a + 1) + b + 1
                    cols[n_target, t * CI + r : t * CI + r + 16, :] = win.astype(bf16)

    halo_finish(ext, halo)
    build(lambda n, r: ext[n, r : r + 16, :], 0)
    group_finish(sc)

    co = dot(wcg[...].reshape(GP, AP), cols[0]) + bias(1)
    conv_out[...] = co
    hid = co * sigmoid(co)
    hidden[...] = hid
    ones = jnp.ones((8, PX), bf16)
    rows8 = lax.broadcasted_iota(jnp.int32, (8, 128), 0)

    def sums_start(v, buf):
        tile = jnp.zeros((8, 128), f32)
        for j in range(3):
            part = v[128 * j : min(128 * (j + 1), GP)]
            if j == 2:
                part = jnp.concatenate([part, jnp.zeros((64, PX), f32)], axis=0)
            tile = jnp.where(rows8 == 3 * img + j, split_right(dot_nt, ones, part), tile)
        buf[0] = tile
        return [copy(buf.at[0], buf.at[k], z, peer(k)) for k in range(1, 4)]

    def sums_tiles(copies, buf, wider):
        for c in copies:
            c.wait_recv()
        wider[0] = buf[0] + buf[1] + buf[2] + buf[3]
        return [copy(wider.at[0], wider.at[k], flip(z, k), me) for k in (4, 3, 5, 2, 6, 1, 7)]

    def sums_finish(copies, wider):
        for c in copies:
            c.wait_recv()
        tile = sum(wider[k] for k in range(8))
        parts = [
            jnp.where(rows8 == 0, tile[j : j + 1], jnp.where(rows8 == 1, tile[3 + j : 4 + j], 0.0))
            for j in range(3)
        ]
        return jnp.concatenate(parts, axis=1)[:, 0:GP]

    def squeeze_start(v, buf):
        low, high = jnp.zeros((8, 128), f32), jnp.zeros((8, 128), f32)
        for j in range(5):
            part = v[:, 128 * j : 128 * (j + 1)]
            low = jnp.where(rows8 == j, part[0:1], low)
            high = jnp.where(rows8 == j, part[1:2], high)
        buf[0, 0] = low
        buf[0, 1] = high
        return [copy(buf.at[0], buf.at[n + 1], z, peer(k)) for n, k in enumerate(g_masks)]

    def squeeze_finish(copies, buf):
        for c in copies:
            c.wait_recv()
        low = sum(buf[n, 0] for n in range(8))
        high = sum(buf[n, 1] for n in range(8))
        parts = [
            jnp.where(rows8 == 0, low[j : j + 1], jnp.where(rows8 == 1, high[j : j + 1], 0.0))
            for j in range(5)
        ]
        return jnp.concatenate(parts, axis=1)

    ah = sums_start(hid, hs)
    ssm = group_forward(ssm, smg)
    sext = group_start(ext, extg)
    sh = sums_tiles(ah, hs, hz)
    group_finish(ssm)
    fb_copy.wait()
    for b in range(GRP):
        v = fb_in[CH_DEV * b : CH_DEV * (b + 1), :]
        v = jnp.concatenate([v, jnp.zeros((CB - CH_DEV, BASIS), f32)], axis=0)
        top = v.astype(bf16)
        fbp[0, CB * b : CB * (b + 1), :] = top
        fbp[1, CB * b : CB * (b + 1), :] = (v - top.astype(f32)).astype(bf16)
    means = sums_finish(sh, hz) * (1.0 / CELLS)
    sq_w = smg[:, :, 0:SQP].reshape(GP, SQP)
    ex_w = smg[:, :, SQP : 2 * SQP].reshape(GP, SQP)
    bh = squeeze_start(split_left(dot, means, sq_w), hb8)
    for q in range(4):
        cq[q] = dot_nt(eye, c_in[q]).astype(bf16)
    s2 = group_forward(s2, w2r)
    group_finish(s2)
    spread(w2r, w2g)
    xb = dot_tn(fbp[0], x_rows) + dot_tn(fbp[1], x_rows)
    xb_top = xb.astype(bf16)
    xbt[0:BASIS, :] = xb_top
    xbt[BASIS:, :] = (xb - xb_top.astype(f32)).astype(bf16)
    squeeze_pre = squeeze_finish(bh, hb8) + sqb[0:1]
    squeeze = squeeze_pre * sigmoid(squeeze_pre)
    excite = sigmoid(split_right(dot_nt, ex_w, squeeze) + bias(2))
    ex_col = jnp.where(img == 0, excite[:, 0:1], excite[:, 1:2])
    scaled = (hidden[...] * ex_col).astype(bf16)

    unit_a, unit_b, unit_c, unit_d = 2, 3, 1, 0

    def unit(r):
        return pl.ds(2 * flip(col // 2, r), 2)

    def reduce_send(inner, side, r, device):
        at = unit(r)
        return copy(rs_out.at[inner, side, at], rs_in.at[inner, side, at], z, device)

    def reduce_near(inner, side, r, device):
        at = unit(r)
        rs_out[inner, side, at] = rs_keep[side, at].astype(bf16)
        return reduce_send(inner, side, r, device)

    def reduce_pass(inner, side, r, device, arrived):
        at = unit(r)
        arrived.wait_recv()
        rs_out[inner, side, at] = (rs_keep[side, at] + rs_rel[inner, at].astype(f32)).astype(bf16)
        return reduce_send(inner, side, r, device)

    def reduce_start(weights, rhs, inner):
        def part(step):
            at = pl.multiple_of(lax.rem(xx + step, 4) * (8 * CB), 128)
            return dot_tn(weights[:, pl.ds(at, 8 * CB)], rhs).reshape(8, CB, PX)

        rs_far[inner] = part(2).astype(bf16)
        far = {}
        for r, device in ((unit_a, right), (unit_c, left), (unit_b, right), (unit_d, left)):
            far[r] = copy(rs_far.at[inner, unit(r)], rs_rel.at[inner, unit(r)], z, device)
        rs_keep[0] = part(1)
        near = {(0, unit_c): reduce_near(inner, 0, unit_c, right)}
        rs_keep[1] = part(3)
        near[1, unit_a] = reduce_near(inner, 1, unit_a, left)
        rs_own[...] = part(0)
        return far, near

    def reduce_relay(state, inner):
        far, near = state
        near[0, unit_a] = reduce_pass(inner, 0, unit_a, right, far[unit_a])
        near[1, unit_c] = reduce_pass(inner, 1, unit_c, left, far[unit_c])
        near[0, unit_d] = reduce_near(inner, 0, unit_d, right)
        near[1, unit_b] = reduce_near(inner, 1, unit_b, left)
        near[0, unit_b] = reduce_pass(inner, 0, unit_b, right, far[unit_b])
        near[1, unit_d] = reduce_pass(inner, 1, unit_d, left, far[unit_d])
        return near

    def reduce_column(near, inner):
        out = [None] * 7
        for r in (unit_a, unit_c, unit_b, unit_d):
            at = unit(r)
            near[0, r].wait_recv()
            near[1, r].wait_recv()
            total = rs_own[at] + rs_in[inner, 0, at].astype(f32) + rs_in[inner, 1, at].astype(f32)
            rs2_send[inner, at] = total.astype(bf16)
            for k in (2 * r, 2 * r + 1):
                if k:
                    out[k - 1] = copy(rs2_send.at[inner, flip(col, k)], rs2_recv.at[inner, k], z, peer(k))
        return out

    def reduce_quarter(copies, inner, kk):
        copies[kk + 3].wait_recv()
        if kk:
            copies[kk - 1].wait_recv()
            first = rs2_recv[inner, kk]
        else:
            first = rs2_send[inner, col]
        return first.astype(f32) + rs2_recv[inner, kk + 4].astype(f32)

    r1 = reduce_start(w2g, scaled, 0)
    sl = slope(conv_out[...]).astype(bf16)
    for n in range(2):
        exts[n + 1] = sl[:, 128 * n : 128 * (n + 1)]
    halo_s = halo_start(exts)
    sls[...] = sl.reshape(4, CB, PX)
    ssl = [copy(sls.at[flip(m, k)], slr.at[k], z, peer(k)) for k in range(1, 4)]
    r1 = reduce_relay(r1, 0)
    ssb = group_forward(ssb, sbg)
    group_finish(ssb)
    sb_top = sbg[:, :, 0:BASIS].reshape(GP, BASIS)
    sb_low = sbg[:, :, BASIS:].reshape(GP, BASIS)
    u2 = dot_tn(sb_top, scaled) + dot_tn(sb_low, scaled)
    usend[...] = u2.astype(bf16).reshape(8, 32, PX)
    us = [copy(usend.at[flip(g, k // 4)], urecv.at[n + 1], z, peer(k)) for n, k in enumerate(g_masks)]
    ex_row = sigmoid(
        split_left(dot_nt, squeeze, ex_w)
        + split_right(
            dot_nt,
            jnp.where(lax.broadcasted_iota(jnp.int32, (8, 128), 1) == 2, 1.0, 0.0).astype(bf16),
            big[...].reshape(GP, 128),
        )
    )
    halo_finish(exts, halo_s)
    c2cols = reduce_column(r1, 0)
    sext = group_forward(sext, extg)
    back_copies = [None] * 7
    for kk in range(4):
        q = flip(m, kk)
        total = xq[q].astype(f32) + reduce_quarter(c2cols, 0, kk)
        sig = sigmoid(total)
        bo[q] = (total * sig).astype(bf16)
        bq[q] = (cq[q].astype(f32) * (sig * (1.0 + total * (1.0 - sig)))).astype(bf16)
        for k in (kk, kk + 4):
            if k:
                back_copies[k - 1] = copy(bq.at[q], ball.at[me], z, peer(k))
    ball[me] = bq[m]
    bring = ring_start(back_copies, ball, block)
    brows = ring_relay(bring, ball, block)
    for q in range(4):
        bo_out[q] = dot_tn(bo[q], eye).astype(bf16)
    for c in us:
        c.wait_recv()
    u_own = usend[g].astype(f32)
    for n in range(1, 8):
        u_own = u_own + urecv[n].astype(f32)
    u_top = u_own.astype(bf16)
    u_low = (u_own - u_top.astype(f32)).astype(bf16)
    group_finish(sext)

    def build_other(k, carry):
        q = m + (k % 2) * (1 - 2 * (m % 2)) + 2 * (k // 2) * (1 - 2 * (m // 2))
        build(lambda n, r: extg[q, n, r : r + 16, :], k)
        return carry

    lax.fori_loop(1, 4, build_other, 0)
    for c in ssl:
        c.wait_recv()
    gs[0] = dot_nt(sls[m], cols[0]) + dot_nt(slr[1], cols[1])
    gs[1] = dot_nt(slr[2], cols[2]) + dot_nt(slr[3], cols[3])
    for c in brows:
        c.wait_recv()

    back_rows = ball[...].reshape(AP, PX)
    scaled_back = dot(w2g[...], back_rows)
    ae = sums_start(scaled_back * hidden[...], es)
    scaled_back = scaled_back * ex_col
    sback[...] = scaled_back
    edge = scaled_back.astype(bf16)
    for n in range(2):
        exta[n + 1] = edge[:, 128 * n : 128 * (n + 1)]
    halo_a = halo_start(exta)
    hbs[...] = (scaled_back * slope(conv_out[...])).astype(bf16).reshape(4, CB, PX)
    hsw = [copy(hbs.at[flip(m, k)], hbr.at[k], z, peer(k)) for k in range(1, 4)]
    se_ = sums_tiles(ae, es, ez)
    coords = dot_nt(u_top, back_rows) + dot_nt(u_low, back_rows)
    for k in range(4):
        c2s[k] = coords[:, 640 * k : 640 * (k + 1)].astype(bf16)
    c2g = [copy(c2s.at[flip(m, k)], c2r.at[k], z, peer(k)) for k in range(1, 4)]
    for c in hsw:
        c.wait_recv()
    acc = dot_nt(hbs[m], cols[0])
    for k in range(1, 4):
        acc = acc + dot_nt(hbr[k], cols[k])
    ga[...] = acc
    excite_back = sums_finish(se_, ez)
    sig_back = excite_back * ex_row * (1.0 - ex_row)
    be = squeeze_start(split_left(dot, sig_back, ex_w), eb8)
    for c in c2g:
        c.wait_recv()
    c2 = c2s[m].astype(f32) + c2r[1].astype(f32) + c2r[2].astype(f32) + c2r[3].astype(f32)
    c2z[...] = c2.astype(bf16)
    c2t = [copy(c2z, c2zr.at[k], flip(z, k), me) for k in range(1, 8)]
    halo_finish(exta, halo_a)
    squeeze_back = squeeze_finish(be, eb8) * slope(squeeze_pre)
    means_back = split_right(dot_nt, sq_w, squeeze_back)
    mb_col = jnp.where(img == 0, means_back[:, 0:1], means_back[:, 1:2]) * (1.0 / CELLS)
    hb = ((sback[...] + mb_col) * slope(conv_out[...])).astype(bf16)
    mb_all[...] = means_back
    mb_own = mb_all[pl.ds(pl.multiple_of(CB * m, 16), CB), :] * (1.0 / CELLS)
    mb_same = jnp.where(img == 0, mb_own[:, 0:1], mb_own[:, 1:2])
    mb_far = jnp.where(img == 0, mb_own[:, 1:2], mb_own[:, 0:1])
    grads = ga[...] + mb_same * gs[0] + mb_far * gs[1]
    for k in range(TILES - 2):
        zf[k] = grads[:, ZC * k : ZC * (k + 1)]
        zs[k] = grads[:, ZC * k : ZC * (k + 1)].astype(bf16)
    tail = grads[:, ZC * (TILES - 2) :]
    z1 = []
    for k in range(1, 8):
        there = flip(z, k)
        z1.append(later(zs.at[there], zr.at[k], there, me))
        pl.when(there < TILES - 2)(z1[-1].start)
    before, after = [
        ((exta[n].astype(f32) + mb_col) * exts[n].astype(f32)).astype(bf16) for n in (0, 3)
    ]
    hb_wide = jnp.concatenate([before, hb, after], axis=1)

    zbuf[...] = dot_tn(wcg[...].reshape(GP, AP), hb_wide)
    lanes8 = lax.broadcasted_iota(jnp.int32, (16, PX), 1) % 64
    for i in range(CI // 16):
        r = 16 * i
        acc = jnp.zeros((16, PX), f32)
        for b in (-1, 0, 1):
            up = zbuf[CI * (b + 1) + r : CI * (b + 1) + r + 16, :]
            mid = zbuf[CI * (b + 4) + r : CI * (b + 4) + r + 16, :]
            down = zbuf[CI * (b + 7) + r : CI * (b + 7) + r + 16, :]
            y = mid[:, 128:384] + pltpu.roll(up, 64, 1)[:, 256:512] + pltpu.roll(down, 64, 1)[:, 128:384]
            if b == 1:
                y = jnp.where(lanes8 == 0, 0.0, pltpu.roll(y, 1, 1))
            elif b == -1:
                y = jnp.where(lanes8 == 63, 0.0, pltpu.roll(y, PX - 1, 1))
            acc = acc + y
        pre[r : r + 16, :] = acc * slope(pre[r : r + 16, :])
    unpack = packing((GP, CI), 1)
    ag = dot(unpack, pre[...].astype(bf16)).astype(bf16)
    c1 = dot_nt(ag, xbt[0:BASIS, :]) + dot_nt(ag, xbt[BASIS:, :])
    c1s[...] = c1.astype(bf16).reshape(4, CB, BASIS)
    c1g = [copy(c1s.at[flip(m, k)], c1r.at[k], z, peer(k)) for k in range(1, 4)]
    r2 = reduce_start(w1g, ag, 1)

    for c in c1g:
        c.wait_recv()
    c1 = c1s[m].astype(f32) + c1r[1].astype(f32) + c1r[2].astype(f32) + c1r[3].astype(f32)
    both = jnp.concatenate([tail, c1, jnp.zeros((CB, TILES * ZC - AP - BASIS), f32)], axis=1)
    for k in (TILES - 2, TILES - 1):
        part = both[:, ZC * (k - TILES + 2) : ZC * (k - TILES + 3)]
        zf[k] = part
        zs[k] = part.astype(bf16)
    for k in range(1, 8):
        pl.when(flip(z, k) >= TILES - 2)(z1[k - 1].start)
    r2 = reduce_relay(r2, 1)
    for c in c2t:
        c.wait_recv()
    c2 = c2z[...].astype(f32)
    for k in range(1, 8):
        c2 = c2 + c2zr[k].astype(f32)

    def slot2(device, k):
        d = flip(device, k)
        return (d % 4) * 8 + d // 4

    same = (0, 2, 4, 6)
    c2all[slot2(me, 0)] = c2.astype(bf16)
    c2c = gather_column(lambda k: c2all.at[slot2(me, 0)], c2all, slot2, same[1:])
    c2cols = reduce_column(r2, 1)
    c2ring = ring_start(c2c, c2all, slot2, same)
    for c in z1:
        c.wait_recv()
    chunk = zf[z]
    for k in range(1, 8):
        chunk = chunk + zr[k].astype(f32)
    zall[z] = chunk.astype(bf16)
    z2 = [copy(zall.at[z], zall.at[z], flip(z, k), me) for k in range(1, 8)]
    c2rows = ring_relay(c2ring, c2all, slot2, same)
    for kk in range(4):
        q = flip(m, kk)
        ig_out[q] = dot_tn((bq[q].astype(f32) + reduce_quarter(c2cols, 1, kk)).astype(bf16), eye).astype(bf16)
    swaps = [copy(c2all.at[slot2(me, k)], c2all.at[slot2(me, k)], z, peer(1)) for k in same]
    for c in c2rows:
        c.wait_recv()
    for step in (1, 2, 3):
        there = lax.rem(me + 8 * step, GRP)
        for k in same:
            at = slot2(there, k)
            swaps.append(copy(c2all.at[at], c2all.at[at], z, peer(1)))

    first = lax.broadcasted_iota(jnp.int32, (CB, GP), 0) + CB * m
    mine = jnp.where(first == lax.broadcasted_iota(jnp.int32, (CB, GP), 1), 1.0, 0.0).astype(bf16)
    own = split_right(dot_nt, mine, means)
    grad = own[:, 0:1] * squeeze_back[0:1] + own[:, 1:2] * squeeze_back[1:2]
    sqg[...] = (grad * GRAD_SCALE)[0:CH_DEV, 0:SQ]
    own = split_right(dot_nt, mine, sig_back)
    grad = own[:, 0:1] * squeeze[0:1] + own[:, 1:2] * squeeze[1:2]
    exg[...] = (grad * GRAD_SCALE)[0:CH_DEV, 0:SQ]
    for n, (start, width, low) in enumerate(windows(NCH, CH_DEV, AP, CB)):
        hots2[n] = one_hot(512, low, 256, start, CH_DEV, CB)
    fb = fb_in[...]
    top = fb.astype(bf16)
    fbn[0] = top
    fbn[1] = (fb - top.astype(f32)).astype(bf16)
    for c in swaps:
        c.wait_recv()
    wide = jnp.concatenate([c2all[8 * k : 8 * (k + 1)].reshape(BASIS, 640) for k in range(4)], axis=1)
    own_top = sbp[:, 0:BASIS]
    own_low = sbp[:, BASIS:]
    for n, (start, width, low) in enumerate(windows(NCH, CH_DEV, AP, CB)):
        v = dot(wide[:, low : low + 512], hots2[n]).astype(bf16)
        v = (dot(own_top, v) + dot(own_low, v)) * GRAD_SCALE
        sg[:, start : start + width] = v[0:CH_DEV, 0:width]
    for c in z2:
        c.wait_recv()
    lanes_left = AP - ZC * 6
    c1 = jnp.concatenate([zall[6, :, lanes_left:], zall[7, :, 0 : BASIS - (ZC - lanes_left)]], axis=1)
    v = (dot_nt(c1, fbn[0]) + dot_nt(c1, fbn[1])) * GRAD_SCALE
    fg[...] = v[0:CH_DEV]
    sums = jnp.concatenate([zall[k] for k in range(7)], axis=1).astype(f32) * GRAD_SCALE
    for t in range(9):
        cg[t] = sums[0:CH_DEV, CI * t : CI * t + 264]
    for c in started:
        c.wait_send()


def copy_out(*refs):
    sems = refs[14]
    copies = [pltpu.make_async_copy(refs[n], refs[n + 7], sems.at[n]) for n in range(7)]
    for c in copies:
        c.start()
    for c in copies:
        c.wait()


def per_device(
    inputs,
    cotangent,
    first_weight,
    first_bias,
    conv_weight,
    conv_bias,
    squeeze_weight,
    squeeze_bias,
    excite_weight,
    excite_bias,
    second_weight,
    first_basis,
    second_basis,
):
    V = pltpu.VMEM
    scratch = [
        V((4, CB, PX), bf16),
        V((4, CB, PX), bf16),
        V((NCH, BASIS), f32),
        V((8, 128), f32),
        V((8, SQP), f32),
        V((GRP, CB, PX), bf16),
        V((GRP, CB, PX), bf16),
        V((CB, RAW), bf16),
        V((CB, RAW), bf16),
        V((CB, AP), bf16),
        V((CB, 2 * SQP), bf16),
        V((CB, 2 * BASIS), bf16),
        V((CB, 128), f32),
        V((4, CB, RAW), bf16),
        V((4, CB, RAW), bf16),
        V((GP, AP), bf16),
        V((4, CB, AP), bf16),
        V((GP, AP), bf16),
        V((4, CB, 2 * SQP), bf16),
        V((4, CB, 2 * BASIS), bf16),
        V((4, CB, 128), f32),
        V((10, 512, 256), bf16),
        V((9, 512, 256), bf16),
        V((2, AP, BASIS), bf16),
        V((2, NCH, BASIS), bf16),
        V((4, CI, 128), bf16),
        V((4, 4, CI, 128), bf16),
        V((4, GP, 128), bf16),
        V((4, GP, 128), bf16),
        V((4, AP, PX), bf16),
        V((CI, PX), f32),
        V((GP, PX), f32),
        V((GP, PX), f32),
        V((GP, PX), f32),
        V((2 * BASIS, PX), bf16),
        V((AP, 512), f32),
        V((4, CB, PX), bf16),
        V((2, 8, CB, PX), bf16),
        V((2, 8, CB, PX), bf16),
        V((2, 8, CB, PX), f32),
        V((2, 2, 8, CB, PX), bf16),
        V((2, 2, 8, CB, PX), bf16),
        V((8, CB, PX), f32),
        V((2, 8, CB, PX), bf16),
        V((2, 8, CB, PX), bf16),
        V((4, CB, PX), bf16),
        V((8, 32, PX), bf16),
        V((8, 32, PX), bf16),
        V((4, 32, 640), bf16),
        V((4, 32, 640), bf16),
        V((32, 640), bf16),
        V((8, 32, 640), bf16),
        V((32, 32, 640), bf16),
        V((4, CB, PX), bf16),
        V((4, CB, PX), bf16),
        V((2, CB, AP), f32),
        V((CB, AP), f32),
        V((GP, 8), f32),
        V((4, 8, 128), f32),
        V((8, 8, 128), f32),
        V((8, 2, 8, 128), f32),
        V((4, 8, 128), f32),
        V((8, 8, 128), f32),
        V((8, 2, 8, 128), f32),
        V((4, CB, PX), bf16),
        V((4, CB, PX), bf16),
        V((4, CB, BASIS), bf16),
        V((4, CB, BASIS), bf16),
        V((TILES, CB, ZC), bf16),
        V((TILES, CB, ZC), f32),
        V((TILES, CB, ZC), bf16),
        V((TILES, CB, ZC), bf16),
        pltpu.SemaphoreType.DMA((NSEM,)),
        pltpu.SemaphoreType.DMA((NSEM,)),
        pltpu.SemaphoreType.DMA((16,)),
    ]
    spec = pl.BlockSpec(memory_space=pltpu.VMEM)
    shape = jax.ShapeDtypeStruct
    bo, ig, fg, sg, cg, sqg, exg = pl.pallas_call(
        body,
        out_shape=[
            shape((4, PX, CH_DEV), bf16),
            shape((4, PX, CH_DEV), bf16),
            shape((CH_DEV, NCH), f32),
            shape((CH_DEV, NCH), f32),
            shape((9, CH_DEV, 264), f32),
            shape((CH_DEV, SQ), f32),
            shape((CH_DEV, SQ), f32),
        ],
        in_specs=[spec] * 8 + [pl.BlockSpec(memory_space=pl.ANY)] + [spec] * 4,
        out_specs=[spec] * 7,
        scratch_shapes=scratch,
        compiler_params=pltpu.CompilerParams(
            collective_id=0, has_side_effects=True, vmem_limit_bytes=62 * 1024 * 1024
        ),
    )(
        inputs.reshape(4, PX, CH_DEV), cotangent.reshape(4, PX, CH_DEV),
        first_weight.T, conv_weight.transpose(1, 0, 2), second_weight,
        squeeze_weight, excite_weight.T, second_basis, first_basis,
        first_bias[None], conv_bias[None], excite_bias[None], squeeze_bias[None],
    )

    results = (bo, ig, fg, sg, cg, sqg, exg)
    bo, ig, fg, sg, cg, sqg, exg = pl.pallas_call(
        copy_out,
        out_shape=[shape(v.shape, v.dtype) for v in results],
        in_specs=[pl.BlockSpec(memory_space=pl.ANY)] * 7,
        out_specs=[pl.BlockSpec(memory_space=pl.ANY)] * 7,
        scratch_shapes=[pltpu.SemaphoreType.DMA((7,))],
    )(*results)
    return (bo.reshape(inputs.shape), ig.reshape(inputs.shape), fg.T, sg, cg.transpose(1, 0, 2), sqg, exg.T)


def solution(mesh):
    placed = (
        P(None, "tile", None, "grp"),
        P(None, "tile", None, "grp"),
        P(None, "grp"),
        P("grp"),
        P("grp", None, None),
        P("grp"),
        P("grp", None),
        P(),
        P(None, "grp"),
        P("grp"),
        P("grp", None),
        P(),
        P("grp", None),
    )
    return jax.shard_map(
        per_device,
        mesh=mesh,
        in_specs=placed,
        out_specs=(
            P(None, "tile", None, "grp"),
            P(None, "tile", None, "grp"),
            P(None, "grp"),
            P("grp", None),
            P("grp", None, None),
            P("grp", None),
            P(None, "grp"),
        ),
        check_vma=False,
    )
```

```python
import math

import jax
import jax.numpy as jnp
from jax import lax
from jax.experimental import pallas as pl
from jax.experimental.pallas import tpu as pltpu
from jax.sharding import PartitionSpec as P

MESH = pl.DeviceIdType.MESH
highest = lax.Precision.HIGHEST
bf16, f32 = jnp.bfloat16, jnp.float32

TILES = 8
GRP = 32
CH_DEV = 66
CB = 80
PX = 256
GP = 4 * CB
AP = GRP * CB
CI = 272
SQ = 528
SQP = 640
BASIS = 256
ZC = 384
CELLS = 4096.0
NSEM = 250
RAW = 2176
NCH = 2112
GRAD_SCALE = 1.0 / math.sqrt(8192.0)


def flip(index, mask):
    out = index
    for bit in range(5):
        if mask >> bit & 1:
            step = 1 << bit
            out = out + step * (1 - 2 * ((index // step) % 2))
    return out


def sigmoid(v):
    return 1.0 / (1.0 + jnp.exp(-v))


def slope(v):
    sig = sigmoid(v)
    return sig * (1.0 + v * (1.0 - sig))


def dot(a, b):
    return lax.dot_general(a, b, (((1,), (0,)), ((), ())), preferred_element_type=f32)


def dot_nt(a, b):
    return lax.dot_general(a, b, (((1,), (1,)), ((), ())), preferred_element_type=f32)


def pieces(v, count):
    out = []
    for _ in range(count - 1):
        top = v.astype(bf16)
        out.append(top)
        v = v - top.astype(f32)
    out.append(v.astype(bf16))
    return out


def dot_tn(a, b):
    return lax.dot_general(a, b, (((0,), (0,)), ((), ())), preferred_element_type=f32)


def one_hot(rows, row_start, lanes, lane_start, out_width, in_width):
    r = lax.broadcasted_iota(jnp.int32, (rows, lanes), 0) + row_start
    out = lax.broadcasted_iota(jnp.int32, (rows, lanes), 1) + lane_start
    blk = (out * ((1 << 22) // out_width + 1)) >> 22
    hit = (out - out_width * blk < CH_DEV) & (r == out + (in_width - out_width) * blk) & (blk < GRP)
    return jnp.where(hit, 1.0, 0.0).astype(bf16)


def windows(out_lanes, out_width, in_lanes, in_width):
    for start in range(0, out_lanes, 256):
        width = min(256, out_lanes - start)
        low = min(start // out_width * in_width // 128 * 128, in_lanes - 512)
        yield start, width, low


def split_left(op, a, b, count=3):
    return sum(op(p, b) for p in pieces(a, count))


def split_right(op, a, b, count=3):
    return sum(op(a, p) for p in pieces(b, count))


def body(
    x_in, c_in, w1, wc, w2, sqw, exw, sb_in, fb_hbm, b1, b2, b3, b4,
    bo_out, ig_out, fg, sg, cg, sqg, exg,
    xq, cq, fb_in, bt, sqb, xall, ball, w1p, w2p, wcp, smp, sbp, bip, w1r, w2r, w1g, wcg, w2g, smg, sbg, big,
    hots, hots2, fbp, fbn,
    ext, extg, exts, exta, cols, pre, conv_out, hidden, sback, xbt, zbuf,
    bo, rs_far, rs_rel, rs_keep, rs_out, rs_in, rs_own, rs2_send, rs2_recv, bq,
    usend, urecv, c2s, c2r, c2z, c2zr, c2all,
    sls, slr, gs, ga, mb_all, hs, hz, hb8, es, ez, eb8, hbs, hbr, c1s, c1r, zs, zf, zr, zall,
    send, recv, local,
):
    z = lax.axis_index("tile")
    me = lax.axis_index("grp")
    xx = me // 8
    col = me % 8
    m = me % 4
    g = me // 4
    core = me % 2
    img = (me // 2) % 2
    count = [0]
    started = []
    locals_ = []

    def later(src, dst, tile, grp):
        i = count[0]
        count[0] += 1
        c = pltpu.make_async_remote_copy(
            src_ref=src, dst_ref=dst, send_sem=send.at[i], recv_sem=recv.at[i],
            device_id=(tile, grp), device_id_type=MESH,
        )
        started.append(c)
        return c

    def copy(src, dst, tile, grp):
        c = later(src, dst, tile, grp)
        c.start()
        return c

    def keep(src, dst):
        c = pltpu.make_async_copy(src, dst, local.at[len(locals_)])
        c.start()
        locals_.append(c)
        return c

    def peer(mask):
        return flip(me, mask)

    right, left = lax.rem(me + 8, GRP), lax.rem(me + 24, GRP)
    other = (lax.rem(z + 2 * core - 1 + TILES, TILES), flip(me, 1))
    grp_masks = [1, 2, 3, 4, 5, 6, 7, 8, 16, 24, 12, 20, 28]
    g_masks = [4, 8, 12, 16, 20, 24, 28]

    barrier = pltpu.get_barrier_semaphore()
    for mask in grp_masks:
        pl.semaphore_signal(barrier, inc=1, device_id=(z, peer(mask)), device_id_type=MESH)
    for mask in range(1, 8):
        pl.semaphore_signal(barrier, inc=1, device_id=(flip(z, mask), me), device_id_type=MESH)
    pl.semaphore_signal(barrier, inc=1, device_id=other, device_id_type=MESH)

    fb_copy = keep(fb_hbm, fb_in)
    diagonal = lax.broadcasted_iota(jnp.int32, (CB, CH_DEV), 0) == lax.broadcasted_iota(jnp.int32, (CB, CH_DEV), 1)
    eye = jnp.where(diagonal, 1.0, 0.0).astype(bf16)
    for q in range(4):
        xq[q] = dot_nt(eye, x_in[q]).astype(bf16)
    w1p[...] = jnp.zeros(w1p.shape, bf16)
    w1p[0:CH_DEV, 0:NCH] = w1[...]
    bt[...] = jnp.zeros(bt.shape, f32)
    for n, vector in enumerate((b1, b2, b3)):
        bt[n : n + 1, 0:CH_DEV] = vector[...]
    bip[...] = jnp.zeros(bip.shape, f32)
    bip[:, 0:8] = bt[...].T[0:CB]
    pl.semaphore_wait(barrier, len(grp_masks) + 8)

    def gather_column(pick, dst, slot, masks=range(1, 8)):
        return [copy(pick(k), dst.at[slot(me, 0)], z, peer(k)) for k in masks]

    def ring_start(arrived, dst, slot, masks=range(8)):
        to_right, to_left = [], []
        for n, k in enumerate(masks):
            if n:
                arrived[n - 1].wait_recv()
            at = slot(me, k)
            to_right.append(copy(dst.at[at], dst.at[at], z, right))
            to_left.append(copy(dst.at[at], dst.at[at], z, left))
        return to_right, to_left

    def ring_relay(state, dst, slot, masks=range(8)):
        to_right, to_left = state
        half = len(masks) // 2
        relayed = []
        for n in range(half):
            to_right[n].wait_recv()
            at = slot(left, masks[n])
            relayed.append(copy(dst.at[at], dst.at[at], z, right))
            to_left[n + half].wait_recv()
            at = slot(right, masks[n + half])
            relayed.append(copy(dst.at[at], dst.at[at], z, left))
        return to_right[half:] + to_left[:half] + relayed

    def group_start(src, dst):
        mine = keep(src, dst.at[m])
        return mine, copy(src, dst.at[m], z, peer(1)), copy(src, dst.at[m], z, peer(2))

    def group_forward(state, dst):
        mine, near, far = state
        far.wait_recv()
        slot = flip(m, 2)
        return mine, near, copy(dst.at[slot], dst.at[slot], z, peer(1))

    def group_finish(state):
        state[0].wait()
        state[1].wait_recv()
        state[2].wait_recv()

    def halo_start(buf):
        return (
            copy(buf.at[2 - core], buf.at[3 * core], z, peer(1)),
            copy(buf.at[1 + core], buf.at[3 - 3 * core], other[0], other[1]),
        )

    def halo_finish(buf, copies):
        for c in copies:
            c.wait_recv()

        @pl.when((z == 0) & (core == 0))
        def _():
            buf[0] = jnp.zeros(buf.shape[1:], buf.dtype)

        @pl.when((z == TILES - 1) & (core == 1))
        def _():
            buf[3] = jnp.zeros(buf.shape[1:], buf.dtype)

    def block(device, k):
        return flip(device, k)

    def bias(n):
        return big[...].reshape(GP, 128)[:, n : n + 1]

    def spread(source, target):
        for n, (start, width, low) in enumerate(windows(AP, CB, RAW, CH_DEV)):
            v = dot(source[:, :, low : low + 512].reshape(GP, 512), hots[n])
            target[:, start : start + 256] = v.astype(bf16)

    xs = gather_column(lambda k: xq.at[flip(m, k & 3)], xall, block)
    s1 = group_start(w1p, w1r)
    sbi = group_start(bip, big)
    keep(xq.at[m], xall.at[me]).wait()
    xring = ring_start(xs, xall, block)
    sqb[...] = jnp.zeros(sqb.shape, f32)
    sqb[0:1, 0:SQ] = b4[...]
    wcp[...] = jnp.zeros(wcp.shape, bf16)
    for t in range(9):
        wcp[0:CH_DEV, CI * t : CI * t + 264] = wc[t]
    xrows = ring_relay(xring, xall, block)
    sc = group_start(wcp, wcg)
    for n, (start, width, low) in enumerate(windows(AP, CB, RAW, CH_DEV)):
        hots[n] = one_hot(512, low, 256, start, CB, CH_DEV)
    s1 = group_forward(s1, w1r)
    sbi = group_forward(sbi, big)

    def packing(shape, packed_dim):
        row = lax.broadcasted_iota(jnp.int32, shape, packed_dim)
        lane = lax.broadcasted_iota(jnp.int32, shape, 1 - packed_dim)
        shifted = row
        for part in (1, 2, 3):
            shifted = shifted + jnp.where(row >= CH_DEV * part, CB - CH_DEV, 0)
        return jnp.where((shifted == lane) & (row < 4 * CH_DEV), 1.0, 0.0).astype(bf16)

    group_finish(s1)
    spread(w1r, w1g)
    group_finish(sbi)
    for c in xrows:
        c.wait_recv()

    x_rows = xall[...].reshape(AP, PX)
    first_pre = dot(w1g[...], x_rows) + bias(0)
    active = (first_pre * sigmoid(first_pre)).astype(bf16)
    pack = packing((CI, GP), 0)
    packed = dot(pack, active).astype(bf16)
    ext[1] = packed[:, 0:128]
    ext[2] = packed[:, 128:256]
    halo = halo_start(ext)
    smp[...] = jnp.zeros(smp.shape, bf16)
    smp[0:CH_DEV, 0:SQ] = sqw[...]
    smp[0:CH_DEV, SQP : SQP + SQ] = exw[...]
    ssm = group_start(smp, smg)
    w2p[...] = jnp.zeros(w2p.shape, bf16)
    w2p[0:CH_DEV, 0:NCH] = w2[...]
    s2 = group_start(w2p, w2r)
    sb = sb_in[...]
    sb_top = sb.astype(bf16)
    sbp[...] = jnp.zeros(sbp.shape, bf16)
    sbp[0:CH_DEV, 0:BASIS] = sb_top
    sbp[0:CH_DEV, BASIS:] = (sb - sb_top.astype(f32)).astype(bf16)
    ssb = group_start(sbp, sbg)
    pre[...] = split_right(dot, pack, first_pre)
    sc = group_forward(sc, wcg)
    for k in range(4):
        cols[k, 9 * CI :, :] = jnp.zeros((AP - 9 * CI, PX), bf16)

    def build(read, n_target):
        lanes = lax.broadcasted_iota(jnp.int32, (16, 512), 1) % 64
        for i in range(CI // 16):
            r = 16 * i
            e = jnp.concatenate([read(n, r) for n in range(4)], axis=1).astype(f32)
            for b in (-1, 0, 1):
                if b == 0:
                    v = e
                elif b == 1:
                    v = jnp.where(lanes == 63, 0.0, pltpu.roll(e, 511, 1))
                else:
                    v = jnp.where(lanes == 0, 0.0, pltpu.roll(e, 1, 1))
                s = pltpu.roll(v, 64, 1)
                for a, win in ((-1, s[:, 128:384]), (0, v[:, 128:384]), (1, s[:, 256:512])):
                    t = 3 * (a + 1) + b + 1
                    cols[n_target, t * CI + r : t * CI + r + 16, :] = win.astype(bf16)

    halo_finish(ext, halo)
    build(lambda n, r: ext[n, r : r + 16, :], 0)
    group_finish(sc)

    co = dot(wcg[...].reshape(GP, AP), cols[0]) + bias(1)
    conv_out[...] = co
    hid = co * sigmoid(co)
    hidden[...] = hid
    ones = jnp.ones((8, PX), bf16)
    rows8 = lax.broadcasted_iota(jnp.int32, (8, 128), 0)

    def sums_start(v, buf):
        tile = jnp.zeros((8, 128), f32)
        for j in range(3):
            part = v[128 * j : min(128 * (j + 1), GP)]
            if j == 2:
                part = jnp.concatenate([part, jnp.zeros((64, PX), f32)], axis=0)
            tile = jnp.where(rows8 == 3 * img + j, split_right(dot_nt, ones, part), tile)
        buf[0] = tile
        return [copy(buf.at[0], buf.at[k], z, peer(k)) for k in range(1, 4)]

    def sums_tiles(copies, buf, wider):
        for c in copies:
            c.wait_recv()
        wider[0] = buf[0] + buf[1] + buf[2] + buf[3]
        return [copy(wider.at[0], wider.at[k], flip(z, k), me) for k in (4, 3, 5, 2, 6, 1, 7)]

    def sums_finish(copies, wider):
        for c in copies:
            c.wait_recv()
        tile = sum(wider[k] for k in range(8))
        parts = [
            jnp.where(rows8 == 0, tile[j : j + 1], jnp.where(rows8 == 1, tile[3 + j : 4 + j], 0.0))
            for j in range(3)
        ]
        return jnp.concatenate(parts, axis=1)[:, 0:GP]

    def squeeze_start(v, buf):
        low, high = jnp.zeros((8, 128), f32), jnp.zeros((8, 128), f32)
        for j in range(5):
            part = v[:, 128 * j : 128 * (j + 1)]
            low = jnp.where(rows8 == j, part[0:1], low)
            high = jnp.where(rows8 == j, part[1:2], high)
        buf[0, 0] = low
        buf[0, 1] = high
        return [copy(buf.at[0], buf.at[n + 1], z, peer(k)) for n, k in enumerate(g_masks)]

    def squeeze_finish(copies, buf):
        for c in copies:
            c.wait_recv()
        low = sum(buf[n, 0] for n in range(8))
        high = sum(buf[n, 1] for n in range(8))
        parts = [
            jnp.where(rows8 == 0, low[j : j + 1], jnp.where(rows8 == 1, high[j : j + 1], 0.0))
            for j in range(5)
        ]
        return jnp.concatenate(parts, axis=1)

    ah = sums_start(hid, hs)
    ssm = group_forward(ssm, smg)
    sext = group_start(ext, extg)
    sh = sums_tiles(ah, hs, hz)
    group_finish(ssm)
    fb_copy.wait()
    for b in range(GRP):
        v = fb_in[CH_DEV * b : CH_DEV * (b + 1), :]
        v = jnp.concatenate([v, jnp.zeros((CB - CH_DEV, BASIS), f32)], axis=0)
        top = v.astype(bf16)
        fbp[0, CB * b : CB * (b + 1), :] = top
        fbp[1, CB * b : CB * (b + 1), :] = (v - top.astype(f32)).astype(bf16)
    means = sums_finish(sh, hz) * (1.0 / CELLS)
    sq_w = smg[:, :, 0:SQP].reshape(GP, SQP)
    ex_w = smg[:, :, SQP : 2 * SQP].reshape(GP, SQP)
    bh = squeeze_start(split_left(dot, means, sq_w), hb8)
    for q in range(4):
        cq[q] = dot_nt(eye, c_in[q]).astype(bf16)
    s2 = group_forward(s2, w2r)
    group_finish(s2)
    spread(w2r, w2g)
    xb = dot_tn(fbp[0], x_rows) + dot_tn(fbp[1], x_rows)
    xb_top = xb.astype(bf16)
    xbt[0:BASIS, :] = xb_top
    xbt[BASIS:, :] = (xb - xb_top.astype(f32)).astype(bf16)
    squeeze_pre = squeeze_finish(bh, hb8) + sqb[0:1]
    squeeze = squeeze_pre * sigmoid(squeeze_pre)
    excite = sigmoid(split_right(dot_nt, ex_w, squeeze) + bias(2))
    ex_col = jnp.where(img == 0, excite[:, 0:1], excite[:, 1:2])
    scaled = (hidden[...] * ex_col).astype(bf16)

    unit_a, unit_b, unit_c, unit_d = 2, 3, 1, 0

    def unit(r):
        return pl.ds(2 * flip(col // 2, r), 2)

    def reduce_send(inner, side, r, device):
        at = unit(r)
        return copy(rs_out.at[inner, side, at], rs_in.at[inner, side, at], z, device)

    def reduce_near(inner, side, r, device):
        at = unit(r)
        rs_out[inner, side, at] = rs_keep[side, at].astype(bf16)
        return reduce_send(inner, side, r, device)

    def reduce_pass(inner, side, r, device, arrived):
        at = unit(r)
        arrived.wait_recv()
        rs_out[inner, side, at] = (rs_keep[side, at] + rs_rel[inner, at].astype(f32)).astype(bf16)
        return reduce_send(inner, side, r, device)

    def reduce_start(weights, rhs, inner):
        def part(step):
            at = pl.multiple_of(lax.rem(xx + step, 4) * (8 * CB), 128)
            return dot_tn(weights[:, pl.ds(at, 8 * CB)], rhs).reshape(8, CB, PX)

        rs_far[inner] = part(2).astype(bf16)
        far = {}
        for r, device in ((unit_a, right), (unit_c, left), (unit_b, right), (unit_d, left)):
            far[r] = copy(rs_far.at[inner, unit(r)], rs_rel.at[inner, unit(r)], z, device)
        rs_keep[0] = part(1)
        near = {(0, unit_c): reduce_near(inner, 0, unit_c, right)}
        rs_keep[1] = part(3)
        near[1, unit_a] = reduce_near(inner, 1, unit_a, left)
        rs_own[...] = part(0)
        return far, near

    def reduce_relay(state, inner):
        far, near = state
        near[0, unit_a] = reduce_pass(inner, 0, unit_a, right, far[unit_a])
        near[1, unit_c] = reduce_pass(inner, 1, unit_c, left, far[unit_c])
        near[0, unit_d] = reduce_near(inner, 0, unit_d, right)
        near[1, unit_b] = reduce_near(inner, 1, unit_b, left)
        near[0, unit_b] = reduce_pass(inner, 0, unit_b, right, far[unit_b])
        near[1, unit_d] = reduce_pass(inner, 1, unit_d, left, far[unit_d])
        return near

    def reduce_column(near, inner):
        out = [None] * 7
        for r in (unit_a, unit_c, unit_b, unit_d):
            at = unit(r)
            near[0, r].wait_recv()
            near[1, r].wait_recv()
            total = rs_own[at] + rs_in[inner, 0, at].astype(f32) + rs_in[inner, 1, at].astype(f32)
            rs2_send[inner, at] = total.astype(bf16)
            for k in (2 * r, 2 * r + 1):
                if k:
                    out[k - 1] = copy(rs2_send.at[inner, flip(col, k)], rs2_recv.at[inner, k], z, peer(k))
        return out

    def reduce_quarter(copies, inner, kk):
        copies[kk + 3].wait_recv()
        if kk:
            copies[kk - 1].wait_recv()
            first = rs2_recv[inner, kk]
        else:
            first = rs2_send[inner, col]
        return first.astype(f32) + rs2_recv[inner, kk + 4].astype(f32)

    r1 = reduce_start(w2g, scaled, 0)
    sl = slope(conv_out[...]).astype(bf16)
    for n in range(2):
        exts[n + 1] = sl[:, 128 * n : 128 * (n + 1)]
    halo_s = halo_start(exts)
    sls[...] = sl.reshape(4, CB, PX)
    ssl = [copy(sls.at[flip(m, k)], slr.at[k], z, peer(k)) for k in range(1, 4)]
    r1 = reduce_relay(r1, 0)
    ssb = group_forward(ssb, sbg)
    group_finish(ssb)
    sb_top = sbg[:, :, 0:BASIS].reshape(GP, BASIS)
    sb_low = sbg[:, :, BASIS:].reshape(GP, BASIS)
    u2 = dot_tn(sb_top, scaled) + dot_tn(sb_low, scaled)
    usend[...] = u2.astype(bf16).reshape(8, 32, PX)
    us = [copy(usend.at[flip(g, k // 4)], urecv.at[n + 1], z, peer(k)) for n, k in enumerate(g_masks)]
    ex_row = sigmoid(
        split_left(dot_nt, squeeze, ex_w)
        + split_right(
            dot_nt,
            jnp.where(lax.broadcasted_iota(jnp.int32, (8, 128), 1) == 2, 1.0, 0.0).astype(bf16),
            big[...].reshape(GP, 128),
        )
    )
    halo_finish(exts, halo_s)
    c2cols = reduce_column(r1, 0)
    sext = group_forward(sext, extg)
    back_copies = [None] * 7
    for kk in range(4):
        q = flip(m, kk)
        total = xq[q].astype(f32) + reduce_quarter(c2cols, 0, kk)
        sig = sigmoid(total)
        bo[q] = (total * sig).astype(bf16)
        bq[q] = (cq[q].astype(f32) * (sig * (1.0 + total * (1.0 - sig)))).astype(bf16)
        for k in (kk, kk + 4):
            if k:
                back_copies[k - 1] = copy(bq.at[q], ball.at[me], z, peer(k))
    ball[me] = bq[m]
    bring = ring_start(back_copies, ball, block)
    brows = ring_relay(bring, ball, block)
    for q in range(4):
        bo_out[q] = dot_tn(bo[q], eye).astype(bf16)
    for c in us:
        c.wait_recv()
    u_own = usend[g].astype(f32)
    for n in range(1, 8):
        u_own = u_own + urecv[n].astype(f32)
    u_top = u_own.astype(bf16)
    u_low = (u_own - u_top.astype(f32)).astype(bf16)
    group_finish(sext)

    def build_other(k, carry):
        q = m + (k % 2) * (1 - 2 * (m % 2)) + 2 * (k // 2) * (1 - 2 * (m // 2))
        build(lambda n, r: extg[q, n, r : r + 16, :], k)
        return carry

    lax.fori_loop(1, 4, build_other, 0)
    for c in ssl:
        c.wait_recv()
    gs[0] = dot_nt(sls[m], cols[0]) + dot_nt(slr[1], cols[1])
    gs[1] = dot_nt(slr[2], cols[2]) + dot_nt(slr[3], cols[3])
    for c in brows:
        c.wait_recv()

    back_rows = ball[...].reshape(AP, PX)
    scaled_back = dot(w2g[...], back_rows)
    ae = sums_start(scaled_back * hidden[...], es)
    scaled_back = scaled_back * ex_col
    sback[...] = scaled_back
    edge = scaled_back.astype(bf16)
    for n in range(2):
        exta[n + 1] = edge[:, 128 * n : 128 * (n + 1)]
    halo_a = halo_start(exta)
    hbs[...] = (scaled_back * slope(conv_out[...])).astype(bf16).reshape(4, CB, PX)
    hsw = [copy(hbs.at[flip(m, k)], hbr.at[k], z, peer(k)) for k in range(1, 4)]
    se_ = sums_tiles(ae, es, ez)
    coords = dot_nt(u_top, back_rows) + dot_nt(u_low, back_rows)
    for k in range(4):
        c2s[k] = coords[:, 640 * k : 640 * (k + 1)].astype(bf16)
    c2g = [copy(c2s.at[flip(m, k)], c2r.at[k], z, peer(k)) for k in range(1, 4)]
    for c in hsw:
        c.wait_recv()
    acc = dot_nt(hbs[m], cols[0])
    for k in range(1, 4):
        acc = acc + dot_nt(hbr[k], cols[k])
    ga[...] = acc
    excite_back = sums_finish(se_, ez)
    sig_back = excite_back * ex_row * (1.0 - ex_row)
    be = squeeze_start(split_left(dot, sig_back, ex_w), eb8)
    for c in c2g:
        c.wait_recv()
    c2 = c2s[m].astype(f32) + c2r[1].astype(f32) + c2r[2].astype(f32) + c2r[3].astype(f32)
    c2z[...] = c2.astype(bf16)
    c2t = [copy(c2z, c2zr.at[k], flip(z, k), me) for k in range(1, 8)]
    halo_finish(exta, halo_a)
    squeeze_back = squeeze_finish(be, eb8) * slope(squeeze_pre)
    means_back = split_right(dot_nt, sq_w, squeeze_back)
    mb_col = jnp.where(img == 0, means_back[:, 0:1], means_back[:, 1:2]) * (1.0 / CELLS)
    hb = ((sback[...] + mb_col) * slope(conv_out[...])).astype(bf16)
    mb_all[...] = means_back
    mb_own = mb_all[pl.ds(pl.multiple_of(CB * m, 16), CB), :] * (1.0 / CELLS)
    mb_same = jnp.where(img == 0, mb_own[:, 0:1], mb_own[:, 1:2])
    mb_far = jnp.where(img == 0, mb_own[:, 1:2], mb_own[:, 0:1])
    grads = ga[...] + mb_same * gs[0] + mb_far * gs[1]
    for k in range(TILES - 2):
        zf[k] = grads[:, ZC * k : ZC * (k + 1)]
        zs[k] = grads[:, ZC * k : ZC * (k + 1)].astype(bf16)
    tail = grads[:, ZC * (TILES - 2) :]
    z1 = []
    for k in range(1, 8):
        there = flip(z, k)
        z1.append(later(zs.at[there], zr.at[k], there, me))
        pl.when(there < TILES - 2)(z1[-1].start)
    before, after = [
        ((exta[n].astype(f32) + mb_col) * exts[n].astype(f32)).astype(bf16) for n in (0, 3)
    ]
    hb_wide = jnp.concatenate([before, hb, after], axis=1)

    zbuf[...] = dot_tn(wcg[...].reshape(GP, AP), hb_wide)
    lanes8 = lax.broadcasted_iota(jnp.int32, (16, PX), 1) % 64
    for i in range(CI // 16):
        r = 16 * i
        acc = jnp.zeros((16, PX), f32)
        for b in (-1, 0, 1):
            up = zbuf[CI * (b + 1) + r : CI * (b + 1) + r + 16, :]
            mid = zbuf[CI * (b + 4) + r : CI * (b + 4) + r + 16, :]
            down = zbuf[CI * (b + 7) + r : CI * (b + 7) + r + 16, :]
            y = mid[:, 128:384] + pltpu.roll(up, 64, 1)[:, 256:512] + pltpu.roll(down, 64, 1)[:, 128:384]
            if b == 1:
                y = jnp.where(lanes8 == 0, 0.0, pltpu.roll(y, 1, 1))
            elif b == -1:
                y = jnp.where(lanes8 == 63, 0.0, pltpu.roll(y, PX - 1, 1))
            acc = acc + y
        pre[r : r + 16, :] = acc * slope(pre[r : r + 16, :])
    unpack = packing((GP, CI), 1)
    ag = dot(unpack, pre[...].astype(bf16)).astype(bf16)
    c1 = dot_nt(ag, xbt[0:BASIS, :]) + dot_nt(ag, xbt[BASIS:, :])
    c1s[...] = c1.astype(bf16).reshape(4, CB, BASIS)
    c1g = [copy(c1s.at[flip(m, k)], c1r.at[k], z, peer(k)) for k in range(1, 4)]
    r2 = reduce_start(w1g, ag, 1)

    for c in c2t:
        c.wait_recv()
    c2 = c2z[...].astype(f32)
    for k in range(1, 8):
        c2 = c2 + c2zr[k].astype(f32)

    def slot2(device, k):
        d = flip(device, k)
        return (d % 4) * 8 + d // 4

    same = (0, 2, 4, 6)
    c2all[slot2(me, 0)] = c2.astype(bf16)
    c2c = gather_column(lambda k: c2all.at[slot2(me, 0)], c2all, slot2, same[1:])
    for c in c1g:
        c.wait_recv()
    c1 = c1s[m].astype(f32) + c1r[1].astype(f32) + c1r[2].astype(f32) + c1r[3].astype(f32)
    both = jnp.concatenate([tail, c1, jnp.zeros((CB, TILES * ZC - AP - BASIS), f32)], axis=1)
    for k in (TILES - 2, TILES - 1):
        part = both[:, ZC * (k - TILES + 2) : ZC * (k - TILES + 3)]
        zf[k] = part
        zs[k] = part.astype(bf16)
    for k in range(1, 8):
        pl.when(flip(z, k) >= TILES - 2)(z1[k - 1].start)
    r2 = reduce_relay(r2, 1)
    c2ring = ring_start(c2c, c2all, slot2, same)
    swaps = [copy(c2all.at[slot2(me, k)], c2all.at[slot2(me, k)], z, peer(1)) for k in same]
    c2cols = reduce_column(r2, 1)
    for c in z1:
        c.wait_recv()
    chunk = zf[z]
    for k in range(1, 8):
        chunk = chunk + zr[k].astype(f32)
    zall[z] = chunk.astype(bf16)
    z2 = [copy(zall.at[z], zall.at[z], flip(z, k), me) for k in range(1, 8)]
    c2rows = ring_relay(c2ring, c2all, slot2, same)
    for kk in range(4):
        q = flip(m, kk)
        ig_out[q] = dot_tn((bq[q].astype(f32) + reduce_quarter(c2cols, 1, kk)).astype(bf16), eye).astype(bf16)
    for c in c2rows:
        c.wait_recv()
    for step in (1, 2, 3):
        there = lax.rem(me + 8 * step, GRP)
        for k in same:
            at = slot2(there, k)
            swaps.append(copy(c2all.at[at], c2all.at[at], z, peer(1)))

    first = lax.broadcasted_iota(jnp.int32, (CB, GP), 0) + CB * m
    mine = jnp.where(first == lax.broadcasted_iota(jnp.int32, (CB, GP), 1), 1.0, 0.0).astype(bf16)
    own = split_right(dot_nt, mine, means)
    grad = own[:, 0:1] * squeeze_back[0:1] + own[:, 1:2] * squeeze_back[1:2]
    sqg[...] = (grad * GRAD_SCALE)[0:CH_DEV, 0:SQ]
    own = split_right(dot_nt, mine, sig_back)
    grad = own[:, 0:1] * squeeze[0:1] + own[:, 1:2] * squeeze[1:2]
    exg[...] = (grad * GRAD_SCALE)[0:CH_DEV, 0:SQ]
    for n, (start, width, low) in enumerate(windows(NCH, CH_DEV, AP, CB)):
        hots2[n] = one_hot(512, low, 256, start, CH_DEV, CB)
    fb = fb_in[...]
    top = fb.astype(bf16)
    fbn[0] = top
    fbn[1] = (fb - top.astype(f32)).astype(bf16)
    for c in swaps:
        c.wait_recv()
    wide = jnp.concatenate([c2all[8 * k : 8 * (k + 1)].reshape(BASIS, 640) for k in range(4)], axis=1)
    own_top = sbp[:, 0:BASIS]
    own_low = sbp[:, BASIS:]
    for n, (start, width, low) in enumerate(windows(NCH, CH_DEV, AP, CB)):
        v = dot(wide[:, low : low + 512], hots2[n]).astype(bf16)
        v = (dot(own_top, v) + dot(own_low, v)) * GRAD_SCALE
        sg[:, start : start + width] = v[0:CH_DEV, 0:width]
    for c in z2:
        c.wait_recv()
    lanes_left = AP - ZC * 6
    c1 = jnp.concatenate([zall[6, :, lanes_left:], zall[7, :, 0 : BASIS - (ZC - lanes_left)]], axis=1)
    v = (dot_nt(c1, fbn[0]) + dot_nt(c1, fbn[1])) * GRAD_SCALE
    fg[...] = v[0:CH_DEV]
    sums = jnp.concatenate([zall[k] for k in range(7)], axis=1).astype(f32) * GRAD_SCALE
    for t in range(9):
        cg[t] = sums[0:CH_DEV, CI * t : CI * t + 264]
    for c in started:
        c.wait_send()


def copy_out(*refs):
    for source, target in zip(refs[:7], refs[7:]):
        target[...] = source[...]


def per_device(
    inputs,
    cotangent,
    first_weight,
    first_bias,
    conv_weight,
    conv_bias,
    squeeze_weight,
    squeeze_bias,
    excite_weight,
    excite_bias,
    second_weight,
    first_basis,
    second_basis,
):
    V = pltpu.VMEM
    scratch = [
        V((4, CB, PX), bf16),
        V((4, CB, PX), bf16),
        V((NCH, BASIS), f32),
        V((8, 128), f32),
        V((8, SQP), f32),
        V((GRP, CB, PX), bf16),
        V((GRP, CB, PX), bf16),
        V((CB, RAW), bf16),
        V((CB, RAW), bf16),
        V((CB, AP), bf16),
        V((CB, 2 * SQP), bf16),
        V((CB, 2 * BASIS), bf16),
        V((CB, 128), f32),
        V((4, CB, RAW), bf16),
        V((4, CB, RAW), bf16),
        V((GP, AP), bf16),
        V((4, CB, AP), bf16),
        V((GP, AP), bf16),
        V((4, CB, 2 * SQP), bf16),
        V((4, CB, 2 * BASIS), bf16),
        V((4, CB, 128), f32),
        V((10, 512, 256), bf16),
        V((9, 512, 256), bf16),
        V((2, AP, BASIS), bf16),
        V((2, NCH, BASIS), bf16),
        V((4, CI, 128), bf16),
        V((4, 4, CI, 128), bf16),
        V((4, GP, 128), bf16),
        V((4, GP, 128), bf16),
        V((4, AP, PX), bf16),
        V((CI, PX), f32),
        V((GP, PX), f32),
        V((GP, PX), f32),
        V((GP, PX), f32),
        V((2 * BASIS, PX), bf16),
        V((AP, 512), f32),
        V((4, CB, PX), bf16),
        V((2, 8, CB, PX), bf16),
        V((2, 8, CB, PX), bf16),
        V((2, 8, CB, PX), f32),
        V((2, 2, 8, CB, PX), bf16),
        V((2, 2, 8, CB, PX), bf16),
        V((8, CB, PX), f32),
        V((2, 8, CB, PX), bf16),
        V((2, 8, CB, PX), bf16),
        V((4, CB, PX), bf16),
        V((8, 32, PX), bf16),
        V((8, 32, PX), bf16),
        V((4, 32, 640), bf16),
        V((4, 32, 640), bf16),
        V((32, 640), bf16),
        V((8, 32, 640), bf16),
        V((32, 32, 640), bf16),
        V((4, CB, PX), bf16),
        V((4, CB, PX), bf16),
        V((2, CB, AP), f32),
        V((CB, AP), f32),
        V((GP, 8), f32),
        V((4, 8, 128), f32),
        V((8, 8, 128), f32),
        V((8, 2, 8, 128), f32),
        V((4, 8, 128), f32),
        V((8, 8, 128), f32),
        V((8, 2, 8, 128), f32),
        V((4, CB, PX), bf16),
        V((4, CB, PX), bf16),
        V((4, CB, BASIS), bf16),
        V((4, CB, BASIS), bf16),
        V((TILES, CB, ZC), bf16),
        V((TILES, CB, ZC), f32),
        V((TILES, CB, ZC), bf16),
        V((TILES, CB, ZC), bf16),
        pltpu.SemaphoreType.DMA((NSEM,)),
        pltpu.SemaphoreType.DMA((NSEM,)),
        pltpu.SemaphoreType.DMA((16,)),
    ]
    spec = pl.BlockSpec(memory_space=pltpu.VMEM)
    shape = jax.ShapeDtypeStruct
    bo, ig, fg, sg, cg, sqg, exg = pl.pallas_call(
        body,
        out_shape=[
            shape((4, PX, CH_DEV), bf16),
            shape((4, PX, CH_DEV), bf16),
            shape((CH_DEV, NCH), f32),
            shape((CH_DEV, NCH), f32),
            shape((9, CH_DEV, 264), f32),
            shape((CH_DEV, SQ), f32),
            shape((CH_DEV, SQ), f32),
        ],
        in_specs=[spec] * 8 + [pl.BlockSpec(memory_space=pl.ANY)] + [spec] * 4,
        out_specs=[spec] * 7,
        scratch_shapes=scratch,
        compiler_params=pltpu.CompilerParams(
            collective_id=0, has_side_effects=True, vmem_limit_bytes=62 * 1024 * 1024
        ),
    )(
        inputs.reshape(4, PX, CH_DEV), cotangent.reshape(4, PX, CH_DEV),
        first_weight.T, conv_weight.transpose(1, 0, 2), second_weight,
        squeeze_weight, excite_weight.T, second_basis, first_basis,
        first_bias[None], conv_bias[None], excite_bias[None], squeeze_bias[None],
    )

    results = (bo, ig, fg, sg, cg, sqg, exg)
    bo, ig, fg, sg, cg, sqg, exg = pl.pallas_call(
        copy_out,
        out_shape=[shape(v.shape, v.dtype) for v in results],
        in_specs=[spec] * 7,
        out_specs=[spec] * 7,
        compiler_params=pltpu.CompilerParams(vmem_limit_bytes=32 * 1024 * 1024),
    )(*results)
    return (bo.reshape(inputs.shape), ig.reshape(inputs.shape), fg.T, sg, cg.transpose(1, 0, 2), sqg, exg.T)


def solution(mesh):
    placed = (
        P(None, "tile", None, "grp"),
        P(None, "tile", None, "grp"),
        P(None, "grp"),
        P("grp"),
        P("grp", None, None),
        P("grp"),
        P("grp", None),
        P(),
        P(None, "grp"),
        P("grp"),
        P("grp", None),
        P(),
        P("grp", None),
    )
    return jax.shard_map(
        per_device,
        mesh=mesh,
        in_specs=placed,
        out_specs=(
            P(None, "tile", None, "grp"),
            P(None, "tile", None, "grp"),
            P(None, "grp"),
            P("grp", None),
            P("grp", None, None),
            P("grp", None),
            P(None, "grp"),
        ),
        check_vma=False,
    )
```

```python
import math

import jax
import jax.numpy as jnp
from jax import lax
from jax.experimental import pallas as pl
from jax.experimental.pallas import tpu as pltpu
from jax.sharding import PartitionSpec as P

MESH = pl.DeviceIdType.MESH
highest = lax.Precision.HIGHEST
bf16, f32 = jnp.bfloat16, jnp.float32

TILES = 8
GRP = 32
CH_DEV = 66
CB = 80
PX = 256
GP = 4 * CB
AP = GRP * CB
CI = 272
SQ = 528
SQP = 640
BASIS = 256
ZC = 384
CELLS = 4096.0
NSEM = 250
RAW = 2176
NCH = 2112
GRAD_SCALE = 1.0 / math.sqrt(8192.0)


def flip(index, mask):
    out = index
    for bit in range(5):
        if mask >> bit & 1:
            step = 1 << bit
            out = out + step * (1 - 2 * ((index // step) % 2))
    return out


def sigmoid(v):
    return 1.0 / (1.0 + jnp.exp(-v))


def slope(v):
    sig = sigmoid(v)
    return sig * (1.0 + v * (1.0 - sig))


def dot(a, b):
    return lax.dot_general(a, b, (((1,), (0,)), ((), ())), preferred_element_type=f32)


def dot_nt(a, b):
    return lax.dot_general(a, b, (((1,), (1,)), ((), ())), preferred_element_type=f32)


def pieces(v, count):
    out = []
    for _ in range(count - 1):
        top = v.astype(bf16)
        out.append(top)
        v = v - top.astype(f32)
    out.append(v.astype(bf16))
    return out


def dot_tn(a, b):
    return lax.dot_general(a, b, (((0,), (0,)), ((), ())), preferred_element_type=f32)


def one_hot(rows, row_start, lanes, lane_start, out_width, in_width):
    r = lax.broadcasted_iota(jnp.int32, (rows, lanes), 0) + row_start
    out = lax.broadcasted_iota(jnp.int32, (rows, lanes), 1) + lane_start
    blk = (out * ((1 << 22) // out_width + 1)) >> 22
    hit = (out - out_width * blk < CH_DEV) & (r == out + (in_width - out_width) * blk) & (blk < GRP)
    return jnp.where(hit, 1.0, 0.0).astype(bf16)


def windows(out_lanes, out_width, in_lanes, in_width):
    for start in range(0, out_lanes, 256):
        width = min(256, out_lanes - start)
        low = min(start // out_width * in_width // 128 * 128, in_lanes - 512)
        yield start, width, low


def split_left(op, a, b, count=3):
    return sum(op(p, b) for p in pieces(a, count))


def split_right(op, a, b, count=3):
    return sum(op(a, p) for p in pieces(b, count))


def body(
    x_hbm, c_hbm, w1, wc, w2, sqw, exw, sb_hbm, fb_hbm, b1_hbm, b2_hbm, b3_hbm, b4_hbm,
    bo_out, ig_out, fg, sg, cg, sqg, exg,
    x_in, c_in, sb_in, b1, b2, b3, b4, xq, cq, fb_in, bt, sqb, xall, ball, w1p, w2p, wcp, smp, sbp, bip, w1r, w2r, w1g, wcg, w2g, smg, sbg, big,
    hots, hots2, fbp, fbn,
    ext, extg, exts, exta, cols, pre, conv_out, hidden, sback, xbt, zbuf,
    bo, rs_far, rs_rel, rs_keep, rs_out, rs_in, rs_own, rs2_send, rs2_recv, bq,
    usend, urecv, c2s, c2r, c2z, c2zr, c2all,
    sls, slr, gs, ga, mb_all, hs, hz, hb8, es, ez, eb8, hbs, hbr, c1s, c1r, zs, zf, zr, zall,
    send, recv, local,
):
    z = lax.axis_index("tile")
    me = lax.axis_index("grp")
    xx = me // 8
    col = me % 8
    m = me % 4
    g = me // 4
    core = me % 2
    img = (me // 2) % 2
    count = [0]
    started = []
    locals_ = []

    def later(src, dst, tile, grp):
        i = count[0]
        count[0] += 1
        c = pltpu.make_async_remote_copy(
            src_ref=src, dst_ref=dst, send_sem=send.at[i], recv_sem=recv.at[i],
            device_id=(tile, grp), device_id_type=MESH,
        )
        started.append(c)
        return c

    def copy(src, dst, tile, grp):
        c = later(src, dst, tile, grp)
        c.start()
        return c

    def keep(src, dst):
        c = pltpu.make_async_copy(src, dst, local.at[len(locals_)])
        c.start()
        locals_.append(c)
        return c

    def peer(mask):
        return flip(me, mask)

    right, left = lax.rem(me + 8, GRP), lax.rem(me + 24, GRP)
    other = (lax.rem(z + 2 * core - 1 + TILES, TILES), flip(me, 1))
    grp_masks = [1, 2, 3, 4, 5, 6, 7, 8, 16, 24, 12, 20, 28]
    g_masks = [4, 8, 12, 16, 20, 24, 28]

    barrier = pltpu.get_barrier_semaphore()
    for mask in grp_masks:
        pl.semaphore_signal(barrier, inc=1, device_id=(z, peer(mask)), device_id_type=MESH)
    for mask in range(1, 8):
        pl.semaphore_signal(barrier, inc=1, device_id=(flip(z, mask), me), device_id_type=MESH)
    pl.semaphore_signal(barrier, inc=1, device_id=other, device_id_type=MESH)

    x_copy = keep(x_hbm, x_in)
    bias_copies = [keep(b1_hbm, b1), keep(b2_hbm, b2), keep(b3_hbm, b3)]
    late_copies = [keep(b4_hbm, b4), keep(sb_hbm, sb_in), keep(c_hbm, c_in)]
    fb_copy = keep(fb_hbm, fb_in)
    diagonal = lax.broadcasted_iota(jnp.int32, (CB, CH_DEV), 0) == lax.broadcasted_iota(jnp.int32, (CB, CH_DEV), 1)
    eye = jnp.where(diagonal, 1.0, 0.0).astype(bf16)
    w1p[...] = jnp.zeros(w1p.shape, bf16)
    w1p[0:CH_DEV, 0:NCH] = w1[...]
    x_copy.wait()
    for q in range(4):
        xq[q] = dot_nt(eye, x_in[q]).astype(bf16)
    for c in bias_copies:
        c.wait()
    bt[...] = jnp.zeros(bt.shape, f32)
    for n, vector in enumerate((b1, b2, b3)):
        bt[n : n + 1, 0:CH_DEV] = vector[...]
    bip[...] = jnp.zeros(bip.shape, f32)
    bip[:, 0:8] = bt[...].T[0:CB]
    pl.semaphore_wait(barrier, len(grp_masks) + 8)

    def gather_column(pick, dst, slot, masks=range(1, 8)):
        return [copy(pick(k), dst.at[slot(me, 0)], z, peer(k)) for k in masks]

    def ring_start(arrived, dst, slot, masks=range(8)):
        to_right, to_left = [], []
        for n, k in enumerate(masks):
            if n:
                arrived[n - 1].wait_recv()
            at = slot(me, k)
            to_right.append(copy(dst.at[at], dst.at[at], z, right))
            to_left.append(copy(dst.at[at], dst.at[at], z, left))
        return to_right, to_left

    def ring_relay(state, dst, slot, masks=range(8)):
        to_right, to_left = state
        half = len(masks) // 2
        relayed = []
        for n in range(half):
            to_right[n].wait_recv()
            at = slot(left, masks[n])
            relayed.append(copy(dst.at[at], dst.at[at], z, right))
            to_left[n + half].wait_recv()
            at = slot(right, masks[n + half])
            relayed.append(copy(dst.at[at], dst.at[at], z, left))
        return to_right[half:] + to_left[:half] + relayed

    def group_start(src, dst):
        mine = keep(src, dst.at[m])
        return mine, copy(src, dst.at[m], z, peer(1)), copy(src, dst.at[m], z, peer(2))

    def group_forward(state, dst):
        mine, near, far = state
        far.wait_recv()
        slot = flip(m, 2)
        return mine, near, copy(dst.at[slot], dst.at[slot], z, peer(1))

    def group_finish(state):
        state[0].wait()
        state[1].wait_recv()
        state[2].wait_recv()

    def halo_start(buf):
        return (
            copy(buf.at[2 - core], buf.at[3 * core], z, peer(1)),
            copy(buf.at[1 + core], buf.at[3 - 3 * core], other[0], other[1]),
        )

    def halo_finish(buf, copies):
        for c in copies:
            c.wait_recv()

        @pl.when((z == 0) & (core == 0))
        def _():
            buf[0] = jnp.zeros(buf.shape[1:], buf.dtype)

        @pl.when((z == TILES - 1) & (core == 1))
        def _():
            buf[3] = jnp.zeros(buf.shape[1:], buf.dtype)

    def block(device, k):
        return flip(device, k)

    def bias(n):
        return big[...].reshape(GP, 128)[:, n : n + 1]

    def spread(source, target):
        for n, (start, width, low) in enumerate(windows(AP, CB, RAW, CH_DEV)):
            v = dot(source[:, :, low : low + 512].reshape(GP, 512), hots[n])
            target[:, start : start + 256] = v.astype(bf16)

    xs = gather_column(lambda k: xq.at[flip(m, k & 3)], xall, block)
    s1 = group_start(w1p, w1r)
    sbi = group_start(bip, big)
    keep(xq.at[m], xall.at[me]).wait()
    xring = ring_start(xs, xall, block)
    for c in late_copies:
        c.wait()
    sqb[...] = jnp.zeros(sqb.shape, f32)
    sqb[0:1, 0:SQ] = b4[...]
    wcp[...] = jnp.zeros(wcp.shape, bf16)
    for t in range(9):
        wcp[0:CH_DEV, CI * t : CI * t + 264] = wc[t]
    xrows = ring_relay(xring, xall, block)
    sc = group_start(wcp, wcg)
    for n, (start, width, low) in enumerate(windows(AP, CB, RAW, CH_DEV)):
        hots[n] = one_hot(512, low, 256, start, CB, CH_DEV)
    s1 = group_forward(s1, w1r)
    sbi = group_forward(sbi, big)

    def packing(shape, packed_dim):
        row = lax.broadcasted_iota(jnp.int32, shape, packed_dim)
        lane = lax.broadcasted_iota(jnp.int32, shape, 1 - packed_dim)
        shifted = row
        for part in (1, 2, 3):
            shifted = shifted + jnp.where(row >= CH_DEV * part, CB - CH_DEV, 0)
        return jnp.where((shifted == lane) & (row < 4 * CH_DEV), 1.0, 0.0).astype(bf16)

    group_finish(s1)
    spread(w1r, w1g)
    group_finish(sbi)
    for c in xrows:
        c.wait_recv()

    x_rows = xall[...].reshape(AP, PX)
    first_pre = dot(w1g[...], x_rows) + bias(0)
    active = (first_pre * sigmoid(first_pre)).astype(bf16)
    pack = packing((CI, GP), 0)
    packed = dot(pack, active).astype(bf16)
    ext[1] = packed[:, 0:128]
    ext[2] = packed[:, 128:256]
    halo = halo_start(ext)
    smp[...] = jnp.zeros(smp.shape, bf16)
    smp[0:CH_DEV, 0:SQ] = sqw[...]
    smp[0:CH_DEV, SQP : SQP + SQ] = exw[...]
    ssm = group_start(smp, smg)
    w2p[...] = jnp.zeros(w2p.shape, bf16)
    w2p[0:CH_DEV, 0:NCH] = w2[...]
    s2 = group_start(w2p, w2r)
    sb = sb_in[...]
    sb_top = sb.astype(bf16)
    sbp[...] = jnp.zeros(sbp.shape, bf16)
    sbp[0:CH_DEV, 0:BASIS] = sb_top
    sbp[0:CH_DEV, BASIS:] = (sb - sb_top.astype(f32)).astype(bf16)
    ssb = group_start(sbp, sbg)
    pre[...] = split_right(dot, pack, first_pre)
    sc = group_forward(sc, wcg)
    for k in range(4):
        cols[k, 9 * CI :, :] = jnp.zeros((AP - 9 * CI, PX), bf16)

    def build(read, n_target):
        lanes = lax.broadcasted_iota(jnp.int32, (16, 512), 1) % 64
        for i in range(CI // 16):
            r = 16 * i
            e = jnp.concatenate([read(n, r) for n in range(4)], axis=1).astype(f32)
            for b in (-1, 0, 1):
                if b == 0:
                    v = e
                elif b == 1:
                    v = jnp.where(lanes == 63, 0.0, pltpu.roll(e, 511, 1))
                else:
                    v = jnp.where(lanes == 0, 0.0, pltpu.roll(e, 1, 1))
                s = pltpu.roll(v, 64, 1)
                for a, win in ((-1, s[:, 128:384]), (0, v[:, 128:384]), (1, s[:, 256:512])):
                    t = 3 * (a + 1) + b + 1
                    cols[n_target, t * CI + r : t * CI + r + 16, :] = win.astype(bf16)

    halo_finish(ext, halo)
    build(lambda n, r: ext[n, r : r + 16, :], 0)
    group_finish(sc)

    co = dot(wcg[...].reshape(GP, AP), cols[0]) + bias(1)
    conv_out[...] = co
    hid = co * sigmoid(co)
    hidden[...] = hid
    ones = jnp.ones((8, PX), bf16)
    rows8 = lax.broadcasted_iota(jnp.int32, (8, 128), 0)

    def sums_start(v, buf):
        tile = jnp.zeros((8, 128), f32)
        for j in range(3):
            part = v[128 * j : min(128 * (j + 1), GP)]
            if j == 2:
                part = jnp.concatenate([part, jnp.zeros((64, PX), f32)], axis=0)
            tile = jnp.where(rows8 == 3 * img + j, split_right(dot_nt, ones, part), tile)
        buf[0] = tile
        return [copy(buf.at[0], buf.at[k], z, peer(k)) for k in range(1, 4)]

    def sums_tiles(copies, buf, wider):
        for c in copies:
            c.wait_recv()
        wider[0] = buf[0] + buf[1] + buf[2] + buf[3]
        return [copy(wider.at[0], wider.at[k], flip(z, k), me) for k in (4, 3, 5, 2, 6, 1, 7)]

    def sums_finish(copies, wider):
        for c in copies:
            c.wait_recv()
        tile = sum(wider[k] for k in range(8))
        parts = [
            jnp.where(rows8 == 0, tile[j : j + 1], jnp.where(rows8 == 1, tile[3 + j : 4 + j], 0.0))
            for j in range(3)
        ]
        return jnp.concatenate(parts, axis=1)[:, 0:GP]

    def squeeze_start(v, buf):
        low, high = jnp.zeros((8, 128), f32), jnp.zeros((8, 128), f32)
        for j in range(5):
            part = v[:, 128 * j : 128 * (j + 1)]
            low = jnp.where(rows8 == j, part[0:1], low)
            high = jnp.where(rows8 == j, part[1:2], high)
        buf[0, 0] = low
        buf[0, 1] = high
        return [copy(buf.at[0], buf.at[n + 1], z, peer(k)) for n, k in enumerate(g_masks)]

    def squeeze_finish(copies, buf):
        for c in copies:
            c.wait_recv()
        low = sum(buf[n, 0] for n in range(8))
        high = sum(buf[n, 1] for n in range(8))
        parts = [
            jnp.where(rows8 == 0, low[j : j + 1], jnp.where(rows8 == 1, high[j : j + 1], 0.0))
            for j in range(5)
        ]
        return jnp.concatenate(parts, axis=1)

    ah = sums_start(hid, hs)
    ssm = group_forward(ssm, smg)
    sext = group_start(ext, extg)
    sh = sums_tiles(ah, hs, hz)
    group_finish(ssm)
    fb_copy.wait()
    for b in range(GRP):
        v = fb_in[CH_DEV * b : CH_DEV * (b + 1), :]
        v = jnp.concatenate([v, jnp.zeros((CB - CH_DEV, BASIS), f32)], axis=0)
        top = v.astype(bf16)
        fbp[0, CB * b : CB * (b + 1), :] = top
        fbp[1, CB * b : CB * (b + 1), :] = (v - top.astype(f32)).astype(bf16)
    means = sums_finish(sh, hz) * (1.0 / CELLS)
    sq_w = smg[:, :, 0:SQP].reshape(GP, SQP)
    ex_w = smg[:, :, SQP : 2 * SQP].reshape(GP, SQP)
    bh = squeeze_start(split_left(dot, means, sq_w), hb8)
    for q in range(4):
        cq[q] = dot_nt(eye, c_in[q]).astype(bf16)
    s2 = group_forward(s2, w2r)
    group_finish(s2)
    spread(w2r, w2g)
    xb = dot_tn(fbp[0], x_rows) + dot_tn(fbp[1], x_rows)
    xb_top = xb.astype(bf16)
    xbt[0:BASIS, :] = xb_top
    xbt[BASIS:, :] = (xb - xb_top.astype(f32)).astype(bf16)
    squeeze_pre = squeeze_finish(bh, hb8) + sqb[0:1]
    squeeze = squeeze_pre * sigmoid(squeeze_pre)
    excite = sigmoid(split_right(dot_nt, ex_w, squeeze) + bias(2))
    ex_col = jnp.where(img == 0, excite[:, 0:1], excite[:, 1:2])
    scaled = (hidden[...] * ex_col).astype(bf16)

    unit_a, unit_b, unit_c, unit_d = 2, 3, 1, 0

    def unit(r):
        return pl.ds(2 * flip(col // 2, r), 2)

    def reduce_send(inner, side, r, device):
        at = unit(r)
        return copy(rs_out.at[inner, side, at], rs_in.at[inner, side, at], z, device)

    def reduce_near(inner, side, r, device):
        at = unit(r)
        rs_out[inner, side, at] = rs_keep[side, at].astype(bf16)
        return reduce_send(inner, side, r, device)

    def reduce_pass(inner, side, r, device, arrived):
        at = unit(r)
        arrived.wait_recv()
        rs_out[inner, side, at] = (rs_keep[side, at] + rs_rel[inner, at].astype(f32)).astype(bf16)
        return reduce_send(inner, side, r, device)

    def reduce_start(weights, rhs, inner):
        def part(step):
            at = pl.multiple_of(lax.rem(xx + step, 4) * (8 * CB), 128)
            return dot_tn(weights[:, pl.ds(at, 8 * CB)], rhs).reshape(8, CB, PX)

        rs_far[inner] = part(2).astype(bf16)
        far = {}
        for r, device in ((unit_a, right), (unit_c, left), (unit_b, right), (unit_d, left)):
            far[r] = copy(rs_far.at[inner, unit(r)], rs_rel.at[inner, unit(r)], z, device)
        rs_keep[0] = part(1)
        near = {(0, unit_c): reduce_near(inner, 0, unit_c, right)}
        rs_keep[1] = part(3)
        near[1, unit_a] = reduce_near(inner, 1, unit_a, left)
        rs_own[...] = part(0)
        return far, near

    def reduce_relay(state, inner):
        far, near = state
        near[0, unit_a] = reduce_pass(inner, 0, unit_a, right, far[unit_a])
        near[1, unit_c] = reduce_pass(inner, 1, unit_c, left, far[unit_c])
        near[0, unit_d] = reduce_near(inner, 0, unit_d, right)
        near[1, unit_b] = reduce_near(inner, 1, unit_b, left)
        near[0, unit_b] = reduce_pass(inner, 0, unit_b, right, far[unit_b])
        near[1, unit_d] = reduce_pass(inner, 1, unit_d, left, far[unit_d])
        return near

    def reduce_column(near, inner):
        out = [None] * 7
        for r in (unit_a, unit_c, unit_b, unit_d):
            at = unit(r)
            near[0, r].wait_recv()
            near[1, r].wait_recv()
            total = rs_own[at] + rs_in[inner, 0, at].astype(f32) + rs_in[inner, 1, at].astype(f32)
            rs2_send[inner, at] = total.astype(bf16)
            for k in (2 * r, 2 * r + 1):
                if k:
                    out[k - 1] = copy(rs2_send.at[inner, flip(col, k)], rs2_recv.at[inner, k], z, peer(k))
        return out

    def reduce_quarter(copies, inner, kk):
        copies[kk + 3].wait_recv()
        if kk:
            copies[kk - 1].wait_recv()
            first = rs2_recv[inner, kk]
        else:
            first = rs2_send[inner, col]
        return first.astype(f32) + rs2_recv[inner, kk + 4].astype(f32)

    r1 = reduce_start(w2g, scaled, 0)
    sl = slope(conv_out[...]).astype(bf16)
    for n in range(2):
        exts[n + 1] = sl[:, 128 * n : 128 * (n + 1)]
    halo_s = halo_start(exts)
    sls[...] = sl.reshape(4, CB, PX)
    ssl = [copy(sls.at[flip(m, k)], slr.at[k], z, peer(k)) for k in range(1, 4)]
    r1 = reduce_relay(r1, 0)
    ssb = group_forward(ssb, sbg)
    group_finish(ssb)
    sb_top = sbg[:, :, 0:BASIS].reshape(GP, BASIS)
    sb_low = sbg[:, :, BASIS:].reshape(GP, BASIS)
    u2 = dot_tn(sb_top, scaled) + dot_tn(sb_low, scaled)
    usend[...] = u2.astype(bf16).reshape(8, 32, PX)
    us = [copy(usend.at[flip(g, k // 4)], urecv.at[n + 1], z, peer(k)) for n, k in enumerate(g_masks)]
    ex_row = sigmoid(
        split_left(dot_nt, squeeze, ex_w)
        + split_right(
            dot_nt,
            jnp.where(lax.broadcasted_iota(jnp.int32, (8, 128), 1) == 2, 1.0, 0.0).astype(bf16),
            big[...].reshape(GP, 128),
        )
    )
    halo_finish(exts, halo_s)
    c2cols = reduce_column(r1, 0)
    sext = group_forward(sext, extg)
    back_copies = [None] * 7
    for kk in range(4):
        q = flip(m, kk)
        total = xq[q].astype(f32) + reduce_quarter(c2cols, 0, kk)
        sig = sigmoid(total)
        bo[q] = (total * sig).astype(bf16)
        bq[q] = (cq[q].astype(f32) * (sig * (1.0 + total * (1.0 - sig)))).astype(bf16)
        for k in (kk, kk + 4):
            if k:
                back_copies[k - 1] = copy(bq.at[q], ball.at[me], z, peer(k))
    ball[me] = bq[m]
    bring = ring_start(back_copies, ball, block)
    brows = ring_relay(bring, ball, block)
    for q in range(4):
        bo_out[q] = dot_tn(bo[q], eye).astype(bf16)
    for c in us:
        c.wait_recv()
    u_own = usend[g].astype(f32)
    for n in range(1, 8):
        u_own = u_own + urecv[n].astype(f32)
    u_top = u_own.astype(bf16)
    u_low = (u_own - u_top.astype(f32)).astype(bf16)
    group_finish(sext)

    def build_other(k, carry):
        q = m + (k % 2) * (1 - 2 * (m % 2)) + 2 * (k // 2) * (1 - 2 * (m // 2))
        build(lambda n, r: extg[q, n, r : r + 16, :], k)
        return carry

    lax.fori_loop(1, 4, build_other, 0)
    for c in ssl:
        c.wait_recv()
    gs[0] = dot_nt(sls[m], cols[0]) + dot_nt(slr[1], cols[1])
    gs[1] = dot_nt(slr[2], cols[2]) + dot_nt(slr[3], cols[3])
    for c in brows:
        c.wait_recv()

    back_rows = ball[...].reshape(AP, PX)
    scaled_back = dot(w2g[...], back_rows)
    ae = sums_start(scaled_back * hidden[...], es)
    scaled_back = scaled_back * ex_col
    sback[...] = scaled_back
    edge = scaled_back.astype(bf16)
    for n in range(2):
        exta[n + 1] = edge[:, 128 * n : 128 * (n + 1)]
    halo_a = halo_start(exta)
    hbs[...] = (scaled_back * slope(conv_out[...])).astype(bf16).reshape(4, CB, PX)
    hsw = [copy(hbs.at[flip(m, k)], hbr.at[k], z, peer(k)) for k in range(1, 4)]
    se_ = sums_tiles(ae, es, ez)
    coords = dot_nt(u_top, back_rows) + dot_nt(u_low, back_rows)
    for k in range(4):
        c2s[k] = coords[:, 640 * k : 640 * (k + 1)].astype(bf16)
    c2g = [copy(c2s.at[flip(m, k)], c2r.at[k], z, peer(k)) for k in range(1, 4)]
    for c in hsw:
        c.wait_recv()
    acc = dot_nt(hbs[m], cols[0])
    for k in range(1, 4):
        acc = acc + dot_nt(hbr[k], cols[k])
    ga[...] = acc
    excite_back = sums_finish(se_, ez)
    sig_back = excite_back * ex_row * (1.0 - ex_row)
    be = squeeze_start(split_left(dot, sig_back, ex_w), eb8)
    for c in c2g:
        c.wait_recv()
    c2 = c2s[m].astype(f32) + c2r[1].astype(f32) + c2r[2].astype(f32) + c2r[3].astype(f32)
    c2z[...] = c2.astype(bf16)
    c2t = [copy(c2z, c2zr.at[k], flip(z, k), me) for k in range(1, 8)]
    halo_finish(exta, halo_a)
    squeeze_back = squeeze_finish(be, eb8) * slope(squeeze_pre)
    means_back = split_right(dot_nt, sq_w, squeeze_back)
    mb_col = jnp.where(img == 0, means_back[:, 0:1], means_back[:, 1:2]) * (1.0 / CELLS)
    hb = ((sback[...] + mb_col) * slope(conv_out[...])).astype(bf16)
    mb_all[...] = means_back
    mb_own = mb_all[pl.ds(pl.multiple_of(CB * m, 16), CB), :] * (1.0 / CELLS)
    mb_same = jnp.where(img == 0, mb_own[:, 0:1], mb_own[:, 1:2])
    mb_far = jnp.where(img == 0, mb_own[:, 1:2], mb_own[:, 0:1])
    grads = ga[...] + mb_same * gs[0] + mb_far * gs[1]
    for k in range(TILES - 2):
        zf[k] = grads[:, ZC * k : ZC * (k + 1)]
        zs[k] = grads[:, ZC * k : ZC * (k + 1)].astype(bf16)
    tail = grads[:, ZC * (TILES - 2) :]
    z1 = []
    for k in range(1, 8):
        there = flip(z, k)
        z1.append(later(zs.at[there], zr.at[k], there, me))
        pl.when(there < TILES - 2)(z1[-1].start)
    before, after = [
        ((exta[n].astype(f32) + mb_col) * exts[n].astype(f32)).astype(bf16) for n in (0, 3)
    ]
    hb_wide = jnp.concatenate([before, hb, after], axis=1)

    zbuf[...] = dot_tn(wcg[...].reshape(GP, AP), hb_wide)
    lanes8 = lax.broadcasted_iota(jnp.int32, (16, PX), 1) % 64
    for i in range(CI // 16):
        r = 16 * i
        acc = jnp.zeros((16, PX), f32)
        for b in (-1, 0, 1):
            up = zbuf[CI * (b + 1) + r : CI * (b + 1) + r + 16, :]
            mid = zbuf[CI * (b + 4) + r : CI * (b + 4) + r + 16, :]
            down = zbuf[CI * (b + 7) + r : CI * (b + 7) + r + 16, :]
            y = mid[:, 128:384] + pltpu.roll(up, 64, 1)[:, 256:512] + pltpu.roll(down, 64, 1)[:, 128:384]
            if b == 1:
                y = jnp.where(lanes8 == 0, 0.0, pltpu.roll(y, 1, 1))
            elif b == -1:
                y = jnp.where(lanes8 == 63, 0.0, pltpu.roll(y, PX - 1, 1))
            acc = acc + y
        pre[r : r + 16, :] = acc * slope(pre[r : r + 16, :])
    unpack = packing((GP, CI), 1)
    ag = dot(unpack, pre[...].astype(bf16)).astype(bf16)
    c1 = dot_nt(ag, xbt[0:BASIS, :]) + dot_nt(ag, xbt[BASIS:, :])
    c1s[...] = c1.astype(bf16).reshape(4, CB, BASIS)
    c1g = [copy(c1s.at[flip(m, k)], c1r.at[k], z, peer(k)) for k in range(1, 4)]
    r2 = reduce_start(w1g, ag, 1)

    for c in c2t:
        c.wait_recv()
    c2 = c2z[...].astype(f32)
    for k in range(1, 8):
        c2 = c2 + c2zr[k].astype(f32)

    def slot2(device, k):
        d = flip(device, k)
        return (d % 4) * 8 + d // 4

    same = (0, 2, 4, 6)
    c2all[slot2(me, 0)] = c2.astype(bf16)
    c2c = gather_column(lambda k: c2all.at[slot2(me, 0)], c2all, slot2, same[1:])
    for c in c1g:
        c.wait_recv()
    c1 = c1s[m].astype(f32) + c1r[1].astype(f32) + c1r[2].astype(f32) + c1r[3].astype(f32)
    both = jnp.concatenate([tail, c1, jnp.zeros((CB, TILES * ZC - AP - BASIS), f32)], axis=1)
    for k in (TILES - 2, TILES - 1):
        part = both[:, ZC * (k - TILES + 2) : ZC * (k - TILES + 3)]
        zf[k] = part
        zs[k] = part.astype(bf16)
    for k in range(1, 8):
        pl.when(flip(z, k) >= TILES - 2)(z1[k - 1].start)
    r2 = reduce_relay(r2, 1)
    c2ring = ring_start(c2c, c2all, slot2, same)
    swaps = [copy(c2all.at[slot2(me, k)], c2all.at[slot2(me, k)], z, peer(1)) for k in same]
    c2cols = reduce_column(r2, 1)
    for c in z1:
        c.wait_recv()
    chunk = zf[z]
    for k in range(1, 8):
        chunk = chunk + zr[k].astype(f32)
    zall[z] = chunk.astype(bf16)
    z2 = [copy(zall.at[z], zall.at[z], flip(z, k), me) for k in range(1, 8)]
    c2rows = ring_relay(c2ring, c2all, slot2, same)
    for kk in range(4):
        q = flip(m, kk)
        ig_out[q] = dot_tn((bq[q].astype(f32) + reduce_quarter(c2cols, 1, kk)).astype(bf16), eye).astype(bf16)
    for c in c2rows:
        c.wait_recv()
    for step in (1, 2, 3):
        there = lax.rem(me + 8 * step, GRP)
        for k in same:
            at = slot2(there, k)
            swaps.append(copy(c2all.at[at], c2all.at[at], z, peer(1)))

    first = lax.broadcasted_iota(jnp.int32, (CB, GP), 0) + CB * m
    mine = jnp.where(first == lax.broadcasted_iota(jnp.int32, (CB, GP), 1), 1.0, 0.0).astype(bf16)
    own = split_right(dot_nt, mine, means)
    grad = own[:, 0:1] * squeeze_back[0:1] + own[:, 1:2] * squeeze_back[1:2]
    sqg[...] = (grad * GRAD_SCALE)[0:CH_DEV, 0:SQ]
    own = split_right(dot_nt, mine, sig_back)
    grad = own[:, 0:1] * squeeze[0:1] + own[:, 1:2] * squeeze[1:2]
    exg[...] = (grad * GRAD_SCALE)[0:CH_DEV, 0:SQ]
    for n, (start, width, low) in enumerate(windows(NCH, CH_DEV, AP, CB)):
        hots2[n] = one_hot(512, low, 256, start, CH_DEV, CB)
    fb = fb_in[...]
    top = fb.astype(bf16)
    fbn[0] = top
    fbn[1] = (fb - top.astype(f32)).astype(bf16)
    for c in swaps:
        c.wait_recv()
    wide = jnp.concatenate([c2all[8 * k : 8 * (k + 1)].reshape(BASIS, 640) for k in range(4)], axis=1)
    own_top = sbp[:, 0:BASIS]
    own_low = sbp[:, BASIS:]
    for n, (start, width, low) in enumerate(windows(NCH, CH_DEV, AP, CB)):
        v = dot(wide[:, low : low + 512], hots2[n]).astype(bf16)
        v = (dot(own_top, v) + dot(own_low, v)) * GRAD_SCALE
        sg[:, start : start + width] = v[0:CH_DEV, 0:width]
    for c in z2:
        c.wait_recv()
    lanes_left = AP - ZC * 6
    c1 = jnp.concatenate([zall[6, :, lanes_left:], zall[7, :, 0 : BASIS - (ZC - lanes_left)]], axis=1)
    v = (dot_nt(c1, fbn[0]) + dot_nt(c1, fbn[1])) * GRAD_SCALE
    fg[...] = v[0:CH_DEV]
    sums = jnp.concatenate([zall[k] for k in range(7)], axis=1).astype(f32) * GRAD_SCALE
    for t in range(9):
        cg[t] = sums[0:CH_DEV, CI * t : CI * t + 264]
    for c in started:
        c.wait_send()


def copy_out(*refs):
    sems = refs[14]
    copies = [pltpu.make_async_copy(refs[n], refs[n + 7], sems.at[n]) for n in range(7)]
    for c in copies:
        c.start()
    for c in copies:
        c.wait()


def per_device(
    inputs,
    cotangent,
    first_weight,
    first_bias,
    conv_weight,
    conv_bias,
    squeeze_weight,
    squeeze_bias,
    excite_weight,
    excite_bias,
    second_weight,
    first_basis,
    second_basis,
):
    V = pltpu.VMEM
    scratch = [
        V((4, PX, CH_DEV), bf16),
        V((4, PX, CH_DEV), bf16),
        V((CH_DEV, BASIS), f32),
        V((1, CH_DEV), f32),
        V((1, CH_DEV), f32),
        V((1, CH_DEV), f32),
        V((1, SQ), f32),
        V((4, CB, PX), bf16),
        V((4, CB, PX), bf16),
        V((NCH, BASIS), f32),
        V((8, 128), f32),
        V((8, SQP), f32),
        V((GRP, CB, PX), bf16),
        V((GRP, CB, PX), bf16),
        V((CB, RAW), bf16),
        V((CB, RAW), bf16),
        V((CB, AP), bf16),
        V((CB, 2 * SQP), bf16),
        V((CB, 2 * BASIS), bf16),
        V((CB, 128), f32),
        V((4, CB, RAW), bf16),
        V((4, CB, RAW), bf16),
        V((GP, AP), bf16),
        V((4, CB, AP), bf16),
        V((GP, AP), bf16),
        V((4, CB, 2 * SQP), bf16),
        V((4, CB, 2 * BASIS), bf16),
        V((4, CB, 128), f32),
        V((10, 512, 256), bf16),
        V((9, 512, 256), bf16),
        V((2, AP, BASIS), bf16),
        V((2, NCH, BASIS), bf16),
        V((4, CI, 128), bf16),
        V((4, 4, CI, 128), bf16),
        V((4, GP, 128), bf16),
        V((4, GP, 128), bf16),
        V((4, AP, PX), bf16),
        V((CI, PX), f32),
        V((GP, PX), f32),
        V((GP, PX), f32),
        V((GP, PX), f32),
        V((2 * BASIS, PX), bf16),
        V((AP, 512), f32),
        V((4, CB, PX), bf16),
        V((2, 8, CB, PX), bf16),
        V((2, 8, CB, PX), bf16),
        V((2, 8, CB, PX), f32),
        V((2, 2, 8, CB, PX), bf16),
        V((2, 2, 8, CB, PX), bf16),
        V((8, CB, PX), f32),
        V((2, 8, CB, PX), bf16),
        V((2, 8, CB, PX), bf16),
        V((4, CB, PX), bf16),
        V((8, 32, PX), bf16),
        V((8, 32, PX), bf16),
        V((4, 32, 640), bf16),
        V((4, 32, 640), bf16),
        V((32, 640), bf16),
        V((8, 32, 640), bf16),
        V((32, 32, 640), bf16),
        V((4, CB, PX), bf16),
        V((4, CB, PX), bf16),
        V((2, CB, AP), f32),
        V((CB, AP), f32),
        V((GP, 8), f32),
        V((4, 8, 128), f32),
        V((8, 8, 128), f32),
        V((8, 2, 8, 128), f32),
        V((4, 8, 128), f32),
        V((8, 8, 128), f32),
        V((8, 2, 8, 128), f32),
        V((4, CB, PX), bf16),
        V((4, CB, PX), bf16),
        V((4, CB, BASIS), bf16),
        V((4, CB, BASIS), bf16),
        V((TILES, CB, ZC), bf16),
        V((TILES, CB, ZC), f32),
        V((TILES, CB, ZC), bf16),
        V((TILES, CB, ZC), bf16),
        pltpu.SemaphoreType.DMA((NSEM,)),
        pltpu.SemaphoreType.DMA((NSEM,)),
        pltpu.SemaphoreType.DMA((32,)),
    ]
    spec, held = pl.BlockSpec(memory_space=pltpu.VMEM), pl.BlockSpec(memory_space=pl.ANY)
    shape = jax.ShapeDtypeStruct
    bo, ig, fg, sg, cg, sqg, exg = pl.pallas_call(
        body,
        out_shape=[
            shape((4, PX, CH_DEV), bf16),
            shape((4, PX, CH_DEV), bf16),
            shape((CH_DEV, NCH), f32),
            shape((CH_DEV, NCH), f32),
            shape((9, CH_DEV, 264), f32),
            shape((CH_DEV, SQ), f32),
            shape((CH_DEV, SQ), f32),
        ],
        in_specs=[held] * 2 + [spec] * 5 + [held] * 6,
        out_specs=[spec] * 7,
        scratch_shapes=scratch,
        compiler_params=pltpu.CompilerParams(
            collective_id=0, has_side_effects=True, vmem_limit_bytes=62 * 1024 * 1024
        ),
    )(
        inputs.reshape(4, PX, CH_DEV), cotangent.reshape(4, PX, CH_DEV),
        first_weight.T, conv_weight.transpose(1, 0, 2), second_weight,
        squeeze_weight, excite_weight.T, second_basis, first_basis,
        first_bias[None], conv_bias[None], excite_bias[None], squeeze_bias[None],
    )

    results = (bo, ig, fg, sg, cg, sqg, exg)
    bo, ig, fg, sg, cg, sqg, exg = pl.pallas_call(
        copy_out,
        out_shape=[shape(v.shape, v.dtype) for v in results],
        in_specs=[pl.BlockSpec(memory_space=pl.ANY)] * 7,
        out_specs=[spec] * 7,
        scratch_shapes=[pltpu.SemaphoreType.DMA((7,))],
        compiler_params=pltpu.CompilerParams(vmem_limit_bytes=62 * 1024 * 1024),
    )(*results)
    return (bo.reshape(inputs.shape), ig.reshape(inputs.shape), fg.T, sg, cg.transpose(1, 0, 2), sqg, exg.T)


def solution(mesh):
    placed = (
        P(None, "tile", None, "grp"),
        P(None, "tile", None, "grp"),
        P(None, "grp"),
        P("grp"),
        P("grp", None, None),
        P("grp"),
        P("grp", None),
        P(),
        P(None, "grp"),
        P("grp"),
        P("grp", None),
        P(),
        P("grp", None),
    )
    return jax.shard_map(
        per_device,
        mesh=mesh,
        in_specs=placed,
        out_specs=(
            P(None, "tile", None, "grp"),
            P(None, "tile", None, "grp"),
            P(None, "grp"),
            P("grp", None),
            P("grp", None, None),
            P("grp", None),
            P(None, "grp"),
        ),
        check_vma=False,
    )
```

```python
import math

import jax
import jax.numpy as jnp
from jax import lax
from jax.experimental import pallas as pl
from jax.experimental.pallas import tpu as pltpu
from jax.sharding import PartitionSpec as P

MESH = pl.DeviceIdType.MESH
highest = lax.Precision.HIGHEST
bf16, f32 = jnp.bfloat16, jnp.float32

TILES = 8
GRP = 32
CH_DEV = 66
CB = 80
PX = 256
GP = 4 * CB
AP = GRP * CB
CI = 272
SQ = 528
SQP = 640
BASIS = 256
ZC = 384
CELLS = 4096.0
NSEM = 250
RAW = 2176
NCH = 2112
GRAD_SCALE = 1.0 / math.sqrt(8192.0)


def flip(index, mask):
    out = index
    for bit in range(5):
        if mask >> bit & 1:
            step = 1 << bit
            out = out + step * (1 - 2 * ((index // step) % 2))
    return out


def sigmoid(v):
    return 1.0 / (1.0 + jnp.exp(-v))


def slope(v):
    sig = sigmoid(v)
    return sig * (1.0 + v * (1.0 - sig))


def dot(a, b):
    return lax.dot_general(a, b, (((1,), (0,)), ((), ())), preferred_element_type=f32)


def dot_nt(a, b):
    return lax.dot_general(a, b, (((1,), (1,)), ((), ())), preferred_element_type=f32)


def pieces(v, count):
    out = []
    for _ in range(count - 1):
        top = v.astype(bf16)
        out.append(top)
        v = v - top.astype(f32)
    out.append(v.astype(bf16))
    return out


def dot_tn(a, b):
    return lax.dot_general(a, b, (((0,), (0,)), ((), ())), preferred_element_type=f32)


def one_hot(rows, row_start, lanes, lane_start, out_width, in_width):
    r = lax.broadcasted_iota(jnp.int32, (rows, lanes), 0) + row_start
    out = lax.broadcasted_iota(jnp.int32, (rows, lanes), 1) + lane_start
    blk = (out * ((1 << 22) // out_width + 1)) >> 22
    hit = (out - out_width * blk < CH_DEV) & (r == out + (in_width - out_width) * blk) & (blk < GRP)
    return jnp.where(hit, 1.0, 0.0).astype(bf16)


def windows(out_lanes, out_width, in_lanes, in_width):
    for start in range(0, out_lanes, 256):
        width = min(256, out_lanes - start)
        low = min(start // out_width * in_width // 128 * 128, in_lanes - 512)
        yield start, width, low


def split_left(op, a, b, count=3):
    return sum(op(p, b) for p in pieces(a, count))


def split_right(op, a, b, count=3):
    return sum(op(a, p) for p in pieces(b, count))


def body(
    x_hbm, c_hbm, w1, wc, w2, sqw, exw, sb_hbm, fb_hbm, b1_hbm, b2_hbm, b3_hbm, b4_hbm,
    bo_out, ig_out, fg, sg, cg, sqg, exg,
    x_in, c_in, sb_in, b1, b2, b3, b4, xq, cq, fb_in, bt, sqb, xall, ball, w1p, w2p, wcp, smp, sbp, bip, w1r, w2r, w1g, wcg, w2g, smg, sbg, big,
    hots, hots2, fbp, fbn,
    ext, extg, exts, exta, cols, pre, conv_out, hidden, sback, xbt, zbuf,
    bo, rs_far, rs_rel, rs_keep, rs_out, rs_in, rs_own, rs2_send, rs2_recv, bq,
    usend, urecv, c2s, c2r, c2z, c2zr, c2all,
    sls, slr, gs, ga, mb_all, hs, hz, hb8, es, ez, eb8, hbs, hbr, c1s, c1r, zs, zf, zr, zall,
    send, recv, local,
):
    z = lax.axis_index("tile")
    me = lax.axis_index("grp")
    xx = me // 8
    col = me % 8
    m = me % 4
    g = me // 4
    core = me % 2
    img = (me // 2) % 2
    count = [0]
    started = []
    locals_ = []

    def later(src, dst, tile, grp):
        i = count[0]
        count[0] += 1
        c = pltpu.make_async_remote_copy(
            src_ref=src, dst_ref=dst, send_sem=send.at[i], recv_sem=recv.at[i],
            device_id=(tile, grp), device_id_type=MESH,
        )
        started.append(c)
        return c

    def copy(src, dst, tile, grp):
        c = later(src, dst, tile, grp)
        c.start()
        return c

    def keep(src, dst):
        c = pltpu.make_async_copy(src, dst, local.at[len(locals_)])
        c.start()
        locals_.append(c)
        return c

    def peer(mask):
        return flip(me, mask)

    right, left = lax.rem(me + 8, GRP), lax.rem(me + 24, GRP)
    other = (lax.rem(z + 2 * core - 1 + TILES, TILES), flip(me, 1))
    grp_masks = [1, 2, 3, 4, 5, 6, 7, 8, 16, 24, 12, 20, 28]
    g_masks = [4, 8, 12, 16, 20, 24, 28]

    barrier = pltpu.get_barrier_semaphore()
    for mask in grp_masks:
        pl.semaphore_signal(barrier, inc=1, device_id=(z, peer(mask)), device_id_type=MESH)
    for mask in range(1, 8):
        pl.semaphore_signal(barrier, inc=1, device_id=(flip(z, mask), me), device_id_type=MESH)
    pl.semaphore_signal(barrier, inc=1, device_id=other, device_id_type=MESH)

    x_copy = keep(x_hbm, x_in)
    bias_copies = [keep(b1_hbm, b1), keep(b2_hbm, b2), keep(b3_hbm, b3)]
    late_copies = [keep(b4_hbm, b4), keep(sb_hbm, sb_in), keep(c_hbm, c_in)]
    fb_copy = keep(fb_hbm, fb_in)
    diagonal = lax.broadcasted_iota(jnp.int32, (CB, CH_DEV), 0) == lax.broadcasted_iota(jnp.int32, (CB, CH_DEV), 1)
    eye = jnp.where(diagonal, 1.0, 0.0).astype(bf16)
    w1p[...] = jnp.zeros(w1p.shape, bf16)
    w1p[0:CH_DEV, 0:NCH] = w1[...]
    x_copy.wait()
    for q in range(4):
        xq[q] = dot_nt(eye, x_in[q]).astype(bf16)
    for c in bias_copies:
        c.wait()
    bt[...] = jnp.zeros(bt.shape, f32)
    for n, vector in enumerate((b1, b2, b3)):
        bt[n : n + 1, 0:CH_DEV] = vector[...]
    bip[...] = jnp.zeros(bip.shape, f32)
    bip[:, 0:8] = bt[...].T[0:CB]
    pl.semaphore_wait(barrier, len(grp_masks) + 8)

    def gather_column(pick, dst, slot, masks=range(1, 8)):
        return [copy(pick(k), dst.at[slot(me, 0)], z, peer(k)) for k in masks]

    def ring_start(arrived, dst, slot, masks=range(8)):
        to_right, to_left = [], []
        for n, k in enumerate(masks):
            if n:
                arrived[n - 1].wait_recv()
            at = slot(me, k)
            to_right.append(copy(dst.at[at], dst.at[at], z, right))
            to_left.append(copy(dst.at[at], dst.at[at], z, left))
        return to_right, to_left

    def ring_relay(state, dst, slot, masks=range(8)):
        to_right, to_left = state
        half = len(masks) // 2
        relayed = []
        for n in range(half):
            to_right[n].wait_recv()
            at = slot(left, masks[n])
            relayed.append(copy(dst.at[at], dst.at[at], z, right))
            to_left[n + half].wait_recv()
            at = slot(right, masks[n + half])
            relayed.append(copy(dst.at[at], dst.at[at], z, left))
        return to_right[half:] + to_left[:half] + relayed

    def group_start(src, dst):
        mine = keep(src, dst.at[m])
        return mine, copy(src, dst.at[m], z, peer(1)), copy(src, dst.at[m], z, peer(2))

    def group_forward(state, dst):
        mine, near, far = state
        far.wait_recv()
        slot = flip(m, 2)
        return mine, near, copy(dst.at[slot], dst.at[slot], z, peer(1))

    def group_finish(state):
        state[0].wait()
        state[1].wait_recv()
        state[2].wait_recv()

    def halo_start(buf):
        return (
            copy(buf.at[2 - core], buf.at[3 * core], z, peer(1)),
            copy(buf.at[1 + core], buf.at[3 - 3 * core], other[0], other[1]),
        )

    def halo_finish(buf, copies):
        for c in copies:
            c.wait_recv()

        @pl.when((z == 0) & (core == 0))
        def _():
            buf[0] = jnp.zeros(buf.shape[1:], buf.dtype)

        @pl.when((z == TILES - 1) & (core == 1))
        def _():
            buf[3] = jnp.zeros(buf.shape[1:], buf.dtype)

    def block(device, k):
        return flip(device, k)

    def bias(n):
        return big[...].reshape(GP, 128)[:, n : n + 1]

    def spread(source, target):
        for n, (start, width, low) in enumerate(windows(AP, CB, RAW, CH_DEV)):
            v = dot(source[:, :, low : low + 512].reshape(GP, 512), hots[n])
            target[:, start : start + 256] = v.astype(bf16)

    xs = gather_column(lambda k: xq.at[flip(m, k & 3)], xall, block)
    s1 = group_start(w1p, w1r)
    sbi = group_start(bip, big)
    keep(xq.at[m], xall.at[me]).wait()
    xring = ring_start(xs, xall, block)
    for c in late_copies:
        c.wait()
    sqb[...] = jnp.zeros(sqb.shape, f32)
    sqb[0:1, 0:SQ] = b4[...]
    wcp[...] = jnp.zeros(wcp.shape, bf16)
    for t in range(9):
        wcp[0:CH_DEV, CI * t : CI * t + 264] = wc[t]
    xrows = ring_relay(xring, xall, block)
    sc = group_start(wcp, wcg)
    for n, (start, width, low) in enumerate(windows(AP, CB, RAW, CH_DEV)):
        hots[n] = one_hot(512, low, 256, start, CB, CH_DEV)
    s1 = group_forward(s1, w1r)
    sbi = group_forward(sbi, big)

    def packing(shape, packed_dim):
        row = lax.broadcasted_iota(jnp.int32, shape, packed_dim)
        lane = lax.broadcasted_iota(jnp.int32, shape, 1 - packed_dim)
        shifted = row
        for part in (1, 2, 3):
            shifted = shifted + jnp.where(row >= CH_DEV * part, CB - CH_DEV, 0)
        return jnp.where((shifted == lane) & (row < 4 * CH_DEV), 1.0, 0.0).astype(bf16)

    group_finish(s1)
    spread(w1r, w1g)
    group_finish(sbi)
    for c in xrows:
        c.wait_recv()

    x_rows = xall[...].reshape(AP, PX)
    first_pre = dot(w1g[...], x_rows) + bias(0)
    active = (first_pre * sigmoid(first_pre)).astype(bf16)
    pack = packing((CI, GP), 0)
    packed = dot(pack, active).astype(bf16)
    ext[1] = packed[:, 0:128]
    ext[2] = packed[:, 128:256]
    halo = halo_start(ext)
    smp[...] = jnp.zeros(smp.shape, bf16)
    smp[0:CH_DEV, 0:SQ] = sqw[...]
    smp[0:CH_DEV, SQP : SQP + SQ] = exw[...]
    ssm = group_start(smp, smg)
    w2p[...] = jnp.zeros(w2p.shape, bf16)
    w2p[0:CH_DEV, 0:NCH] = w2[...]
    s2 = group_start(w2p, w2r)
    sb = sb_in[...]
    sb_top = sb.astype(bf16)
    sbp[...] = jnp.zeros(sbp.shape, bf16)
    sbp[0:CH_DEV, 0:BASIS] = sb_top
    sbp[0:CH_DEV, BASIS:] = (sb - sb_top.astype(f32)).astype(bf16)
    ssb = group_start(sbp, sbg)
    pre[...] = split_right(dot, pack, first_pre)
    sc = group_forward(sc, wcg)
    for k in range(4):
        cols[k, 9 * CI :, :] = jnp.zeros((AP - 9 * CI, PX), bf16)

    def build(read, n_target):
        lanes = lax.broadcasted_iota(jnp.int32, (16, 512), 1) % 64
        for i in range(CI // 16):
            r = 16 * i
            e = jnp.concatenate([read(n, r) for n in range(4)], axis=1).astype(f32)
            for b in (-1, 0, 1):
                if b == 0:
                    v = e
                elif b == 1:
                    v = jnp.where(lanes == 63, 0.0, pltpu.roll(e, 511, 1))
                else:
                    v = jnp.where(lanes == 0, 0.0, pltpu.roll(e, 1, 1))
                s = pltpu.roll(v, 64, 1)
                for a, win in ((-1, s[:, 128:384]), (0, v[:, 128:384]), (1, s[:, 256:512])):
                    t = 3 * (a + 1) + b + 1
                    cols[n_target, t * CI + r : t * CI + r + 16, :] = win.astype(bf16)

    halo_finish(ext, halo)
    build(lambda n, r: ext[n, r : r + 16, :], 0)
    group_finish(sc)

    co = dot(wcg[...].reshape(GP, AP), cols[0]) + bias(1)
    conv_out[...] = co
    hid = co * sigmoid(co)
    hidden[...] = hid
    ones = jnp.ones((8, PX), bf16)
    rows8 = lax.broadcasted_iota(jnp.int32, (8, 128), 0)

    def sums_start(v, buf):
        tile = jnp.zeros((8, 128), f32)
        for j in range(3):
            part = v[128 * j : min(128 * (j + 1), GP)]
            if j == 2:
                part = jnp.concatenate([part, jnp.zeros((64, PX), f32)], axis=0)
            tile = jnp.where(rows8 == 3 * img + j, split_right(dot_nt, ones, part), tile)
        buf[0] = tile
        return [copy(buf.at[0], buf.at[k], z, peer(k)) for k in range(1, 4)]

    def sums_tiles(copies, buf, wider):
        for c in copies:
            c.wait_recv()
        wider[0] = buf[0] + buf[1] + buf[2] + buf[3]
        return [copy(wider.at[0], wider.at[k], flip(z, k), me) for k in (4, 3, 5, 2, 6, 1, 7)]

    def sums_finish(copies, wider):
        for c in copies:
            c.wait_recv()
        tile = sum(wider[k] for k in range(8))
        parts = [
            jnp.where(rows8 == 0, tile[j : j + 1], jnp.where(rows8 == 1, tile[3 + j : 4 + j], 0.0))
            for j in range(3)
        ]
        return jnp.concatenate(parts, axis=1)[:, 0:GP]

    def squeeze_start(v, buf):
        low, high = jnp.zeros((8, 128), f32), jnp.zeros((8, 128), f32)
        for j in range(5):
            part = v[:, 128 * j : 128 * (j + 1)]
            low = jnp.where(rows8 == j, part[0:1], low)
            high = jnp.where(rows8 == j, part[1:2], high)
        buf[0, 0] = low
        buf[0, 1] = high
        return [copy(buf.at[0], buf.at[n + 1], z, peer(k)) for n, k in enumerate(g_masks)]

    def squeeze_finish(copies, buf):
        for c in copies:
            c.wait_recv()
        low = sum(buf[n, 0] for n in range(8))
        high = sum(buf[n, 1] for n in range(8))
        parts = [
            jnp.where(rows8 == 0, low[j : j + 1], jnp.where(rows8 == 1, high[j : j + 1], 0.0))
            for j in range(5)
        ]
        return jnp.concatenate(parts, axis=1)

    ah = sums_start(hid, hs)
    ssm = group_forward(ssm, smg)
    sext = group_start(ext, extg)
    sh = sums_tiles(ah, hs, hz)
    group_finish(ssm)
    fb_copy.wait()
    for b in range(GRP):
        v = fb_in[CH_DEV * b : CH_DEV * (b + 1), :]
        v = jnp.concatenate([v, jnp.zeros((CB - CH_DEV, BASIS), f32)], axis=0)
        top = v.astype(bf16)
        fbp[0, CB * b : CB * (b + 1), :] = top
        fbp[1, CB * b : CB * (b + 1), :] = (v - top.astype(f32)).astype(bf16)
    means = sums_finish(sh, hz) * (1.0 / CELLS)
    sq_w = smg[:, :, 0:SQP].reshape(GP, SQP)
    ex_w = smg[:, :, SQP : 2 * SQP].reshape(GP, SQP)
    bh = squeeze_start(split_left(dot, means, sq_w), hb8)
    s2 = group_forward(s2, w2r)
    group_finish(s2)
    spread(w2r, w2g)
    squeeze_pre = squeeze_finish(bh, hb8) + sqb[0:1]
    squeeze = squeeze_pre * sigmoid(squeeze_pre)
    excite = sigmoid(split_right(dot_nt, ex_w, squeeze) + bias(2))
    ex_col = jnp.where(img == 0, excite[:, 0:1], excite[:, 1:2])
    scaled = (hidden[...] * ex_col).astype(bf16)

    unit_a, unit_b, unit_c, unit_d = 2, 3, 1, 0

    def unit(r):
        return pl.ds(2 * flip(col // 2, r), 2)

    def reduce_send(inner, side, r, device):
        at = unit(r)
        return copy(rs_out.at[inner, side, at], rs_in.at[inner, side, at], z, device)

    def reduce_near(inner, side, r, device):
        at = unit(r)
        rs_out[inner, side, at] = rs_keep[side, at].astype(bf16)
        return reduce_send(inner, side, r, device)

    def reduce_pass(inner, side, r, device, arrived):
        at = unit(r)
        arrived.wait_recv()
        rs_out[inner, side, at] = (rs_keep[side, at] + rs_rel[inner, at].astype(f32)).astype(bf16)
        return reduce_send(inner, side, r, device)

    def reduce_start(weights, rhs, inner):
        def part(step):
            at = pl.multiple_of(lax.rem(xx + step, 4) * (8 * CB), 128)
            return dot_tn(weights[:, pl.ds(at, 8 * CB)], rhs).reshape(8, CB, PX)

        rs_far[inner] = part(2).astype(bf16)
        far = {}
        for r, device in ((unit_a, right), (unit_c, left), (unit_b, right), (unit_d, left)):
            far[r] = copy(rs_far.at[inner, unit(r)], rs_rel.at[inner, unit(r)], z, device)
        rs_keep[0] = part(1)
        near = {(0, unit_c): reduce_near(inner, 0, unit_c, right)}
        rs_keep[1] = part(3)
        near[1, unit_a] = reduce_near(inner, 1, unit_a, left)
        rs_own[...] = part(0)
        return far, near

    def reduce_relay(state, inner):
        far, near = state
        near[0, unit_a] = reduce_pass(inner, 0, unit_a, right, far[unit_a])
        near[1, unit_c] = reduce_pass(inner, 1, unit_c, left, far[unit_c])
        near[0, unit_d] = reduce_near(inner, 0, unit_d, right)
        near[1, unit_b] = reduce_near(inner, 1, unit_b, left)
        near[0, unit_b] = reduce_pass(inner, 0, unit_b, right, far[unit_b])
        near[1, unit_d] = reduce_pass(inner, 1, unit_d, left, far[unit_d])
        return near

    def reduce_column(near, inner):
        out = [None] * 7
        for r in (unit_a, unit_c, unit_b, unit_d):
            at = unit(r)
            near[0, r].wait_recv()
            near[1, r].wait_recv()
            total = rs_own[at] + rs_in[inner, 0, at].astype(f32) + rs_in[inner, 1, at].astype(f32)
            rs2_send[inner, at] = total.astype(bf16)
            for k in (2 * r, 2 * r + 1):
                if k:
                    out[k - 1] = copy(rs2_send.at[inner, flip(col, k)], rs2_recv.at[inner, k], z, peer(k))
        return out

    def reduce_quarter(copies, inner, kk):
        copies[kk + 3].wait_recv()
        if kk:
            copies[kk - 1].wait_recv()
            first = rs2_recv[inner, kk]
        else:
            first = rs2_send[inner, col]
        return first.astype(f32) + rs2_recv[inner, kk + 4].astype(f32)

    r1 = reduce_start(w2g, scaled, 0)
    sl = slope(conv_out[...]).astype(bf16)
    for n in range(2):
        exts[n + 1] = sl[:, 128 * n : 128 * (n + 1)]
    halo_s = halo_start(exts)
    sls[...] = sl.reshape(4, CB, PX)
    ssl = [copy(sls.at[flip(m, k)], slr.at[k], z, peer(k)) for k in range(1, 4)]
    r1 = reduce_relay(r1, 0)
    for q in range(4):
        cq[q] = dot_nt(eye, c_in[q]).astype(bf16)
    xb = dot_tn(fbp[0], x_rows) + dot_tn(fbp[1], x_rows)
    xb_top = xb.astype(bf16)
    xbt[0:BASIS, :] = xb_top
    xbt[BASIS:, :] = (xb - xb_top.astype(f32)).astype(bf16)
    ssb = group_forward(ssb, sbg)
    group_finish(ssb)
    sb_top = sbg[:, :, 0:BASIS].reshape(GP, BASIS)
    sb_low = sbg[:, :, BASIS:].reshape(GP, BASIS)
    u2 = dot_tn(sb_top, scaled) + dot_tn(sb_low, scaled)
    usend[...] = u2.astype(bf16).reshape(8, 32, PX)
    us = [copy(usend.at[flip(g, k // 4)], urecv.at[n + 1], z, peer(k)) for n, k in enumerate(g_masks)]
    ex_row = sigmoid(
        split_left(dot_nt, squeeze, ex_w)
        + split_right(
            dot_nt,
            jnp.where(lax.broadcasted_iota(jnp.int32, (8, 128), 1) == 2, 1.0, 0.0).astype(bf16),
            big[...].reshape(GP, 128),
        )
    )
    halo_finish(exts, halo_s)
    c2cols = reduce_column(r1, 0)
    sext = group_forward(sext, extg)
    back_copies = [None] * 7
    for kk in range(4):
        q = flip(m, kk)
        total = xq[q].astype(f32) + reduce_quarter(c2cols, 0, kk)
        sig = sigmoid(total)
        bo[q] = (total * sig).astype(bf16)
        bq[q] = (cq[q].astype(f32) * (sig * (1.0 + total * (1.0 - sig)))).astype(bf16)
        for k in (kk, kk + 4):
            if k:
                back_copies[k - 1] = copy(bq.at[q], ball.at[me], z, peer(k))
    ball[me] = bq[m]
    bring = ring_start(back_copies, ball, block)
    brows = ring_relay(bring, ball, block)
    for q in range(4):
        bo_out[q] = dot_tn(bo[q], eye).astype(bf16)
    for c in us:
        c.wait_recv()
    u_own = usend[g].astype(f32)
    for n in range(1, 8):
        u_own = u_own + urecv[n].astype(f32)
    u_top = u_own.astype(bf16)
    u_low = (u_own - u_top.astype(f32)).astype(bf16)
    group_finish(sext)

    def build_other(k, carry):
        q = m + (k % 2) * (1 - 2 * (m % 2)) + 2 * (k // 2) * (1 - 2 * (m // 2))
        build(lambda n, r: extg[q, n, r : r + 16, :], k)
        return carry

    lax.fori_loop(1, 4, build_other, 0)
    for c in ssl:
        c.wait_recv()
    gs[0] = dot_nt(sls[m], cols[0]) + dot_nt(slr[1], cols[1])
    gs[1] = dot_nt(slr[2], cols[2]) + dot_nt(slr[3], cols[3])
    for c in brows:
        c.wait_recv()

    back_rows = ball[...].reshape(AP, PX)
    scaled_back = dot(w2g[...], back_rows)
    ae = sums_start(scaled_back * hidden[...], es)
    scaled_back = scaled_back * ex_col
    sback[...] = scaled_back
    edge = scaled_back.astype(bf16)
    for n in range(2):
        exta[n + 1] = edge[:, 128 * n : 128 * (n + 1)]
    halo_a = halo_start(exta)
    hbs[...] = (scaled_back * slope(conv_out[...])).astype(bf16).reshape(4, CB, PX)
    hsw = [copy(hbs.at[flip(m, k)], hbr.at[k], z, peer(k)) for k in range(1, 4)]
    se_ = sums_tiles(ae, es, ez)
    coords = dot_nt(u_top, back_rows) + dot_nt(u_low, back_rows)
    for k in range(4):
        c2s[k] = coords[:, 640 * k : 640 * (k + 1)].astype(bf16)
    c2g = [copy(c2s.at[flip(m, k)], c2r.at[k], z, peer(k)) for k in range(1, 4)]
    excite_back = sums_finish(se_, ez)
    sig_back = excite_back * ex_row * (1.0 - ex_row)
    be = squeeze_start(split_left(dot, sig_back, ex_w), eb8)
    for c in c2g:
        c.wait_recv()
    c2 = c2s[m].astype(f32) + c2r[1].astype(f32) + c2r[2].astype(f32) + c2r[3].astype(f32)
    c2z[...] = c2.astype(bf16)
    c2t = [copy(c2z, c2zr.at[k], flip(z, k), me) for k in range(1, 8)]
    for c in hsw:
        c.wait_recv()
    acc = dot_nt(hbs[m], cols[0])
    for k in range(1, 4):
        acc = acc + dot_nt(hbr[k], cols[k])
    ga[...] = acc
    halo_finish(exta, halo_a)
    squeeze_back = squeeze_finish(be, eb8) * slope(squeeze_pre)
    means_back = split_right(dot_nt, sq_w, squeeze_back)
    mb_col = jnp.where(img == 0, means_back[:, 0:1], means_back[:, 1:2]) * (1.0 / CELLS)
    hb = ((sback[...] + mb_col) * slope(conv_out[...])).astype(bf16)
    mb_all[...] = means_back
    mb_own = mb_all[pl.ds(pl.multiple_of(CB * m, 16), CB), :] * (1.0 / CELLS)
    mb_same = jnp.where(img == 0, mb_own[:, 0:1], mb_own[:, 1:2])
    mb_far = jnp.where(img == 0, mb_own[:, 1:2], mb_own[:, 0:1])
    grads = ga[...] + mb_same * gs[0] + mb_far * gs[1]
    for k in range(TILES - 2):
        zf[k] = grads[:, ZC * k : ZC * (k + 1)]
        zs[k] = grads[:, ZC * k : ZC * (k + 1)].astype(bf16)
    tail = grads[:, ZC * (TILES - 2) :]
    z1 = []
    for k in range(1, 8):
        there = flip(z, k)
        z1.append(later(zs.at[there], zr.at[k], there, me))
        pl.when(there < TILES - 2)(z1[-1].start)
    before, after = [
        ((exta[n].astype(f32) + mb_col) * exts[n].astype(f32)).astype(bf16) for n in (0, 3)
    ]
    hb_wide = jnp.concatenate([before, hb, after], axis=1)

    zbuf[...] = dot_tn(wcg[...].reshape(GP, AP), hb_wide)
    lanes8 = lax.broadcasted_iota(jnp.int32, (16, PX), 1) % 64
    for i in range(CI // 16):
        r = 16 * i
        acc = jnp.zeros((16, PX), f32)
        for b in (-1, 0, 1):
            up = zbuf[CI * (b + 1) + r : CI * (b + 1) + r + 16, :]
            mid = zbuf[CI * (b + 4) + r : CI * (b + 4) + r + 16, :]
            down = zbuf[CI * (b + 7) + r : CI * (b + 7) + r + 16, :]
            y = mid[:, 128:384] + pltpu.roll(up, 64, 1)[:, 256:512] + pltpu.roll(down, 64, 1)[:, 128:384]
            if b == 1:
                y = jnp.where(lanes8 == 0, 0.0, pltpu.roll(y, 1, 1))
            elif b == -1:
                y = jnp.where(lanes8 == 63, 0.0, pltpu.roll(y, PX - 1, 1))
            acc = acc + y
        pre[r : r + 16, :] = acc * slope(pre[r : r + 16, :])
    unpack = packing((GP, CI), 1)
    ag = dot(unpack, pre[...].astype(bf16)).astype(bf16)
    c1 = dot_nt(ag, xbt[0:BASIS, :]) + dot_nt(ag, xbt[BASIS:, :])
    c1s[...] = c1.astype(bf16).reshape(4, CB, BASIS)
    c1g = [copy(c1s.at[flip(m, k)], c1r.at[k], z, peer(k)) for k in range(1, 4)]
    r2 = reduce_start(w1g, ag, 1)

    for c in c2t:
        c.wait_recv()
    c2 = c2z[...].astype(f32)
    for k in range(1, 8):
        c2 = c2 + c2zr[k].astype(f32)

    def slot2(device, k):
        d = flip(device, k)
        return (d % 4) * 8 + d // 4

    same = (0, 2, 4, 6)
    c2all[slot2(me, 0)] = c2.astype(bf16)
    c2c = gather_column(lambda k: c2all.at[slot2(me, 0)], c2all, slot2, same[1:])
    for c in c1g:
        c.wait_recv()
    c1 = c1s[m].astype(f32) + c1r[1].astype(f32) + c1r[2].astype(f32) + c1r[3].astype(f32)
    both = jnp.concatenate([tail, c1, jnp.zeros((CB, TILES * ZC - AP - BASIS), f32)], axis=1)
    for k in (TILES - 2, TILES - 1):
        part = both[:, ZC * (k - TILES + 2) : ZC * (k - TILES + 3)]
        zf[k] = part
        zs[k] = part.astype(bf16)
    for k in range(1, 8):
        pl.when(flip(z, k) >= TILES - 2)(z1[k - 1].start)
    r2 = reduce_relay(r2, 1)
    c2ring = ring_start(c2c, c2all, slot2, same)
    swaps = [copy(c2all.at[slot2(me, k)], c2all.at[slot2(me, k)], z, peer(1)) for k in same]
    c2cols = reduce_column(r2, 1)
    for c in z1:
        c.wait_recv()
    chunk = zf[z]
    for k in range(1, 8):
        chunk = chunk + zr[k].astype(f32)
    zall[z] = chunk.astype(bf16)
    z2 = [copy(zall.at[z], zall.at[z], flip(z, k), me) for k in range(1, 8)]
    c2rows = ring_relay(c2ring, c2all, slot2, same)
    for kk in range(4):
        q = flip(m, kk)
        ig_out[q] = dot_tn((bq[q].astype(f32) + reduce_quarter(c2cols, 1, kk)).astype(bf16), eye).astype(bf16)
    for c in c2rows:
        c.wait_recv()
    for step in (1, 2, 3):
        there = lax.rem(me + 8 * step, GRP)
        for k in same:
            at = slot2(there, k)
            swaps.append(copy(c2all.at[at], c2all.at[at], z, peer(1)))

    first = lax.broadcasted_iota(jnp.int32, (CB, GP), 0) + CB * m
    mine = jnp.where(first == lax.broadcasted_iota(jnp.int32, (CB, GP), 1), 1.0, 0.0).astype(bf16)
    own = split_right(dot_nt, mine, means)
    grad = own[:, 0:1] * squeeze_back[0:1] + own[:, 1:2] * squeeze_back[1:2]
    sqg[...] = (grad * GRAD_SCALE)[0:CH_DEV, 0:SQ]
    own = split_right(dot_nt, mine, sig_back)
    grad = own[:, 0:1] * squeeze[0:1] + own[:, 1:2] * squeeze[1:2]
    exg[...] = (grad * GRAD_SCALE)[0:CH_DEV, 0:SQ]
    for n, (start, width, low) in enumerate(windows(NCH, CH_DEV, AP, CB)):
        hots2[n] = one_hot(512, low, 256, start, CH_DEV, CB)
    fb = fb_in[...]
    top = fb.astype(bf16)
    fbn[0] = top
    fbn[1] = (fb - top.astype(f32)).astype(bf16)
    for c in swaps:
        c.wait_recv()
    wide = jnp.concatenate([c2all[8 * k : 8 * (k + 1)].reshape(BASIS, 640) for k in range(4)], axis=1)
    own_top = sbp[:, 0:BASIS]
    own_low = sbp[:, BASIS:]
    for n, (start, width, low) in enumerate(windows(NCH, CH_DEV, AP, CB)):
        v = dot(wide[:, low : low + 512], hots2[n]).astype(bf16)
        v = (dot(own_top, v) + dot(own_low, v)) * GRAD_SCALE
        sg[:, start : start + width] = v[0:CH_DEV, 0:width]
    for c in z2:
        c.wait_recv()
    lanes_left = AP - ZC * 6
    c1 = jnp.concatenate([zall[6, :, lanes_left:], zall[7, :, 0 : BASIS - (ZC - lanes_left)]], axis=1)
    v = (dot_nt(c1, fbn[0]) + dot_nt(c1, fbn[1])) * GRAD_SCALE
    fg[...] = v[0:CH_DEV]
    sums = jnp.concatenate([zall[k] for k in range(7)], axis=1).astype(f32) * GRAD_SCALE
    for t in range(9):
        cg[t] = sums[0:CH_DEV, CI * t : CI * t + 264]
    for c in started:
        c.wait_send()


def copy_out(*refs):
    sems = refs[14]
    copies = [pltpu.make_async_copy(refs[n], refs[n + 7], sems.at[n]) for n in range(7)]
    for c in copies:
        c.start()
    for c in copies:
        c.wait()


def per_device(
    inputs,
    cotangent,
    first_weight,
    first_bias,
    conv_weight,
    conv_bias,
    squeeze_weight,
    squeeze_bias,
    excite_weight,
    excite_bias,
    second_weight,
    first_basis,
    second_basis,
):
    V = pltpu.VMEM
    scratch = [
        V((4, PX, CH_DEV), bf16),
        V((4, PX, CH_DEV), bf16),
        V((CH_DEV, BASIS), f32),
        V((1, CH_DEV), f32),
        V((1, CH_DEV), f32),
        V((1, CH_DEV), f32),
        V((1, SQ), f32),
        V((4, CB, PX), bf16),
        V((4, CB, PX), bf16),
        V((NCH, BASIS), f32),
        V((8, 128), f32),
        V((8, SQP), f32),
        V((GRP, CB, PX), bf16),
        V((GRP, CB, PX), bf16),
        V((CB, RAW), bf16),
        V((CB, RAW), bf16),
        V((CB, AP), bf16),
        V((CB, 2 * SQP), bf16),
        V((CB, 2 * BASIS), bf16),
        V((CB, 128), f32),
        V((4, CB, RAW), bf16),
        V((4, CB, RAW), bf16),
        V((GP, AP), bf16),
        V((4, CB, AP), bf16),
        V((GP, AP), bf16),
        V((4, CB, 2 * SQP), bf16),
        V((4, CB, 2 * BASIS), bf16),
        V((4, CB, 128), f32),
        V((10, 512, 256), bf16),
        V((9, 512, 256), bf16),
        V((2, AP, BASIS), bf16),
        V((2, NCH, BASIS), bf16),
        V((4, CI, 128), bf16),
        V((4, 4, CI, 128), bf16),
        V((4, GP, 128), bf16),
        V((4, GP, 128), bf16),
        V((4, AP, PX), bf16),
        V((CI, PX), f32),
        V((GP, PX), f32),
        V((GP, PX), f32),
        V((GP, PX), f32),
        V((2 * BASIS, PX), bf16),
        V((AP, 512), f32),
        V((4, CB, PX), bf16),
        V((2, 8, CB, PX), bf16),
        V((2, 8, CB, PX), bf16),
        V((2, 8, CB, PX), f32),
        V((2, 2, 8, CB, PX), bf16),
        V((2, 2, 8, CB, PX), bf16),
        V((8, CB, PX), f32),
        V((2, 8, CB, PX), bf16),
        V((2, 8, CB, PX), bf16),
        V((4, CB, PX), bf16),
        V((8, 32, PX), bf16),
        V((8, 32, PX), bf16),
        V((4, 32, 640), bf16),
        V((4, 32, 640), bf16),
        V((32, 640), bf16),
        V((8, 32, 640), bf16),
        V((32, 32, 640), bf16),
        V((4, CB, PX), bf16),
        V((4, CB, PX), bf16),
        V((2, CB, AP), f32),
        V((CB, AP), f32),
        V((GP, 8), f32),
        V((4, 8, 128), f32),
        V((8, 8, 128), f32),
        V((8, 2, 8, 128), f32),
        V((4, 8, 128), f32),
        V((8, 8, 128), f32),
        V((8, 2, 8, 128), f32),
        V((4, CB, PX), bf16),
        V((4, CB, PX), bf16),
        V((4, CB, BASIS), bf16),
        V((4, CB, BASIS), bf16),
        V((TILES, CB, ZC), bf16),
        V((TILES, CB, ZC), f32),
        V((TILES, CB, ZC), bf16),
        V((TILES, CB, ZC), bf16),
        pltpu.SemaphoreType.DMA((NSEM,)),
        pltpu.SemaphoreType.DMA((NSEM,)),
        pltpu.SemaphoreType.DMA((32,)),
    ]
    spec, held = pl.BlockSpec(memory_space=pltpu.VMEM), pl.BlockSpec(memory_space=pl.ANY)
    shape = jax.ShapeDtypeStruct
    bo, ig, fg, sg, cg, sqg, exg = pl.pallas_call(
        body,
        out_shape=[
            shape((4, PX, CH_DEV), bf16),
            shape((4, PX, CH_DEV), bf16),
            shape((CH_DEV, NCH), f32),
            shape((CH_DEV, NCH), f32),
            shape((9, CH_DEV, 264), f32),
            shape((CH_DEV, SQ), f32),
            shape((CH_DEV, SQ), f32),
        ],
        in_specs=[held] * 2 + [spec] * 5 + [held] * 6,
        out_specs=[spec] * 7,
        scratch_shapes=scratch,
        compiler_params=pltpu.CompilerParams(
            collective_id=0, has_side_effects=True, vmem_limit_bytes=62 * 1024 * 1024
        ),
    )(
        inputs.reshape(4, PX, CH_DEV), cotangent.reshape(4, PX, CH_DEV),
        first_weight.T, conv_weight.transpose(1, 0, 2), second_weight,
        squeeze_weight, excite_weight.T, second_basis, first_basis,
        first_bias[None], conv_bias[None], excite_bias[None], squeeze_bias[None],
    )

    results = (bo, ig, fg, sg, cg, sqg, exg)
    bo, ig, fg, sg, cg, sqg, exg = pl.pallas_call(
        copy_out,
        out_shape=[shape(v.shape, v.dtype) for v in results],
        in_specs=[pl.BlockSpec(memory_space=pl.ANY)] * 7,
        out_specs=[spec] * 7,
        scratch_shapes=[pltpu.SemaphoreType.DMA((7,))],
        compiler_params=pltpu.CompilerParams(vmem_limit_bytes=62 * 1024 * 1024),
    )(*results)
    return (bo.reshape(inputs.shape), ig.reshape(inputs.shape), fg.T, sg, cg.transpose(1, 0, 2), sqg, exg.T)


def solution(mesh):
    placed = (
        P(None, "tile", None, "grp"),
        P(None, "tile", None, "grp"),
        P(None, "grp"),
        P("grp"),
        P("grp", None, None),
        P("grp"),
        P("grp", None),
        P(),
        P(None, "grp"),
        P("grp"),
        P("grp", None),
        P(),
        P("grp", None),
    )
    return jax.shard_map(
        per_device,
        mesh=mesh,
        in_specs=placed,
        out_specs=(
            P(None, "tile", None, "grp"),
            P(None, "tile", None, "grp"),
            P(None, "grp"),
            P("grp", None),
            P("grp", None, None),
            P("grp", None),
            P(None, "grp"),
        ),
        check_vma=False,
    )
```
